128 devices in a mesh: seq: 16 (over x, y_lo, core), fsdp: 8 (over z, y_hi).
Axes of the slice: x: 4, y: 4 (y_hi: 2, y_lo: 2; y = y_hi * 2 + y_lo), z: 4, core: 2. Of those that a mesh axis runs over, the one named last changes fastest.
Arguments:
- hidden_in: bfloat16 [8, 2048, 1024], P('fsdp', 'seq'), may hold values from -6 to 6
- norm1_gain: bfloat16 [1024], P('seq'), may hold values from 0.099609375 to 1.8984375
- norm1_shift: bfloat16 [1024], P('seq'), may hold values from -3 to 3
- qkv_weight: bfloat16 [1024, 3072], P('fsdp', 'seq'), may hold values from -0.1875 to 0.1875
- query_bias: bfloat16 [1024], P('seq'), may hold values from -4 to 4
- value_bias: bfloat16 [1024], P('seq'), may hold values from -4 to 4
- proj_weight: bfloat16 [1024, 1024], P('fsdp', 'seq'), may hold values from -0.75 to 0.75
- proj_bias: bfloat16 [1024], P('seq'), may hold values from -4 to 4
- norm2_gain: bfloat16 [1024], P('seq'), may hold values from 0.099609375 to 1.8984375
- norm2_shift: bfloat16 [1024], P('seq'), may hold values from -3 to 3
- up_weight: bfloat16 [1024, 4096], P('fsdp', 'seq'), may hold values from -0.1875 to 0.1875
- up_bias: bfloat16 [4096], P('seq'), may hold values from -4 to 4
- down_weight: bfloat16 [4096, 1024], P('fsdp', 'seq'), may hold values from -0.09375 to 0.09375
- down_bias: bfloat16 [1024], P('seq'), may hold values from -4 to 4
- out_cotangent: bfloat16 [8, 2048, 1024], P('fsdp', 'seq'), may hold values from -6 to 6
Outputs:
- layer_out: bfloat16 [8, 2048, 1024], P('fsdp', 'seq')
- input_grad: bfloat16 [8, 2048, 1024], P('fsdp', 'seq')
- grad_norm1_gain: float32 [1024], P('seq')
- grad_norm1_shift: float32 [1024], P('seq')
- grad_qkv_weight: float32 [1024, 3072], P('fsdp', 'seq')
- grad_query_bias: float32 [1024], P('seq')
- grad_value_bias: float32 [1024], P('seq')
- grad_proj_weight: float32 [1024, 1024], P('fsdp', 'seq')
- grad_proj_bias: float32 [1024], P('seq')
- grad_norm2_gain: float32 [1024], P('seq')
- grad_norm2_shift: float32 [1024], P('seq')
- grad_up_weight: float32 [1024, 4096], P('fsdp', 'seq')
- grad_up_bias: float32 [4096], P('seq')
- grad_down_weight: float32 [4096, 1024], P('fsdp', 'seq')
- grad_down_bias: float32 [1024], P('seq')
The draws below stay inside these ranges and needn't reach their ends.
All inputs are finite; a program needn't handle non-finite values.
Results may differ from the reference program's by a relative error of at most 0.022.
Values may be sent and summed in bfloat16 or wider, within the bound.
A program may use at most 128 MiB of HBM per device.

```python
import jax
import jax.numpy as jnp
from jax import lax

D = 1024
H = 16
HD = 64
FF = 4096
LEN = 2048
SEQS = 8


def shard_levels(key, extent, shards, least, top_value):
    level, own = 1.0, jax.random.fold_in(key, 6)
    for position, blocks in shards:
        draws = jnp.exp(jax.random.uniform(jax.random.fold_in(own, position), (blocks,), jnp.float32, least / len(shards), top_value / len(shards)))
        level = level * jnp.repeat(draws, extent[position] // blocks).reshape([-1 if axis == position else 1 for axis in range(len(extent))])
    return level


def normal_values(key, shape, scale, bound, cuts=(), held_as=jnp.bfloat16):
    array = scale * jax.random.normal(key, shape, jnp.float32)
    if cuts:
        array = array * shard_levels(key, shape, cuts, -0.22, 0.18)
    return jnp.clip(array, -bound, bound).astype(held_as)


def setup_inputs(seed: int = 0) -> dict:
    splits = jax.random.split(jax.random.key(seed), 16)
    hidden_in = normal_values(splits[0], (SEQS, LEN, D), 1.0, 6.0, ((0, 8), (1, 16)))
    norm1_gain = jnp.clip(1.0 + 0.18 * jax.random.normal(splits[1], (D,), jnp.float32), 0.099609375, 1.8984375).astype(jnp.bfloat16)
    norm1_shift = normal_values(splits[2], (D,), 0.3, 3.0, ((0, 16),))
    qkv_weight = normal_values(splits[3], (D, 3 * D), D ** -0.5, 0.1875, ((0, 8), (1, 16)))
    query_bias = normal_values(splits[4], (D,), 0.5, 4.0, ((0, 16),))
    value_bias = normal_values(splits[5], (D,), 0.5, 4.0, ((0, 16),))
    proj_weight = normal_values(splits[6], (D, D), (D // 16) ** -0.5, 0.75, ((0, 8), (1, 16)))
    proj_bias = normal_values(splits[7], (D,), 0.5, 4.0, ((0, 16),))
    norm2_gain = jnp.clip(1.0 + 0.18 * jax.random.normal(splits[8], (D,), jnp.float32), 0.099609375, 1.8984375).astype(jnp.bfloat16)
    norm2_shift = normal_values(splits[9], (D,), 0.3, 3.0, ((0, 16),))
    up_weight = normal_values(splits[10], (D, FF), D ** -0.5, 0.1875, ((0, 8), (1, 16)))
    up_bias = normal_values(splits[11], (FF,), 0.5, 4.0, ((0, 16),))
    down_weight = normal_values(splits[12], (FF, D), FF ** -0.5, 0.09375, ((0, 8), (1, 16)))
    down_bias = normal_values(splits[13], (D,), 0.5, 4.0, ((0, 16),))
    out_cotangent = normal_values(splits[14], (SEQS, LEN, D), 1.0, 6.0, ((0, 8), (1, 16)))
    return dict(hidden_in=hidden_in, norm1_gain=norm1_gain, norm1_shift=norm1_shift, qkv_weight=qkv_weight, query_bias=query_bias, value_bias=value_bias, proj_weight=proj_weight, proj_bias=proj_bias, norm2_gain=norm2_gain, norm2_shift=norm2_shift, up_weight=up_weight, up_bias=up_bias, down_weight=down_weight, down_bias=down_bias, out_cotangent=out_cotangent)


@jax.custom_vjp
def low(v):
    return lax.optimization_barrier(v.astype(jnp.bfloat16)).astype(jnp.float32)

@jax.custom_vjp
def low_back(v):
    return v

def low_keep(v):
    return (low(v), None)

def low_pass(kept, grad):
    return (grad,)

def back_keep(v):
    return (v, None)

def back_low(kept, grad):
    return (low(grad),)
low.defvjp(low_keep, low_pass)
low_back.defvjp(back_keep, back_low)

def layer_norm(values, gain, shift):
    average = lax.optimization_barrier(jnp.mean(values, axis=-1, keepdims=True))
    centered = values - average
    spread = lax.optimization_barrier(jnp.mean(centered * centered, axis=-1, keepdims=True))
    return centered * lax.rsqrt(spread + 1e-05) * gain + shift

def attend(queries, keys, values, slopes):
    length = queries.shape[0]
    block = min(512, length)
    positions = jnp.arange(length)

    def one_block(index):
        start = index * block
        rows = lax.dynamic_slice_in_dim(queries, start, block, 0)
        raw = jnp.einsum('qhd,khd->hqk', rows, keys, precision=lax.Precision.HIGHEST)
        scores = low_back(raw) * HD ** (-0.5)
        row_pos = start + jnp.arange(block)
        offset = (positions[None, :] - row_pos[:, None]).astype(jnp.float32)
        scores = scores + slopes[:, None, None] * offset[None]
        scores = jnp.where((offset <= 0.0)[None], scores, -1e+30)
        weights = low(jax.nn.softmax(scores, axis=-1))
        return jnp.einsum('hqk,khd->qhd', weights, values, precision=lax.Precision.HIGHEST)
    blocks = lax.map(jax.checkpoint(one_block), jnp.arange(length // block))
    return blocks.reshape(length, queries.shape[1] * queries.shape[2])

def layer(seq_in, params):
    gain_one, shift_one, qkv_w, bias_query, bias_value, proj_w, bias_proj, gain_two, shift_two, up_w, bias_up, down_w, bias_down = params
    length = seq_in.shape[0]
    normed_one = low(layer_norm(seq_in, gain_one, shift_one))
    joined = jnp.dot(normed_one, qkv_w, precision=lax.Precision.HIGHEST)
    queries = low(low_back(joined[:, :D] + bias_query))
    keys = low(low_back(joined[:, D:2 * D]))
    values = low(low_back(joined[:, 2 * D:] + bias_value))
    slopes = jnp.exp2(-8.0 * (jnp.arange(H).astype(jnp.float32) + 1.0) / H)
    context = attend(queries.reshape(length, H, HD), keys.reshape(length, H, HD), values.reshape(length, H, HD), slopes)
    context = low(low_back(context))
    branch = low_back(jnp.dot(context, proj_w, precision=lax.Precision.HIGHEST) + bias_proj)
    middle = seq_in + branch
    normed_two = low(layer_norm(middle, gain_two, shift_two))
    upper = low_back(jnp.dot(normed_two, up_w, precision=lax.Precision.HIGHEST) + bias_up)
    activ = low(jax.nn.gelu(upper, approximate=True))
    down = low_back(jnp.dot(activ, down_w, precision=lax.Precision.HIGHEST) + bias_down)
    return middle + down

def reference(hidden_in, norm1_gain, norm1_shift, qkv_weight, query_bias, value_bias, proj_weight, proj_bias, norm2_gain, norm2_shift, up_weight, up_bias, down_weight, down_bias, out_cotangent):
    params = tuple((p.astype(jnp.float32) for p in (norm1_gain, norm1_shift, qkv_weight, query_bias, value_bias, proj_weight, proj_bias, norm2_gain, norm2_shift, up_weight, up_bias, down_weight, down_bias)))

    def per_sequence(totals, slices):
        seq_in, seq_cot = slices
        result, pullback = jax.vjp(layer, seq_in.astype(jnp.float32), params)
        grad_in, grad_params = pullback(seq_cot.astype(jnp.float32))
        totals = jax.tree.map(jnp.add, totals, grad_params)
        return (totals, (result.astype(jnp.bfloat16), grad_in.astype(jnp.bfloat16)))
    zeros = jax.tree.map(jnp.zeros_like, params)
    totals, (outputs, grads_in) = lax.scan(per_sequence, zeros, (hidden_in, out_cotangent))
    g_gain_one, g_shift_one, g_qkv, g_query, g_value, g_proj, g_proj_bias, g_gain_two, g_shift_two, g_up, g_up_bias, g_down, g_down_bias = totals
    return (outputs, grads_in, g_gain_one, g_shift_one, g_qkv, g_query, g_value, g_proj, g_proj_bias, g_gain_two, g_shift_two, g_up, g_up_bias, g_down, g_down_bias)
```

```python
import functools

import jax
import jax.numpy as jnp
from jax import lax
from jax.experimental import pallas as pl
from jax.experimental.pallas import tpu as pltpu
from jax.sharding import PartitionSpec as P

H = 16
HD = 64
D = 1024
HID = 256
TOK = 128
NS = 16
NF = 8
PACK = 768
MESH = pl.DeviceIdType.MESH
F32 = jnp.float32
BF16 = jnp.bfloat16
MIB = 1024 * 1024


def dot(left, right, lc=1, rc=0):
    return lax.dot_general(left, right, (((lc,), (rc,)), ((), ())), preferred_element_type=F32)


def layer_norm(values, gain, shift):
    average = jnp.mean(values, axis=-1, keepdims=True)
    centered = values - average
    spread = jnp.mean(centered * centered, axis=-1, keepdims=True)
    return centered * lax.rsqrt(spread + 1e-05) * gain + shift


def remote(src, dst, send, recv, **where):
    return pltpu.make_async_remote_copy(
        src_ref=src, dst_ref=dst, send_sem=send, recv_sem=recv, device_id=where, device_id_type=MESH
    )


def places():
    me = lax.axis_index("seq")
    core = lax.rem(me, 2)
    return me, core, me + 1 - 2 * core, lax.axis_index("fsdp")


def barrier_seq_all(me):
    sem = pltpu.get_barrier_semaphore()

    def body(k, carry):
        pl.semaphore_signal(sem, inc=1, device_id={"seq": lax.rem(me + k, NS)}, device_id_type=MESH)
        return carry

    lax.fori_loop(1, NS, body, 0)
    return sem


def barrier_fsdp(sem, row):
    def body(k, carry):
        pl.semaphore_signal(sem, inc=1, device_id={"fsdp": lax.rem(row + k, NF)}, device_id_type=MESH)
        return carry

    lax.fori_loop(1, NF, body, 0)


def loop(low, high, body):
    def step(k, carry):
        body(k)
        return carry

    lax.fori_loop(low, high, step, 0)


class Gather:
    def __init__(self, own, out, send, recv, hop):
        self.own, self.out, self.send, self.recv, self.hop = own, out, send, recv, hop
        self.me, self.core, self.sib, _ = places()

    def far(self, k):
        return lax.rem(self.me + 2 * k, NS)

    def start(self):
        me = self.me
        remote(self.own, self.out.at[me], self.send.at[0], self.recv.at[me], seq=self.sib).start()

        def body(k):
            remote(self.own, self.out.at[me], self.send.at[k], self.recv.at[me], seq=self.far(k)).start()

        loop(1, NF, body)

    def arrive(self, block):
        remote(self.out.at[block], self.out.at[block], self.send.at[0], self.recv.at[block], seq=self.sib).wait_recv()

    def relay(self, k):
        block = self.far(k)
        self.arrive(block)
        remote(self.out.at[block], self.out.at[block], self.hop.at[k], self.recv.at[block], seq=self.sib).start()

    def near(self, k):
        self.arrive(lax.rem(self.sib + 2 * k, NS))

    def drain(self):
        def body(k):
            remote(self.own, self.out.at[self.me], self.send.at[k], self.recv.at[self.me], seq=self.sib).wait_send()

        loop(0, NF, body)

        def hops(k):
            block = self.far(k)
            remote(self.out.at[block], self.out.at[block], self.hop.at[k], self.recv.at[block], seq=self.sib).wait_send()

        loop(1, NF, hops)


class Reduce:
    def __init__(self, part, pair, total, got, hop, hoprecv, send, recv):
        self.part, self.pair, self.total, self.got = part, pair, total, got
        self.hop, self.hoprecv, self.send, self.recv = hop, hoprecv, send, recv
        self.me, self.core, self.sib, _ = places()

    def put(self, k, values):
        self.part[pl.ds(2 * k, 2)] = values.astype(BF16).reshape(2, TOK, D)
        self.first(k).start()

    def first(self, k):
        return remote(
            self.part.at[2 * k + 1 - self.core], self.pair.at[k], self.hop.at[k], self.hoprecv.at[k], seq=self.sib
        )

    def second(self, k):
        return remote(
            self.total.at[k], self.got.at[k], self.send.at[k], self.recv.at[k], seq=lax.rem(self.me + 2 * k, NS)
        )

    def merge(self, k):
        self.first(k).wait_recv()
        both = self.part[2 * k + self.core].astype(F32) + self.pair[k].astype(F32)
        self.total[k] = both.astype(BF16)

        @pl.when(k > 0)
        def _():
            self.second(k).start()

    def finish(self, out):
        out[...] = self.total[0].astype(F32)

        def body(k):
            self.second(k).wait_recv()
            out[...] += self.got[k].astype(F32)

        loop(1, NF, body)

    def drain(self):
        loop(0, NF, lambda k: self.first(k).wait_send())
        loop(1, NF, lambda k: self.second(k).wait_send())


def key_extras(rows):
    lane = lax.broadcasted_iota(jnp.int32, (rows, HD), 1)
    pos = lax.broadcasted_iota(jnp.int32, (rows, HD), 0)
    high = (pos // 256) * 256
    value = jnp.where(lane < 3, high, jnp.where(lane < 6, pos - high, 0))
    return value.astype(F32).astype(BF16)


def query_extras(slope_ref):
    return jnp.broadcast_to(slope_ref[...], (HD, 256))


def kernel_a(
    hid_ref, cot_ref, pack_ref, sml_ref, qvb_ref, slope_ref,
    nrm, cota, qkvt, qkvr, lse, mid, n2, ctxr, wq, up, dn, pj, sm,
    hid, wf, smb, wqo, dno, pjo, kr, ctxo, ctxt,
    h_s, h_r, h_h, c_s, c_r, c_h, p_s, p_r, p_h, w_s, w_r, m_s, m_r, q_s, q_r, d_s, d_r, x_s, x_r, l_s,
):
    me, core, sib, row = places()
    sem = barrier_seq_all(me)
    barrier_fsdp(sem, row)
    pl.semaphore_wait(sem, NS - 1 + NF - 1)

    def to_row(k):
        return remote(pack_ref, wf.at[row], w_s.at[k], w_r.at[row], fsdp=lax.rem(row + k, NF))

    def small_to(k):
        return remote(sml_ref, smb.at[me], m_s.at[k], m_r.at[me], seq=lax.rem(me + k, NS))

    loop(1, NF, lambda k: to_row(k).start())
    loop(1, NS, lambda k: small_to(k).start())
    hidden = Gather(hid_ref, hid, h_s, h_r, h_h)
    hidden.start()
    cot_own = pltpu.make_async_copy(cot_ref, cota.at[me], l_s)
    cot_own.start()
    wf[row] = pack_ref[...]
    smb[me] = sml_ref[...]
    hid[me] = hid_ref[...]
    kr[:, HD:] = key_extras(NS * TOK)

    def from_row(k):
        other = lax.rem(row + k, NF)
        remote(pack_ref, wf.at[other], w_s.at[k], w_r.at[other], fsdp=other).wait_recv()

    loop(1, NF, from_row)
    for f in range(NF):
        lanes = slice(f * 128, f * 128 + 128)
        wqo[:, lanes] = wf[f, 0:192, :]
        pjo[:, lanes] = wf[f, 192:256, :]
        up[lanes, 0:128] = wf[f, 512:640, :]
        up[lanes, 128:256] = wf[f, 640:768, :]
        for half in range(2):
            for piece in range(2):
                at = 256 + (2 * half + piece) * 64
                dno[2 * f + half, :, piece * 128 : piece * 128 + 128] = wf[f, at : at + 64, :]

    def q_block(j):
        block = 3 * me + j
        kind, head = block // H, lax.rem(block, H)
        src = wqo.at[pl.ds(j * HD, HD), :]
        dst = wq.at[pl.ds(pl.multiple_of(kind * HD, HD), HD), :]
        return head, kind, src, dst

    for j in range(3):
        head, kind, src, dst = q_block(j)

        @pl.when(head != me)
        def _():
            remote(src, dst, q_s.at[j], q_r.at[kind], seq=head).start()

        @pl.when(head == me)
        def _():
            dst[...] = src[...]

    def down_to(k):
        other = lax.rem(me + k, NS)
        return remote(
            dno.at[other], dn.at[pl.ds(pl.multiple_of(me * HD, HD), HD), :], d_s.at[k], d_r.at[me], seq=other
        )

    def down_from(k):
        other = lax.rem(me + k, NS)
        remote(
            dno.at[me], dn.at[pl.ds(pl.multiple_of(other * HD, HD), HD), :], d_s.at[k], d_r.at[other], seq=other
        ).wait_recv()

    loop(1, NS, lambda k: down_to(k).start())
    dn[pl.ds(pl.multiple_of(me * HD, HD), HD), :] = dno[me]
    proj = Gather(pjo, pj, p_s, p_r, p_h)
    proj.start()
    pj[me] = pjo[...]

    def small_from(k):
        other = lax.rem(me + k, NS)
        remote(sml_ref, smb.at[other], m_s.at[k], m_r.at[other], seq=other).wait_recv()

    loop(1, NS, small_from)
    for t in range(NF):
        sm[:, t * 128 : t * 128 + 128] = smb[2 * t].astype(F32) + smb[2 * t + 1].astype(F32)

    for kind in range(3):

        @pl.when((kind * H + me) // 3 != me)
        def _():
            remote(
                wqo.at[pl.ds(0, HD), :], wq.at[pl.ds(kind * HD, HD), :], q_s.at[0], q_r.at[kind], seq=sib
            ).wait_recv()

    def norm_and_project(k):
        @pl.when(k > 0)
        def _():
            hidden.relay(k)

        hidden.near(k)
        m = lax.rem(me // 2 + k, NF)
        values = hid[pl.ds(2 * m, 2)].reshape(2 * TOK, D).astype(F32)
        normed = layer_norm(values, sm[0:1, :], sm[1:2, :]).astype(BF16)
        nrm[pl.ds(2 * m, 2)] = normed.reshape(2, TOK, D)
        block = dot(wq[...], normed, 1, 1) + qvb_ref[:, 0:1]
        qkvt[m] = block.astype(BF16)
        at = pl.ds(pl.multiple_of(m * 256, 256), 256)
        qkvr[0, at, :] = block[0:64].T.astype(BF16)
        keys = block[64:128].T.astype(BF16)
        qkvr[1, at, :] = keys
        kr[at, 0:HD] = keys
        qkvr[2, at, :] = block[128:192].T.astype(BF16)

    loop(0, NF, norm_and_project)
    cot = Gather(cot_ref, cota, c_s, c_r, c_h)
    cot.start()

    extras = query_extras(slope_ref)

    def ctx_to(j):
        return remote(ctxo.at[j], ctxt.at[me], x_s.at[j], x_r.at[me], seq=j)

    for j in range(NF):
        n = (j + 1) * 256
        queries = jnp.concatenate([(qkvt[j, 0:64, :].astype(F32) * 0.125).astype(BF16), extras], axis=0)
        scores = dot(kr[0:n, :], queries)
        kpos = lax.broadcasted_iota(jnp.int32, (256, 256), 0)
        qpos = lax.broadcasted_iota(jnp.int32, (256, 256), 1)
        last = jnp.where(kpos <= qpos, scores[n - 256 :], -1e30)
        scores = last if j == 0 else jnp.concatenate([scores[: n - 256], last], axis=0)
        peak = jnp.max(scores, axis=0, keepdims=True)
        expo = jnp.exp(scores - peak)
        total = jnp.sum(expo, axis=0, keepdims=True)
        lse[j : j + 1, :] = peak + jnp.log(total)
        weights = expo.astype(BF16)
        acc = dot(qkvt[0, 128:192, :], weights[0:256])
        for i in range(1, j + 1):
            acc += dot(qkvt[i, 128:192, :], weights[i * 256 : i * 256 + 256])
        context = (acc / total).astype(BF16)
        for half in range(2):
            target = 2 * j + half
            ctxo[target] = context[:, half * 128 : half * 128 + 128]

            @pl.when(me != target)
            def _():
                ctx_to(target).start()

            @pl.when(me == target)
            def _():
                ctxt[target] = ctxo[target]

    loop(1, NF, proj.relay)
    loop(0, NF, proj.near)

    def ctx_from(k):
        other = lax.rem(me + k, NS)
        remote(ctxo.at[other], ctxt.at[other], x_s.at[other], x_r.at[other], seq=other).wait_recv()

    loop(1, NS, ctx_from)
    context = ctxt[...].reshape(D, TOK).astype(F32).T.astype(BF16)
    ctxr[...] = context
    middle = hid_ref[...].astype(F32) + dot(context, pj[...].reshape(D, D), 1, 1) + sm[2:3, :]
    mid[...] = middle
    n2[...] = layer_norm(middle, sm[3:4, :], sm[4:5, :]).astype(BF16)

    loop(1, NS, down_from)
    loop(1, NF, cot.relay)
    loop(0, NF, cot.near)
    cot_own.wait()
    hidden.drain()
    cot.drain()
    proj.drain()
    loop(1, NF, lambda k: to_row(k).wait_send())
    loop(1, NS, lambda k: small_to(k).wait_send())
    loop(1, NS, lambda k: down_to(k).wait_send())
    for j in range(3):
        head, kind, src, dst = q_block(j)

        @pl.when(head != me)
        def _():
            remote(src, dst, q_s.at[j], q_r.at[kind], seq=head).wait_send()

    def ctx_sent(k):
        other = lax.rem(me + k, NS)
        remote(ctxo.at[other], ctxt.at[me], x_s.at[other], x_r.at[me], seq=other).wait_send()

    loop(1, NS, ctx_sent)


def vm():
    return pl.BlockSpec(memory_space=pltpu.VMEM)


def hbm():
    return pl.BlockSpec(memory_space=pl.ANY)


def sems(*counts):
    return [pltpu.SemaphoreType.DMA((n,)) for n in counts]


def params(number):
    return pltpu.CompilerParams(collective_id=number, has_side_effects=True, vmem_limit_bytes=56 * MIB)


def run_a(hid, cot, pack, small, qvb, slope):
    shapes = [
        ((NS, TOK, D), BF16), ((NS, TOK, D), BF16), ((NF, 192, 256), BF16), ((3, NS * TOK, HD), BF16),
        ((NF, 256), F32), ((TOK, D), F32), ((TOK, D), BF16), ((TOK, D), BF16), ((192, D), BF16),
        ((D, HID), BF16), ((D, HID), BF16), ((NS, HD, D), BF16), ((16, D), F32),
    ]
    specs = [vm() for _ in shapes]
    specs[1] = hbm()
    return pl.pallas_call(
        kernel_a,
        out_shape=[jax.ShapeDtypeStruct(*s) for s in shapes],
        in_specs=[vm(), hbm(), vm(), vm(), vm(), vm()],
        out_specs=specs,
        scratch_shapes=[
            pltpu.VMEM((NS, TOK, D), BF16),
            pltpu.VMEM((NF, PACK, 128), BF16),
            pltpu.VMEM((NS, 16, 128), BF16),
            pltpu.VMEM((192, D), BF16),
            pltpu.VMEM((NS, HD, HID), BF16),
            pltpu.VMEM((HD, D), BF16),
            pltpu.VMEM((NS * TOK, 128), BF16),
            pltpu.VMEM((NS, HD, TOK), BF16),
            pltpu.VMEM((NS, HD, TOK), BF16),
        ]
        + sems(8, 16, 8, 8, 16, 8, 8, 16, 8, 8, 8, 16, 16, 3, 3, 16, 16, 16, 16)
        + [pltpu.SemaphoreType.DMA],
        compiler_params=params(0),
        name="gather_attend",
    )(hid, cot, pack, small, qvb, slope)


def kernel_m(
    n2_ref, cot_ref, up_ref, dn_ref, ub_ref,
    gn2, dsum, gup, gdn, gub,
    xa, act, gu, g_part, g_pair, g_total, g_got, d_part, d_pair, d_total, d_got,
    n_s, n_r, n_h, g1s, g1r, g2s, g2r, d1s, d1r, d2s, d2r,
):
    me, core, sib, _ = places()
    sem = pltpu.get_barrier_semaphore()
    pl.semaphore_signal(sem, inc=1, device_id={"seq": sib}, device_id_type=MESH)

    def greet(k):
        pl.semaphore_signal(sem, inc=1, device_id={"seq": lax.rem(me + 2 * k, NS)}, device_id_type=MESH)

    loop(1, NF, greet)
    pl.semaphore_wait(sem, NF)
    tokens = Gather(n2_ref, xa, n_s, n_r, n_h)
    tokens.start()
    xa[me] = n2_ref[...]
    grads = Reduce(g_part, g_pair, g_total, g_got, g1s, g1r, g2s, g2r)
    downs = Reduce(d_part, d_pair, d_total, d_got, d1s, d1r, d2s, d2r)
    gub[...] = jnp.zeros_like(gub)

    def step(k):
        @pl.when(k > 0)
        def _():
            tokens.relay(k)

        tokens.near(k)
        m = lax.rem(me // 2 + k, NF)
        rows = xa[pl.ds(2 * m, 2)].reshape(2 * TOK, D)
        upper = dot(rows, up_ref[...]) + ub_ref[...]
        square = upper * upper
        bend = jnp.tanh(0.7978845608 * upper * (1.0 + 0.044715 * square))
        half = 0.5 * (1.0 + bend)
        active = (upper * half).astype(BF16)
        slope = half + 0.5 * upper * (1.0 - bend * bend) * (0.7978845608 * (1.0 + 0.134145 * square))
        cots = cot_ref[pl.ds(2 * m, 2)].reshape(2 * TOK, D)
        grad = (dot(cots, dn_ref[...]) * slope).astype(BF16)
        at = pl.ds(pl.multiple_of(m * 256, 256), 256)
        act[at, :] = active
        gu[at, :] = grad
        gub[0:1, :] += jnp.sum(grad.astype(F32), axis=0, keepdims=True)
        grads.put(k, dot(grad, up_ref[...], 1, 1))
        downs.put(k, dot(active, dn_ref[...], 1, 1))

        @pl.when(k > 0)
        def _():
            grads.merge(k - 1)
            downs.merge(k - 1)

    loop(0, NF, step)
    grads.merge(NF - 1)
    downs.merge(NF - 1)
    gup[...] = dot(xa[...].reshape(NS * TOK, D), gu[...], 0, 0).astype(BF16)
    gdn[...] = dot(cot_ref[...].reshape(NS * TOK, D), act[...], 0, 0).astype(BF16)
    grads.finish(gn2)
    downs.finish(dsum)
    tokens.drain()
    grads.drain()
    downs.drain()


def reduce_scratch():
    return [
        pltpu.VMEM((NS, TOK, D), BF16),
        pltpu.VMEM((NF, TOK, D), BF16),
        pltpu.VMEM((NF, TOK, D), BF16),
        pltpu.VMEM((NF, TOK, D), BF16),
    ]


def run_m(n2, cot, up, dn, ub):
    shapes = [((TOK, D), F32), ((TOK, D), F32), ((D, HID), BF16), ((D, HID), BF16), ((8, HID), F32)]
    return pl.pallas_call(
        kernel_m,
        out_shape=[jax.ShapeDtypeStruct(*s) for s in shapes],
        in_specs=[vm()] * 5,
        out_specs=[vm()] * 5,
        scratch_shapes=[
            pltpu.VMEM((NS, TOK, D), BF16),
            pltpu.VMEM((NS * TOK, HID), BF16),
            pltpu.VMEM((NS * TOK, HID), BF16),
        ]
        + reduce_scratch()
        + reduce_scratch()
        + sems(8, 16, 8, 8, 8, 8, 8, 8, 8, 8, 8),
        compiler_params=params(1),
        name="feed_forward",
    )(n2, cot, up, dn, ub)


def kernel_b(
    gc_ref, qkvt, qkvr, lse, wq, nrm, slope_ref,
    gn1, gqkv, gsum,
    dct, gjt, kr, dk, dv, part, pair, total, got,
    x_s, x_r, r1s, r1r, r2s, r2r,
):
    me, core, sib, _ = places()
    sem = barrier_seq_all(me)
    pl.semaphore_wait(sem, NS - 1)

    def ctx_to(k):
        other = lax.rem(me + k, NS)
        return remote(gc_ref.at[other], dct.at[me], x_s.at[k], x_r.at[me], seq=other)

    def ctx_from(k):
        other = lax.rem(me + k, NS)
        remote(gc_ref.at[me], dct.at[other], x_s.at[k], x_r.at[other], seq=other).wait_recv()

    loop(1, NS, lambda k: ctx_to(k).start())
    dct[me] = gc_ref[me]
    kr[:, HD:] = key_extras(NS * TOK)
    kr[:, 0:HD] = qkvr[1]
    dk[...] = jnp.zeros_like(dk)
    dv[...] = jnp.zeros_like(dv)
    extras = query_extras(slope_ref)
    loop(1, NS, ctx_from)
    for j in range(NF):
        n = (j + 1) * 256
        at = slice(j * 256, n)
        queries = jnp.concatenate([(qkvt[j, 0:64, :].astype(F32) * 0.125).astype(BF16), extras], axis=0)
        scores = dot(kr[0:n, :], queries)
        probs = jnp.exp(scores - lse[j : j + 1, :])
        kpos = lax.broadcasted_iota(jnp.int32, (256, 256), 0)
        qpos = lax.broadcasted_iota(jnp.int32, (256, 256), 1)
        last = jnp.where(kpos <= qpos, probs[n - 256 :], 0.0)
        probs = last if j == 0 else jnp.concatenate([probs[: n - 256], last], axis=0)
        gctx = jnp.concatenate([dct[2 * j], dct[2 * j + 1]], axis=1)
        gprobs = dot(qkvr[2, 0:n, :], gctx)
        inner = jnp.sum(probs * gprobs, axis=0, keepdims=True)
        gscores = (probs * (gprobs - inner) * 0.125).astype(BF16)
        gq = dot(qkvt[0, 64:128, :], gscores[0:256])
        for i in range(1, j + 1):
            gq += dot(qkvt[i, 64:128, :], gscores[i * 256 : i * 256 + 256])
        gjt[j, 0:64, :] = gq.astype(BF16)
        dk[0:n, :] += dot(gscores, qkvr[0, at, :])
        dv[0:n, :] += dot(probs.astype(BF16), gctx.astype(F32).T.astype(BF16))
    for j in range(NF):
        at = slice(j * 256, j * 256 + 256)
        gjt[j, 64:128, :] = dk[at, :].T.astype(BF16)
        gjt[j, 128:192, :] = dv[at, :].T.astype(BF16)

    norms = Reduce(part, pair, total, got, r1s, r1r, r2s, r2r)

    def step(k):
        m = lax.rem(me // 2 + k, NF)
        rows = gjt[m].astype(F32).T.astype(BF16)
        norms.put(k, dot(rows, wq[...]))

        @pl.when(k > 0)
        def _():
            norms.merge(k - 1)

    loop(0, NF, step)
    norms.merge(NF - 1)
    acc = jnp.zeros((192, D), F32)
    sums = jnp.zeros((192, 1), F32)
    for j in range(NF):
        acc += dot(gjt[j], nrm[2 * j : 2 * j + 2].reshape(2 * TOK, D))
        sums += jnp.sum(gjt[j].astype(F32), axis=1, keepdims=True)
    gqkv[...] = acc.astype(BF16)
    gsum[...] = jnp.broadcast_to(sums, (192, 128))
    norms.finish(gn1)
    norms.drain()
    loop(1, NS, lambda k: ctx_to(k).wait_send())


def run_b(gc, qkvt, qkvr, lse, wq, nrm, slope):
    shapes = [((TOK, D), F32), ((192, D), BF16), ((192, 128), F32)]
    return pl.pallas_call(
        kernel_b,
        out_shape=[jax.ShapeDtypeStruct(*s) for s in shapes],
        in_specs=[vm()] * 7,
        out_specs=[vm()] * 3,
        scratch_shapes=[
            pltpu.VMEM((NS, HD, TOK), BF16),
            pltpu.VMEM((NF, 192, 256), BF16),
            pltpu.VMEM((NS * TOK, 128), BF16),
            pltpu.VMEM((NS * TOK, HD), F32),
            pltpu.VMEM((NS * TOK, HD), F32),
        ]
        + reduce_scratch()
        + sems(16, 16, 8, 8, 8, 8),
        compiler_params=params(2),
        name="attend_back",
    )(gc, qkvt, qkvr, lse, wq, nrm, slope)


def kernel_c(
    gdn, gup, gqkv, gpj, token_ref, local_ref,
    out, small,
    d1, j1, q1, m1, pack, got, m2, sgot,
    d_s, d_r, j_s, j_r, q_s, q_r, m_s, m_r, w_s, w_r, v_s, v_r,
):
    me, core, sib, row = places()
    sem = barrier_seq_all(me)
    barrier_fsdp(sem, row)
    pl.semaphore_wait(sem, NS - 1 + NF - 1)

    def block(other):
        return pl.ds(pl.multiple_of(other * HD, HD), HD)

    def down(k):
        other = lax.rem(me + k, NS)
        return remote(gdn.at[block(other), :], d1.at[me], d_s.at[k], d_r.at[me], seq=other)

    def proj(k):
        other = lax.rem(me + k, NS)
        return remote(gpj.at[block(other), :], j1.at[me], j_s.at[k], j_r.at[me], seq=other)

    def tokens(k):
        other = lax.rem(me + k, NS)
        return remote(token_ref.at[other // 2], m1.at[me], m_s.at[k], m_r.at[me], seq=other)

    def q_block(kind):
        index = kind * H + me
        holder, slot = index // 3, lax.rem(index, 3)
        src = gqkv.at[pl.ds(kind * HD, HD), :]
        dst = q1.at[block(slot), :]
        return holder, slot, src, dst

    for kind in range(3):
        holder, slot, src, dst = q_block(kind)

        @pl.when(holder != me)
        def _():
            remote(src, dst, q_s.at[kind], q_r.at[slot], seq=holder).start()

        @pl.when(holder == me)
        def _():
            dst[...] = src[...]

    def send(k):
        tokens(k).start()
        down(k).start()
        proj(k).start()

    loop(1, NS, send)
    d1[me] = gdn[block(me), :]
    j1[me] = gpj[block(me), :]
    m1[me] = token_ref[me // 2]

    def receive(k):
        other = lax.rem(me + k, NS)
        remote(token_ref.at[0], m1.at[other], m_s.at[k], m_r.at[other], seq=other).wait_recv()
        remote(gdn.at[block(me), :], d1.at[other], d_s.at[k], d_r.at[other], seq=other).wait_recv()
        remote(gpj.at[block(me), :], j1.at[other], j_s.at[k], j_r.at[other], seq=other).wait_recv()

    loop(1, NS, receive)
    for slot in range(3):

        @pl.when(lax.rem(3 * me + slot, H) != me)
        def _():
            remote(
                gqkv.at[pl.ds(0, HD), :], q1.at[pl.ds(slot * HD, HD), :], q_s.at[0], q_r.at[slot], seq=sib
            ).wait_recv()

    projs = j1[0].astype(F32)
    local = m1[0]
    for p in range(1, NS):
        projs += j1[p].astype(F32)
        local += m1[p]
    m2[0:8, :] = local
    m2[8:16, :] = local_ref[...]
    for f in range(NF):
        lanes = slice(f * 128, f * 128 + 128)
        pack[f, 0:192, :] = q1[:, lanes]
        pack[f, 192:256, :] = projs[:, lanes].astype(BF16)
        for half in range(2):
            for piece in range(2):
                at = 256 + (2 * half + piece) * 64
                pack[f, at : at + 64, :] = d1[2 * f + half, :, piece * 128 : piece * 128 + 128]
        pack[f, 512:640, :] = gup[lanes, 0:128]
        pack[f, 640:768, :] = gup[lanes, 128:256]

    def rows(k):
        other = lax.rem(row + k, NF)
        return remote(pack.at[other], got.at[row], w_s.at[k], w_r.at[row], fsdp=other)

    def vectors(k):
        other = lax.rem(row + k, NF)
        return remote(m2, sgot.at[row], v_s.at[k], v_r.at[row], fsdp=other)

    def send_rows(k):
        vectors(k).start()
        rows(k).start()

    loop(1, NF, send_rows)
    got[row] = pack[row]
    sgot[row] = m2[...]

    def receive_rows(k):
        other = lax.rem(row + k, NF)
        remote(m2, sgot.at[other], v_s.at[k], v_r.at[other], fsdp=other).wait_recv()
        remote(pack.at[other], got.at[other], w_s.at[k], w_r.at[other], fsdp=other).wait_recv()

    loop(1, NF, receive_rows)
    total = got[0].astype(F32)
    vector = sgot[0]
    for f in range(1, NF):
        total += got[f].astype(F32)
        vector += sgot[f]
    out[...] = total
    small[...] = vector

    def sent(k):
        tokens(k).wait_send()
        down(k).wait_send()
        proj(k).wait_send()

    loop(1, NS, sent)

    def rows_sent(k):
        vectors(k).wait_send()
        rows(k).wait_send()

    loop(1, NF, rows_sent)
    for kind in range(3):
        holder, slot, src, dst = q_block(kind)

        @pl.when(holder != me)
        def _():
            remote(src, dst, q_s.at[kind], q_r.at[slot], seq=holder).wait_send()


def run_c(gdn, gup, gqkv, gpj, token, local):
    shapes = [((PACK, 128), F32), ((16, 128), F32)]
    return pl.pallas_call(
        kernel_c,
        out_shape=[jax.ShapeDtypeStruct(*s) for s in shapes],
        in_specs=[vm()] * 6,
        out_specs=[vm()] * 2,
        scratch_shapes=[
            pltpu.VMEM((NS, HD, HID), BF16),
            pltpu.VMEM((NS, HD, D), BF16),
            pltpu.VMEM((192, D), BF16),
            pltpu.VMEM((NS, 8, 128), F32),
            pltpu.VMEM((NF, PACK, 128), BF16),
            pltpu.VMEM((NF, PACK, 128), BF16),
            pltpu.VMEM((16, 128), F32),
            pltpu.VMEM((NF, 16, 128), F32),
        ]
        + sems(16, 16, 16, 16, 3, 3, 16, 16, 8, 8, 8, 8),
        compiler_params=params(3),
        name="sum_weights",
    )(gdn, gup, gqkv, gpj, token, local)


def per_device(
    hidden_in, norm1_gain, norm1_shift, qkv_weight, query_bias, value_bias, proj_weight, proj_bias,
    norm2_gain, norm2_shift, up_weight, up_bias, down_weight, down_bias, out_cotangent,
):
    hid, cot = hidden_in[0], out_cotangent[0]
    me = lax.axis_index("seq")
    even = lax.rem(me, 2) == 0
    down_t = down_weight.T.reshape(HD, 4, 128).transpose(1, 0, 2).reshape(256, 128)
    up_r = up_weight.reshape(128, 2, 128).transpose(1, 0, 2).reshape(256, 128)
    pack = jnp.concatenate([qkv_weight.T, proj_weight.T, down_t, up_r], axis=0)
    vectors = jnp.stack([norm1_gain, norm1_shift, proj_bias, norm2_gain, norm2_shift, down_bias])
    none = jnp.zeros_like(vectors)
    vectors = jnp.concatenate([jnp.where(even, vectors, none), jnp.where(even, none, vectors)], axis=1)
    small = jnp.pad(vectors, ((0, 10), (0, 0)))
    qvb = jnp.concatenate([query_bias, jnp.zeros_like(query_bias), value_bias]).astype(F32)
    qvb = jnp.broadcast_to(qvb[:, None], (192, 128))
    slope = jnp.exp2(-8.0 * (me.astype(F32) + 1.0) / H)
    first = lax.reduce_precision(slope, 8, 7)
    second = lax.reduce_precision(slope - first, 8, 7)
    third = lax.reduce_precision(slope - first - second, 8, 7)
    parts = jnp.stack([first, second, third, first, second, third])
    slopes = jnp.pad(parts, (0, HD - 6)).astype(BF16)
    slopes = jnp.broadcast_to(slopes[:, None], (HD, 256))

    (nrm, cota, qkvt, qkvr, lse, middle, n2, ctx, wq, up, dn, pj, sm) = run_a(hid, cot, pack, small, qvb, slopes)
    gn2, down_sum, gup, gdn, gub = run_m(n2, cota, up, dn, up_bias.astype(F32)[None])
    layer_out = middle + down_sum + sm[5]

    pull = jax.vjp(layer_norm, middle, sm[3], sm[4])[1]
    grad_mid_norm, grad_gain_two, grad_shift_two = pull(gn2)
    cot32 = cot.astype(F32)
    grad_middle = cot32 + grad_mid_norm
    branch = grad_middle.astype(BF16)
    projection = pj.reshape(D, D)
    gpj = dot(branch, ctx, 0, 0).astype(BF16)
    gctx = dot(projection, branch, 0, 1).astype(BF16).reshape(NS, HD, TOK)
    gn1, gqkv, gsum = run_b(gctx, qkvt, qkvr, lse, wq, nrm, slopes)
    pull = jax.vjp(layer_norm, hid.astype(F32), sm[0], sm[1])[1]
    grad_in_norm, grad_gain_one, grad_shift_one = pull(gn1)
    input_grad = grad_middle + grad_in_norm

    nothing = jnp.zeros((D,), F32)
    token = jnp.stack(
        [
            grad_gain_one, grad_shift_one, jnp.sum(branch.astype(F32), axis=0), grad_gain_two, grad_shift_two,
            jnp.sum(cot32, axis=0), nothing, nothing,
        ]
    )
    token = token.reshape(8, 8, 128).transpose(1, 0, 2)
    head = jnp.concatenate([gsum[0:64, 0], gsum[128:192, 0]])[None]
    local = jnp.concatenate([head, gub[0].reshape(2, 128), jnp.zeros((5, 128), F32)], axis=0)
    out, vecs = run_c(gdn, gup, gqkv, gpj, token, local)
    mine = jnp.where(even, vecs[:6, :64], vecs[:6, 64:])
    return (
        layer_out.astype(BF16)[None],
        input_grad.astype(BF16)[None],
        mine[0],
        mine[1],
        out[0:192].T,
        vecs[8, :64],
        vecs[8, 64:],
        out[192:256].T,
        mine[2],
        mine[3],
        mine[4],
        out[512:768].reshape(2, 128, 128).transpose(1, 0, 2).reshape(128, 256),
        vecs[9:11].reshape(256),
        out[256:512].reshape(4, HD, 128).transpose(0, 2, 1).reshape(512, HD),
        mine[5],
    )


def solution(mesh):
    act, vec, mat = P("fsdp", "seq", None), P("seq"), P("fsdp", "seq")
    return jax.shard_map(
        per_device,
        mesh=mesh,
        in_specs=(act, vec, vec, mat, vec, vec, mat, vec, vec, vec, mat, vec, mat, vec, act),
        out_specs=(act, act, vec, vec, mat, vec, vec, mat, vec, vec, vec, mat, vec, mat, vec),
        check_vma=False,
    )
```

```python
import functools

import jax
import jax.numpy as jnp
from jax import lax
from jax.experimental import pallas as pl
from jax.experimental.pallas import tpu as pltpu
from jax.sharding import PartitionSpec as P

H = 16
HD = 64
D = 1024
HID = 256
TOK = 128
NS = 16
NF = 8
PACK = 768
MESH = pl.DeviceIdType.MESH
F32 = jnp.float32
BF16 = jnp.bfloat16
MIB = 1024 * 1024


def dot(left, right, lc=1, rc=0):
    return lax.dot_general(left, right, (((lc,), (rc,)), ((), ())), preferred_element_type=F32)


def layer_norm(values, gain, shift):
    average = jnp.mean(values, axis=-1, keepdims=True)
    centered = values - average
    spread = jnp.mean(centered * centered, axis=-1, keepdims=True)
    return centered * lax.rsqrt(spread + 1e-05) * gain + shift


def remote(src, dst, send, recv, **where):
    return pltpu.make_async_remote_copy(
        src_ref=src, dst_ref=dst, send_sem=send, recv_sem=recv, device_id=where, device_id_type=MESH
    )


def places():
    me = lax.axis_index("seq")
    core = lax.rem(me, 2)
    return me, core, me + 1 - 2 * core, lax.axis_index("fsdp")


def barrier_seq_all(me):
    sem = pltpu.get_barrier_semaphore()

    def body(k, carry):
        pl.semaphore_signal(sem, inc=1, device_id={"seq": lax.rem(me + k, NS)}, device_id_type=MESH)
        return carry

    lax.fori_loop(1, NS, body, 0)
    return sem


def barrier_fsdp(sem, row):
    def body(k, carry):
        pl.semaphore_signal(sem, inc=1, device_id={"fsdp": lax.rem(row + k, NF)}, device_id_type=MESH)
        return carry

    lax.fori_loop(1, NF, body, 0)


def loop(low, high, body):
    def step(k, carry):
        body(k)
        return carry

    lax.fori_loop(low, high, step, 0)


class Chips:
    def __init__(self):
        self.me, self.core, self.sib, self.row = places()
        self.own = self.me // 2
        step = 1 - 2 * lax.rem(self.own, 2)
        self.y = self.own + step
        self.r, self.f, self.l = (lax.rem(self.own + d, NF) for d in (2, 4, 6))
        self.ry, self.fy, self.ly = self.r + step, self.f + step, self.l + step

    def at(self, k):
        j = k // 2
        ring = lax.rem(self.own // 2 + j + (j // 2) * (5 - 2 * j), 4)
        return 2 * ring + lax.rem(self.own + k, 2)

    def device(self, chip):
        return 2 * chip + self.core


class Gather:
    def __init__(self, chips, own, out, send, recv, near):
        self.c, self.own, self.out, self.send, self.recv, self.near_sem = chips, own, out, send, recv, near
        rows = out.shape[1] // 2
        self.halves = (pl.ds(0, rows), pl.ds(rows, rows))

    def message(self, i, chip, half, to):
        c = self.c
        dst = self.out.at[c.device(chip), self.halves[half]]
        src = self.own.at[self.halves[half]] if i < 6 else dst
        return remote(src, dst, self.send.at[i], self.recv.at[chip, half], seq=c.device(to))

    def messages(self):
        c = self.c
        plan = [
            (c.own, 0, c.r), (c.own, 1, c.l), (c.own, 0, c.y), (c.own, 1, c.r), (c.own, 0, c.l), (c.own, 1, c.y),
            (c.l, 0, c.r), (c.r, 1, c.l), (c.y, 0, c.r), (c.y, 0, c.l), (c.y, 1, c.r), (c.y, 1, c.l),
            (c.f, 0, c.y), (c.f, 1, c.y),
        ]
        return [functools.partial(self.message, i, *p) for i, p in enumerate(plan)]

    def begin(self, *which):
        plan = self.messages()
        for i in which:
            plan[i]().start()

    def arrive(self, chip, half):
        self.message(6, chip, half, self.c.own).wait_recv()

    def hand(self, chip, first=False):
        block = self.c.device(chip)
        src = self.own if first else self.out.at[block]
        return remote(src, self.out.at[block], self.send.at[14 + chip], self.near_sem.at[chip], seq=self.c.sib)

    def near(self, chip):
        block = 2 * chip + 1 - self.c.core
        remote(
            self.out.at[block], self.out.at[block], self.send.at[0], self.near_sem.at[chip], seq=self.c.sib
        ).wait_recv()

    def start(self):
        self.begin(0, 1, 2, 3, 4, 5)
        self.hand(self.c.own, True).start()

    def pass_x(self):
        c = self.c
        self.arrive(c.l, 0)
        self.begin(6)
        self.arrive(c.r, 1)
        self.begin(7)

    def pass_y(self):
        c = self.c
        self.arrive(c.y, 0)
        self.begin(8, 9)
        self.arrive(c.y, 1)
        self.begin(10, 11)
        self.hand(c.y).start()

    def pass_f(self):
        c = self.c
        self.arrive(c.f, 0)
        self.begin(12)
        self.arrive(c.f, 1)
        self.begin(13)
        self.hand(c.f).start()

    def take(self, name):
        c = self.c
        chip = getattr(c, name)
        for half in {"r": (0,), "l": (1,)}.get(name, (0, 1)):
            self.arrive(chip, half)
        self.hand(chip).start()

    def step(self, k):
        @pl.when(k == 1)
        def _():
            self.pass_x()
            self.pass_y()

        @pl.when(k == 2)
        def _():
            self.take("r")

        @pl.when(k == 3)
        def _():
            self.pass_f()
            self.take("ry")

        @pl.when(k == 4)
        def _():
            self.take("l")

        @pl.when(k == 5)
        def _():
            self.take("ly")

        @pl.when(k == 7)
        def _():
            self.take("fy")

        self.near(self.c.at(k))

    def finish(self):
        for name in ("r", "ry", "l", "ly", "fy"):
            self.take(name)
        loop(0, NF, self.near)

    def drain(self):
        for message in self.messages():
            message().wait_send()
        loop(0, NF, lambda chip: self.hand(chip, True).wait_send())


class Reduce:
    def __init__(self, chips, part, pair, total, got, hop, hop_recv, send, recv):
        self.c, self.part, self.pair, self.total, self.got = chips, part, pair, total, got
        self.hop, self.hop_recv, self.send, self.recv = hop, hop_recv, send, recv
        rows = total.shape[1]
        self.low, self.high, self.all = pl.ds(0, rows // 2), pl.ds(rows // 2, rows // 2), pl.ds(0, rows)

    def pairing(self, chip):
        src = self.part.at[2 * chip + 1 - self.c.core]
        return remote(src, self.pair.at[chip], self.hop.at[chip], self.hop_recv.at[chip], seq=self.c.sib)

    def merge(self, chip):
        self.pairing(chip).wait_recv()
        both = self.part[self.c.device(chip)].astype(F32) + self.pair[chip].astype(F32)
        self.total[chip] = both.astype(BF16)

    def message(self, i):
        c = self.c
        chip, rows, slot, to = (
            (c.fy, self.low, 0, c.y), (c.fy, self.high, 0, c.y), (c.ly, self.all, 3, c.l), (c.ry, self.all, 2, c.r),
            (c.r, self.high, 4, c.r), (c.l, self.low, 5, c.l), (c.f, self.low, 1, c.r), (c.f, self.high, 1, c.l),
            (c.r, self.low, 4, c.r), (c.l, self.high, 5, c.l), (c.y, self.all, 6, c.y),
        )[i]
        return remote(
            self.total.at[chip, rows], self.got.at[slot, rows], self.send.at[i], self.recv.at[i], seq=c.device(to)
        )

    def begin(self, *which):
        for i in which:
            self.message(i).start()

    def add(self, i, chip, slot, rows):
        self.message(i).wait_recv()
        both = self.total[chip, rows].astype(F32) + self.got[slot, rows].astype(F32)
        self.total[chip, rows] = both.astype(BF16)

    def far(self):
        self.begin(0, 1)

    def sides(self):
        self.begin(2, 3, 4, 5)

    def turn(self):
        c = self.c
        self.add(0, c.f, 0, self.low)
        self.begin(6)
        self.add(1, c.f, 0, self.high)
        self.begin(7)

    def back(self):
        c = self.c
        self.add(6, c.r, 1, self.low)
        self.begin(8)
        self.add(7, c.l, 1, self.high)
        self.begin(9)

    def across(self):
        c = self.c
        self.add(2, c.y, 3, self.all)
        self.add(3, c.y, 2, self.all)
        self.begin(10)

    def finish(self):
        for i in (4, 5, 8, 9, 10):
            self.message(i).wait_recv()
        total = self.total[self.c.own].astype(F32)
        for slot in (4, 5, 6):
            total += self.got[slot].astype(F32)
        return total

    def drain(self, paired=True):
        if paired:
            loop(0, NF, lambda chip: self.pairing(chip).wait_send())
        for i in range(11):
            self.message(i).wait_send()


def key_extras(rows):
    lane = lax.broadcasted_iota(jnp.int32, (rows, HD), 1)
    pos = lax.broadcasted_iota(jnp.int32, (rows, HD), 0)
    high = (pos // 256) * 256
    value = jnp.where(lane < 3, high, jnp.where(lane < 6, pos - high, 0))
    return value.astype(F32).astype(BF16)


def query_extras(slope_ref):
    return jnp.broadcast_to(slope_ref[...], (HD, 256))


def kernel_a(
    hid_ref, cot_ref, pack_ref, sml_ref, qvb_ref, slope_ref,
    nrm, cota, qkvt, qkvr, lse, mid, n2, ctxr, wq, up, dn, pj, sm,
    hid, wf, smb, wqo, dno, pjo, kr, ctxo, ctxt,
    h_s, h_r, h_h, c_s, c_r, c_h, p_s, p_r, p_h, w_s, w_r, o_s, o_r, m_s, m_r, q_s, q_r, d_s, d_r, x_s, x_r, l_s,
):
    me, core, sib, row = places()
    sem = barrier_seq_all(me)
    barrier_fsdp(sem, row)
    pl.semaphore_wait(sem, NS - 1 + NF - 1)

    chips = Chips()
    first, others = pl.ds(0, 192), pl.ds(192, PACK - 192)

    def qkv_to(k):
        return remote(pack_ref.at[first], wf.at[row, first], w_s.at[k], w_r.at[row], fsdp=lax.rem(row + k, NF))

    def rest_to(k):
        return remote(pack_ref.at[others], wf.at[row, others], o_s.at[k], o_r.at[row], fsdp=lax.rem(row + k, NF))

    def small_to(k):
        return remote(sml_ref, smb.at[me], m_s.at[k], m_r.at[me], seq=lax.rem(me + k, NS))

    loop(1, NF, lambda k: qkv_to(k).start())
    loop(1, NS, lambda k: small_to(k).start())
    hidden = Gather(chips, hid_ref, hid, h_s, h_r, h_h)
    hidden.start()
    loop(1, NF, lambda k: rest_to(k).start())
    cot_own = pltpu.make_async_copy(cot_ref, cota.at[me], l_s)
    cot_own.start()
    wf[row] = pack_ref[...]
    smb[me] = sml_ref[...]
    hid[me] = hid_ref[...]
    kr[:, HD:] = key_extras(NS * TOK)

    def qkv_from(k):
        other = lax.rem(row + k, NF)
        remote(pack_ref.at[first], wf.at[other, first], w_s.at[k], w_r.at[other], fsdp=other).wait_recv()

    def rest_from(k):
        other = lax.rem(row + k, NF)
        remote(pack_ref.at[others], wf.at[other, others], o_s.at[k], o_r.at[other], fsdp=other).wait_recv()

    loop(1, NF, qkv_from)
    for f in range(NF):
        wqo[:, f * 128 : f * 128 + 128] = wf[f, 0:192, :]

    def q_block(j):
        block = 3 * me + j
        kind, head = block // H, lax.rem(block, H)
        src = wqo.at[pl.ds(j * HD, HD), :]
        dst = wq.at[pl.ds(pl.multiple_of(kind * HD, HD), HD), :]
        return head, kind, src, dst

    for j in range(3):
        head, kind, src, dst = q_block(j)

        @pl.when(head != me)
        def _():
            remote(src, dst, q_s.at[j], q_r.at[kind], seq=head).start()

        @pl.when(head == me)
        def _():
            dst[...] = src[...]

    def down_to(k):
        other = lax.rem(me + k, NS)
        return remote(
            dno.at[other], dn.at[pl.ds(pl.multiple_of(me * HD, HD), HD), :], d_s.at[k], d_r.at[me], seq=other
        )

    def down_from(k):
        other = lax.rem(me + k, NS)
        remote(
            dno.at[me], dn.at[pl.ds(pl.multiple_of(other * HD, HD), HD), :], d_s.at[k], d_r.at[other], seq=other
        ).wait_recv()

    def small_from(k):
        other = lax.rem(me + k, NS)
        remote(sml_ref, smb.at[other], m_s.at[k], m_r.at[other], seq=other).wait_recv()

    loop(1, NS, small_from)
    for t in range(NF):
        sm[:, t * 128 : t * 128 + 128] = smb[2 * t].astype(F32) + smb[2 * t + 1].astype(F32)

    for kind in range(3):

        @pl.when((kind * H + me) // 3 != me)
        def _():
            remote(
                wqo.at[pl.ds(0, HD), :], wq.at[pl.ds(kind * HD, HD), :], q_s.at[0], q_r.at[kind], seq=sib
            ).wait_recv()

    def norm_and_project(k):
        hidden.step(k)
        m = chips.at(k)
        values = hid[pl.ds(2 * m, 2)].reshape(2 * TOK, D).astype(F32)
        normed = layer_norm(values, sm[0:1, :], sm[1:2, :]).astype(BF16)
        nrm[pl.ds(2 * m, 2)] = normed.reshape(2, TOK, D)
        block = dot(wq[...], normed, 1, 1) + qvb_ref[:, 0:1]
        qkvt[m] = block.astype(BF16)
        at = pl.ds(pl.multiple_of(m * 256, 256), 256)
        qkvr[0, at, :] = block[0:64].T.astype(BF16)
        keys = block[64:128].T.astype(BF16)
        qkvr[1, at, :] = keys
        kr[at, 0:HD] = keys
        qkvr[2, at, :] = block[128:192].T.astype(BF16)

    loop(0, NF, norm_and_project)
    loop(1, NF, rest_from)
    for f in range(NF):
        lanes = slice(f * 128, f * 128 + 128)
        pjo[:, lanes] = wf[f, 192:256, :]
        up[lanes, 0:128] = wf[f, 512:640, :]
        up[lanes, 128:256] = wf[f, 640:768, :]
        for half in range(2):
            for piece in range(2):
                at = 256 + (2 * half + piece) * 64
                dno[2 * f + half, :, piece * 128 : piece * 128 + 128] = wf[f, at : at + 64, :]
    proj = Gather(chips, pjo, pj, p_s, p_r, p_h)
    proj.start()
    loop(1, NS, lambda k: down_to(k).start())
    dn[pl.ds(pl.multiple_of(me * HD, HD), HD), :] = dno[me]
    pj[me] = pjo[...]
    cot = Gather(chips, cot_ref, cota, c_s, c_r, c_h)
    cot.start()

    extras = query_extras(slope_ref)

    def ctx_to(j):
        return remote(ctxo.at[j], ctxt.at[me], x_s.at[j], x_r.at[me], seq=j)

    between = {1: [proj.pass_x], 2: [proj.pass_y], 4: [proj.pass_f], 5: [cot.pass_x], 6: [cot.pass_y]}
    for j in range(NF):
        for relay in between.get(j, []):
            relay()
        n = (j + 1) * 256
        queries = jnp.concatenate([(qkvt[j, 0:64, :].astype(F32) * 0.125).astype(BF16), extras], axis=0)
        scores = dot(kr[0:n, :], queries)
        kpos = lax.broadcasted_iota(jnp.int32, (256, 256), 0)
        qpos = lax.broadcasted_iota(jnp.int32, (256, 256), 1)
        last = jnp.where(kpos <= qpos, scores[n - 256 :], -1e30)
        scores = last if j == 0 else jnp.concatenate([scores[: n - 256], last], axis=0)
        peak = jnp.max(scores, axis=0, keepdims=True)
        expo = jnp.exp(scores - peak)
        total = jnp.sum(expo, axis=0, keepdims=True)
        lse[j : j + 1, :] = peak + jnp.log(total)
        weights = expo.astype(BF16)
        acc = dot(qkvt[0, 128:192, :], weights[0:256])
        for i in range(1, j + 1):
            acc += dot(qkvt[i, 128:192, :], weights[i * 256 : i * 256 + 256])
        context = (acc / total).astype(BF16)
        for half in range(2):
            target = 2 * j + half
            ctxo[target] = context[:, half * 128 : half * 128 + 128]

            @pl.when(me != target)
            def _():
                ctx_to(target).start()

            @pl.when(me == target)
            def _():
                ctxt[target] = ctxo[target]

    proj.finish()

    def ctx_from(k):
        other = lax.rem(me + k, NS)
        remote(ctxo.at[other], ctxt.at[other], x_s.at[other], x_r.at[other], seq=other).wait_recv()

    loop(1, NS, ctx_from)
    context = ctxt[...].reshape(D, TOK).astype(F32).T.astype(BF16)
    ctxr[...] = context
    middle = hid_ref[...].astype(F32) + dot(context, pj[...].reshape(D, D), 1, 1) + sm[2:3, :]
    mid[...] = middle
    n2[...] = layer_norm(middle, sm[3:4, :], sm[4:5, :]).astype(BF16)

    cot.pass_f()
    loop(1, NS, down_from)
    cot.finish()
    cot_own.wait()
    hidden.drain()
    cot.drain()
    proj.drain()
    loop(1, NF, lambda k: qkv_to(k).wait_send())
    loop(1, NF, lambda k: rest_to(k).wait_send())
    loop(1, NS, lambda k: small_to(k).wait_send())
    loop(1, NS, lambda k: down_to(k).wait_send())
    for j in range(3):
        head, kind, src, dst = q_block(j)

        @pl.when(head != me)
        def _():
            remote(src, dst, q_s.at[j], q_r.at[kind], seq=head).wait_send()

    def ctx_sent(k):
        other = lax.rem(me + k, NS)
        remote(ctxo.at[other], ctxt.at[me], x_s.at[other], x_r.at[me], seq=other).wait_send()

    loop(1, NS, ctx_sent)


def vm():
    return pl.BlockSpec(memory_space=pltpu.VMEM)


def hbm():
    return pl.BlockSpec(memory_space=pl.ANY)


def sems(*counts):
    return [pltpu.SemaphoreType.DMA(n if isinstance(n, tuple) else (n,)) for n in counts]


def params(number):
    return pltpu.CompilerParams(collective_id=number, has_side_effects=True, vmem_limit_bytes=56 * MIB)


def run_a(hid, cot, pack, small, qvb, slope):
    shapes = [
        ((NS, TOK, D), BF16), ((NS, TOK, D), BF16), ((NF, 192, 256), BF16), ((3, NS * TOK, HD), BF16),
        ((NF, 256), F32), ((TOK, D), F32), ((TOK, D), BF16), ((TOK, D), BF16), ((192, D), BF16),
        ((D, HID), BF16), ((D, HID), BF16), ((NS, HD, D), BF16), ((16, D), F32),
    ]
    specs = [vm() for _ in shapes]
    specs[1] = hbm()
    return pl.pallas_call(
        kernel_a,
        out_shape=[jax.ShapeDtypeStruct(*s) for s in shapes],
        in_specs=[vm(), hbm(), vm(), vm(), vm(), vm()],
        out_specs=specs,
        scratch_shapes=[
            pltpu.VMEM((NS, TOK, D), BF16),
            pltpu.VMEM((NF, PACK, 128), BF16),
            pltpu.VMEM((NS, 16, 128), BF16),
            pltpu.VMEM((192, D), BF16),
            pltpu.VMEM((NS, HD, HID), BF16),
            pltpu.VMEM((HD, D), BF16),
            pltpu.VMEM((NS * TOK, 128), BF16),
            pltpu.VMEM((NS, HD, TOK), BF16),
            pltpu.VMEM((NS, HD, TOK), BF16),
        ]
        + sems(22, (8, 2), 8) * 3
        + sems(8, 8, 8, 8, 16, 16, 3, 3, 16, 16, 16, 16)
        + [pltpu.SemaphoreType.DMA],
        compiler_params=params(0),
        name="gather_attend",
    )(hid, cot, pack, small, qvb, slope)


def kernel_m(
    n2_ref, cot_ref, up_ref, dn_ref, ub_ref,
    gn2, dtot, gup, gdn, gub,
    xa, act, gu, g_part, g_pair, g_total, g_got, d_part, d_pair,
    n_s, n_r, n_h, g1s, g1r, g2s, g2r, d1s, d1r,
):
    chips = Chips()
    sem = pltpu.get_barrier_semaphore()
    for other in (chips.sib, chips.device(chips.r), chips.device(chips.l), chips.device(chips.y)):
        pl.semaphore_signal(sem, inc=1, device_id={"seq": other}, device_id_type=MESH)
    pl.semaphore_wait(sem, 4)
    tokens = Gather(chips, n2_ref, xa, n_s, n_r, n_h)
    tokens.start()
    xa[chips.me] = n2_ref[...]
    grads = Reduce(chips, g_part, g_pair, g_total, g_got, g1s, g1r, g2s, g2r)
    downs = Reduce(chips, d_part, d_pair, dtot, None, d1s, d1r, None, None)
    gub[...] = jnp.zeros_like(gub)

    def put(side, chip, values):
        side.part[pl.ds(2 * chip, 2)] = values.astype(BF16).reshape(2, TOK, D)
        side.pairing(chip).start()

    def step(k):
        tokens.step(k)
        m = chips.at(k)
        rows = xa[pl.ds(2 * m, 2)].reshape(2 * TOK, D)
        upper = dot(rows, up_ref[...]) + ub_ref[...]
        square = upper * upper
        bend = jnp.tanh(0.7978845608 * upper * (1.0 + 0.044715 * square))
        half = 0.5 * (1.0 + bend)
        active = (upper * half).astype(BF16)
        slope = half + 0.5 * upper * (1.0 - bend * bend) * (0.7978845608 * (1.0 + 0.134145 * square))
        cots = cot_ref[pl.ds(2 * m, 2)].reshape(2 * TOK, D)
        grad = (dot(cots, dn_ref[...]) * slope).astype(BF16)
        at = pl.ds(pl.multiple_of(m * 256, 256), 256)
        act[at, :] = active
        gu[at, :] = grad
        gub[0:1, :] += jnp.sum(grad.astype(F32), axis=0, keepdims=True)
        put(grads, m, dot(grad, up_ref[...], 1, 1))
        put(downs, m, dot(active, dn_ref[...], 1, 1))

        @pl.when(k > 0)
        def _():
            grads.merge(chips.at(k - 1))
            downs.merge(chips.at(k - 1))

    loop(0, NF, step)
    grads.merge(chips.fy)
    grads.far()
    grads.sides()
    downs.merge(chips.fy)
    gup[...] = dot(xa[...].reshape(NS * TOK, D), gu[...], 0, 0).astype(BF16)
    grads.turn()
    gdn[...] = dot(cot_ref[...].reshape(NS * TOK, D), act[...], 0, 0).astype(BF16)
    grads.back()
    grads.across()
    gn2[...] = grads.finish()
    tokens.drain()
    grads.drain()
    loop(0, NF, lambda chip: downs.pairing(chip).wait_send())


def reduce_scratch(rows):
    return [pltpu.VMEM((NF, rows, D), BF16), pltpu.VMEM((NF, rows, D), BF16), pltpu.VMEM((7, rows, D), BF16)]


def run_m(n2, cot, up, dn, ub):
    shapes = [((TOK, D), F32), ((NF, TOK, D), BF16), ((D, HID), BF16), ((D, HID), BF16), ((8, HID), F32)]
    return pl.pallas_call(
        kernel_m,
        out_shape=[jax.ShapeDtypeStruct(*s) for s in shapes],
        in_specs=[vm()] * 5,
        out_specs=[vm()] * 5,
        scratch_shapes=[
            pltpu.VMEM((NS, TOK, D), BF16),
            pltpu.VMEM((NS * TOK, HID), BF16),
            pltpu.VMEM((NS * TOK, HID), BF16),
        ]
        + [pltpu.VMEM((NS, TOK, D), BF16)]
        + reduce_scratch(TOK)
        + [pltpu.VMEM((NS, TOK, D), BF16), pltpu.VMEM((NF, TOK, D), BF16)]
        + sems(22, (8, 2), 8, 8, 8, 16, 16, 8, 8),
        compiler_params=params(1),
        name="feed_forward",
    )(n2, cot, up, dn, ub)


def kernel_b(
    gc_ref, qkvt, qkvr, lse, wq, nrm, slope_ref, dtot, gpj, gdn_ref, gup_ref,
    gn1, gqkv, gsum, dsum, psum, weights,
    dct, gjt, kr, dk, dv, part, pair, total, got, d_total, d_got, p_pair, p_total, p_got, d1, pack, wgot,
    x_s, x_r, r1s, r1r, r2s, r2r, d2s, d2r, p1s, p1r, p2s, p2r, y_s, y_r, w_s, w_r, l_s,
):
    me, core, sib, row = places()
    chips = Chips()
    local = pltpu.make_async_copy(dtot, d_total, l_s)
    local.start()
    sem = barrier_seq_all(me)
    barrier_fsdp(sem, row)
    pl.semaphore_wait(sem, NS - 1 + NF - 1)
    downs = Reduce(chips, None, None, d_total, d_got, None, None, d2s, d2r)
    projs = Reduce(chips, gpj, p_pair, p_total, p_got, p1s, p1r, p2s, p2r)

    def block(other):
        return pl.ds(pl.multiple_of(other * HD, HD), HD)

    def down_to(k):
        other = lax.rem(me + k, NS)
        return remote(gdn_ref.at[block(other), :], d1.at[me], y_s.at[k], y_r.at[me], seq=other)

    def down_from(k):
        other = lax.rem(me + k, NS)
        remote(gdn_ref.at[block(me), :], d1.at[other], y_s.at[k], y_r.at[other], seq=other).wait_recv()

    def rows_to(k):
        other = lax.rem(row + k, NF)
        return remote(pack.at[other], wgot.at[row], w_s.at[k], w_r.at[row], fsdp=other)

    def rows_from(k):
        other = lax.rem(row + k, NF)
        remote(pack.at[other], wgot.at[other], w_s.at[k], w_r.at[other], fsdp=other).wait_recv()

    def send_weights():
        loop(1, NS, down_from)
        for f in range(NF):
            lanes = slice(f * 128, f * 128 + 128)
            for half in range(2):
                for piece in range(2):
                    at = (2 * half + piece) * 64
                    pack[f, at : at + 64, :] = d1[2 * f + half, :, piece * 128 : piece * 128 + 128]
            pack[f, 256:384, :] = gup_ref[lanes, 0:128]
            pack[f, 384:512, :] = gup_ref[lanes, 128:256]
        loop(1, NF, lambda k: rows_to(k).start())
        wgot[row] = pack[row]

    def merge_projs():
        loop(0, NF, projs.merge)
        projs.far()
        projs.sides()

    def ctx_to(k):
        other = lax.rem(me + k, NS)
        return remote(gc_ref.at[other], dct.at[me], x_s.at[k], x_r.at[me], seq=other)

    def ctx_from(k):
        other = lax.rem(me + k, NS)
        remote(gc_ref.at[me], dct.at[other], x_s.at[k], x_r.at[other], seq=other).wait_recv()

    loop(1, NS, lambda k: ctx_to(k).start())
    loop(0, NF, lambda chip: projs.pairing(chip).start())
    loop(1, NS, lambda k: down_to(k).start())
    local.wait()
    downs.far()
    downs.sides()
    dct[me] = gc_ref[me]
    d1[me] = gdn_ref[block(me), :]
    kr[:, HD:] = key_extras(NS * TOK)
    kr[:, 0:HD] = qkvr[1]
    dk[...] = jnp.zeros_like(dk)
    dv[...] = jnp.zeros_like(dv)
    extras = query_extras(slope_ref)
    loop(1, NS, ctx_from)
    between = {
        2: [downs.turn], 3: [merge_projs], 4: [downs.back, send_weights], 5: [downs.across, projs.turn],
        6: [projs.back, projs.across],
    }
    for j in range(NF):
        for relay in between.get(j, []):
            relay()
        n = (j + 1) * 256
        at = slice(j * 256, n)
        queries = jnp.concatenate([(qkvt[j, 0:64, :].astype(F32) * 0.125).astype(BF16), extras], axis=0)
        scores = dot(kr[0:n, :], queries)
        probs = jnp.exp(scores - lse[j : j + 1, :])
        kpos = lax.broadcasted_iota(jnp.int32, (256, 256), 0)
        qpos = lax.broadcasted_iota(jnp.int32, (256, 256), 1)
        last = jnp.where(kpos <= qpos, probs[n - 256 :], 0.0)
        probs = last if j == 0 else jnp.concatenate([probs[: n - 256], last], axis=0)
        gctx = jnp.concatenate([dct[2 * j], dct[2 * j + 1]], axis=1)
        gprobs = dot(qkvr[2, 0:n, :], gctx)
        inner = jnp.sum(probs * gprobs, axis=0, keepdims=True)
        gscores = (probs * (gprobs - inner) * 0.125).astype(BF16)
        gq = dot(qkvt[0, 64:128, :], gscores[0:256])
        for i in range(1, j + 1):
            gq += dot(qkvt[i, 64:128, :], gscores[i * 256 : i * 256 + 256])
        gjt[j, 0:64, :] = gq.astype(BF16)
        dk[0:n, :] += dot(gscores, qkvr[0, at, :])
        dv[0:n, :] += dot(probs.astype(BF16), gctx.astype(F32).T.astype(BF16))
    for j in range(NF):
        at = slice(j * 256, j * 256 + 256)
        gjt[j, 64:128, :] = dk[at, :].T.astype(BF16)
        gjt[j, 128:192, :] = dv[at, :].T.astype(BF16)

    norms = Reduce(chips, part, pair, total, got, r1s, r1r, r2s, r2r)

    def step(k):
        m = chips.at(NF - 1 - k)
        rows = gjt[m].astype(F32).T.astype(BF16)
        part[pl.ds(2 * m, 2)] = dot(rows, wq[...]).astype(BF16).reshape(2, TOK, D)
        norms.pairing(m).start()

        @pl.when(k > 0)
        def _():
            norms.merge(chips.at(NF - k))

        @pl.when(k == 1)
        def _():
            norms.begin(0, 1)

        @pl.when(k == 3)
        def _():
            norms.begin(2)

        @pl.when(k == 5)
        def _():
            norms.begin(5)
            norms.turn()

        @pl.when(k == 6)
        def _():
            norms.begin(3)

    loop(0, NF, step)
    norms.begin(4)
    norms.merge(chips.own)
    norms.back()
    norms.across()
    acc = jnp.zeros((192, D), F32)
    sums = jnp.zeros((192, 1), F32)
    for j in range(NF):
        acc += dot(gjt[j], nrm[2 * j : 2 * j + 2].reshape(2 * TOK, D))
        sums += jnp.sum(gjt[j].astype(F32), axis=1, keepdims=True)
    gqkv[...] = acc.astype(BF16)
    gsum[...] = jnp.broadcast_to(sums, (192, 128))
    loop(1, NF, rows_from)
    summed = wgot[0].astype(F32)
    for f in range(1, NF):
        summed += wgot[f].astype(F32)
    weights[...] = summed
    dsum[...] = downs.finish()
    psum[...] = projs.finish().astype(BF16)
    gn1[...] = norms.finish()
    norms.drain()
    downs.drain(False)
    projs.drain()
    loop(1, NS, lambda k: ctx_to(k).wait_send())
    loop(1, NS, lambda k: down_to(k).wait_send())
    loop(1, NF, lambda k: rows_to(k).wait_send())


def run_b(*operands):
    shapes = [
        ((TOK, D), F32), ((192, D), BF16), ((192, 128), F32), ((TOK, D), F32), ((HD, D), BF16), ((512, 128), F32)
    ]
    return pl.pallas_call(
        kernel_b,
        out_shape=[jax.ShapeDtypeStruct(*s) for s in shapes],
        in_specs=[hbm() if i == 7 else vm() for i in range(len(operands))],
        out_specs=[vm() for _ in shapes],
        scratch_shapes=[
            pltpu.VMEM((NS, HD, TOK), BF16),
            pltpu.VMEM((NF, 192, 256), BF16),
            pltpu.VMEM((NS * TOK, 128), BF16),
            pltpu.VMEM((NS * TOK, HD), F32),
            pltpu.VMEM((NS * TOK, HD), F32),
            pltpu.VMEM((NS, TOK, D), BF16),
        ]
        + reduce_scratch(TOK)
        + [pltpu.VMEM((NF, TOK, D), BF16), pltpu.VMEM((7, TOK, D), BF16)]
        + reduce_scratch(HD)
        + [pltpu.VMEM((NS, HD, HID), BF16), pltpu.VMEM((NF, 512, 128), BF16), pltpu.VMEM((NF, 512, 128), BF16)]
        + sems(16, 16, 8, 8, 16, 16, 16, 16, 8, 8, 16, 16, 16, 16, 8, 8)
        + [pltpu.SemaphoreType.DMA],
        compiler_params=params(2),
        name="attend_back",
    )(*operands)


def kernel_c(
    gqkv, psum, token_ref, local_ref,
    out, small,
    q1, m1, pack, got, m2, sgot,
    q_s, q_r, m_s, m_r, w_s, w_r, v_s, v_r,
):
    me, core, sib, row = places()
    sem = barrier_seq_all(me)
    barrier_fsdp(sem, row)
    pl.semaphore_wait(sem, NS - 1 + NF - 1)

    def tokens(k):
        other = lax.rem(me + k, NS)
        return remote(token_ref.at[other // 2], m1.at[me], m_s.at[k], m_r.at[me], seq=other)

    def q_block(kind):
        index = kind * H + me
        holder, slot = index // 3, lax.rem(index, 3)
        src = gqkv.at[pl.ds(kind * HD, HD), :]
        dst = q1.at[pl.ds(pl.multiple_of(slot * HD, HD), HD), :]
        return holder, slot, src, dst

    for kind in range(3):
        holder, slot, src, dst = q_block(kind)

        @pl.when(holder != me)
        def _():
            remote(src, dst, q_s.at[kind], q_r.at[slot], seq=holder).start()

        @pl.when(holder == me)
        def _():
            dst[...] = src[...]

    loop(1, NS, lambda k: tokens(k).start())
    m1[me] = token_ref[me // 2]
    for f in range(NF):
        pack[f, 192:256, :] = psum[:, f * 128 : f * 128 + 128]
    for slot in range(3):

        @pl.when(lax.rem(3 * me + slot, H) != me)
        def _():
            remote(
                gqkv.at[pl.ds(0, HD), :], q1.at[pl.ds(slot * HD, HD), :], q_s.at[0], q_r.at[slot], seq=sib
            ).wait_recv()

    for f in range(NF):
        pack[f, 0:192, :] = q1[:, f * 128 : f * 128 + 128]

    def rows(k):
        other = lax.rem(row + k, NF)
        return remote(pack.at[other], got.at[row], w_s.at[k], w_r.at[row], fsdp=other)

    def vectors(k):
        other = lax.rem(row + k, NF)
        return remote(m2, sgot.at[row], v_s.at[k], v_r.at[row], fsdp=other)

    loop(1, NF, lambda k: rows(k).start())
    got[row] = pack[row]

    def receive(k):
        other = lax.rem(me + k, NS)
        remote(token_ref.at[0], m1.at[other], m_s.at[k], m_r.at[other], seq=other).wait_recv()

    loop(1, NS, receive)
    local = m1[0]
    for p in range(1, NS):
        local += m1[p]
    m2[0:8, :] = local
    m2[8:16, :] = local_ref[...]
    loop(1, NF, lambda k: vectors(k).start())
    sgot[row] = m2[...]

    def receive_rows(k):
        other = lax.rem(row + k, NF)
        remote(m2, sgot.at[other], v_s.at[k], v_r.at[other], fsdp=other).wait_recv()
        remote(pack.at[other], got.at[other], w_s.at[k], w_r.at[other], fsdp=other).wait_recv()

    loop(1, NF, receive_rows)
    total = got[0].astype(F32)
    vector = sgot[0]
    for f in range(1, NF):
        total += got[f].astype(F32)
        vector += sgot[f]
    out[...] = total
    small[...] = vector
    loop(1, NS, lambda k: tokens(k).wait_send())
    loop(1, NF, lambda k: vectors(k).wait_send())
    loop(1, NF, lambda k: rows(k).wait_send())
    for kind in range(3):
        holder, slot, src, dst = q_block(kind)

        @pl.when(holder != me)
        def _():
            remote(src, dst, q_s.at[kind], q_r.at[slot], seq=holder).wait_send()


def run_c(*operands):
    shapes = [((256, 128), F32), ((16, 128), F32)]
    return pl.pallas_call(
        kernel_c,
        out_shape=[jax.ShapeDtypeStruct(*s) for s in shapes],
        in_specs=[vm() for _ in operands],
        out_specs=[vm() for _ in shapes],
        scratch_shapes=[
            pltpu.VMEM((192, D), BF16),
            pltpu.VMEM((NS, 8, 128), F32),
            pltpu.VMEM((NF, 256, 128), BF16),
            pltpu.VMEM((NF, 256, 128), BF16),
            pltpu.VMEM((16, 128), F32),
            pltpu.VMEM((NF, 16, 128), F32),
        ]
        + sems(3, 3, 16, 16, 8, 8, 8, 8),
        compiler_params=params(3),
        name="sum_weights",
    )(*operands)


def per_device(
    hidden_in, norm1_gain, norm1_shift, qkv_weight, query_bias, value_bias, proj_weight, proj_bias,
    norm2_gain, norm2_shift, up_weight, up_bias, down_weight, down_bias, out_cotangent,
):
    hid, cot = hidden_in[0], out_cotangent[0]
    me = lax.axis_index("seq")
    even = lax.rem(me, 2) == 0
    down_t = down_weight.T.reshape(HD, 4, 128).transpose(1, 0, 2).reshape(256, 128)
    up_r = up_weight.reshape(128, 2, 128).transpose(1, 0, 2).reshape(256, 128)
    pack = jnp.concatenate([qkv_weight.T, proj_weight.T, down_t, up_r], axis=0)
    vectors = jnp.stack([norm1_gain, norm1_shift, proj_bias, norm2_gain, norm2_shift, down_bias])
    none = jnp.zeros_like(vectors)
    vectors = jnp.concatenate([jnp.where(even, vectors, none), jnp.where(even, none, vectors)], axis=1)
    small = jnp.pad(vectors, ((0, 10), (0, 0)))
    qvb = jnp.concatenate([query_bias, jnp.zeros_like(query_bias), value_bias]).astype(F32)
    qvb = jnp.broadcast_to(qvb[:, None], (192, 128))
    slope = jnp.exp2(-8.0 * (me.astype(F32) + 1.0) / H)
    first = lax.reduce_precision(slope, 8, 7)
    second = lax.reduce_precision(slope - first, 8, 7)
    third = lax.reduce_precision(slope - first - second, 8, 7)
    parts = jnp.stack([first, second, third, first, second, third])
    slopes = jnp.pad(parts, (0, HD - 6)).astype(BF16)
    slopes = jnp.broadcast_to(slopes[:, None], (HD, 256))

    (nrm, cota, qkvt, qkvr, lse, middle, n2, ctx, wq, up, dn, pj, sm) = run_a(hid, cot, pack, small, qvb, slopes)
    gn2, downs, gup, gdn, gub = run_m(n2, cota, up, dn, up_bias.astype(F32)[None])

    pull = jax.vjp(layer_norm, middle, sm[3], sm[4])[1]
    grad_mid_norm, grad_gain_two, grad_shift_two = pull(gn2)
    cot32 = cot.astype(F32)
    grad_middle = cot32 + grad_mid_norm
    branch = grad_middle.astype(BF16)
    projection = pj.reshape(D, D)
    gpj = dot(branch, ctx, 0, 0).astype(BF16)
    gctx = dot(projection, branch, 0, 1).astype(BF16).reshape(NS, HD, TOK)
    gn1, gqkv, gsum, down_sum, psum, mlp = run_b(
        gctx, qkvt, qkvr, lse, wq, nrm, slopes, downs, gpj.reshape(NS, HD, D), gdn, gup
    )
    layer_out = middle + down_sum + sm[5]
    pull = jax.vjp(layer_norm, hid.astype(F32), sm[0], sm[1])[1]
    grad_in_norm, grad_gain_one, grad_shift_one = pull(gn1)
    input_grad = grad_middle + grad_in_norm

    nothing = jnp.zeros((D,), F32)
    token = jnp.stack(
        [
            grad_gain_one, grad_shift_one, jnp.sum(branch.astype(F32), axis=0), grad_gain_two, grad_shift_two,
            jnp.sum(cot32, axis=0), nothing, nothing,
        ]
    )
    token = token.reshape(8, 8, 128).transpose(1, 0, 2)
    head = jnp.concatenate([gsum[0:64, 0], gsum[128:192, 0]])[None]
    local = jnp.concatenate([head, gub[0].reshape(2, 128), jnp.zeros((5, 128), F32)], axis=0)
    out, vecs = run_c(gqkv, psum, token, local)
    mine = jnp.where(even, vecs[:6, :64], vecs[:6, 64:])
    return (
        layer_out.astype(BF16)[None],
        input_grad.astype(BF16)[None],
        mine[0],
        mine[1],
        out[0:192].T,
        vecs[8, :64],
        vecs[8, 64:],
        out[192:256].T,
        mine[2],
        mine[3],
        mine[4],
        mlp[256:512].reshape(2, 128, 128).transpose(1, 0, 2).reshape(128, 256),
        vecs[9:11].reshape(256),
        mlp[0:256].reshape(4, HD, 128).transpose(0, 2, 1).reshape(512, HD),
        mine[5],
    )


def solution(mesh):
    act, vec, mat = P("fsdp", "seq", None), P("seq"), P("fsdp", "seq")
    return jax.shard_map(
        per_device,
        mesh=mesh,
        in_specs=(act, vec, vec, mat, vec, vec, mat, vec, vec, vec, mat, vec, mat, vec, act),
        out_specs=(act, act, vec, vec, mat, vec, vec, mat, vec, vec, vec, mat, vec, mat, vec),
        check_vma=False,
    )
```

```python
import functools

import jax
import jax.numpy as jnp
from jax import lax
from jax.experimental import pallas as pl
from jax.experimental.pallas import tpu as pltpu
from jax.sharding import PartitionSpec as P

H = 16
HD = 64
D = 1024
HID = 256
TOK = 128
NS = 16
NF = 8
PACK = 768
MESH = pl.DeviceIdType.MESH
F32 = jnp.float32
BF16 = jnp.bfloat16
MIB = 1024 * 1024


def dot(left, right, lc=1, rc=0):
    return lax.dot_general(left, right, (((lc,), (rc,)), ((), ())), preferred_element_type=F32)


def layer_norm(values, gain, shift):
    average = jnp.mean(values, axis=-1, keepdims=True)
    centered = values - average
    spread = jnp.mean(centered * centered, axis=-1, keepdims=True)
    return centered * lax.rsqrt(spread + 1e-05) * gain + shift


def norm_back(values, gain, grad):
    average = jnp.mean(values, axis=-1, keepdims=True)
    centered = values - average
    spread = jnp.mean(centered * centered, axis=-1, keepdims=True)
    inverse = lax.rsqrt(spread + 1e-05)
    normed = centered * inverse
    scaled = grad * gain
    mean = jnp.mean(scaled, axis=-1, keepdims=True)
    slant = jnp.mean(scaled * normed, axis=-1, keepdims=True)
    back = inverse * (scaled - mean - normed * slant)
    return back, jnp.sum(grad * normed, axis=0, keepdims=True), jnp.sum(grad, axis=0, keepdims=True)


def remote(src, dst, send, recv, **where):
    return pltpu.make_async_remote_copy(
        src_ref=src, dst_ref=dst, send_sem=send, recv_sem=recv, device_id=where, device_id_type=MESH
    )


def places():
    me = lax.axis_index("seq")
    core = lax.rem(me, 2)
    return me, core, me + 1 - 2 * core, lax.axis_index("fsdp")


def barrier_seq_all(me):
    sem = pltpu.get_barrier_semaphore()

    def body(k, carry):
        pl.semaphore_signal(sem, inc=1, device_id={"seq": lax.rem(me + k, NS)}, device_id_type=MESH)
        return carry

    lax.fori_loop(1, NS, body, 0)
    return sem


def barrier_fsdp(sem, row):
    def body(k, carry):
        pl.semaphore_signal(sem, inc=1, device_id={"fsdp": lax.rem(row + k, NF)}, device_id_type=MESH)
        return carry

    lax.fori_loop(1, NF, body, 0)


def loop(low, high, body):
    def step(k, carry):
        body(k)
        return carry

    lax.fori_loop(low, high, step, 0)


class Chips:
    def __init__(self):
        self.me, self.core, self.sib, self.row = places()
        self.own = self.me // 2
        step = 1 - 2 * lax.rem(self.own, 2)
        self.y = self.own + step
        self.r, self.f, self.l = (lax.rem(self.own + d, NF) for d in (2, 4, 6))
        self.ry, self.fy, self.ly = self.r + step, self.f + step, self.l + step

    def at(self, k):
        j = k // 2
        ring = lax.rem(self.own // 2 + j + (j // 2) * (5 - 2 * j), 4)
        return 2 * ring + lax.rem(self.own + k, 2)

    def device(self, chip):
        return 2 * chip + self.core


class Gather:
    def __init__(self, chips, own, out, send, recv, near):
        self.c, self.own, self.out, self.send, self.recv, self.near_sem = chips, own, out, send, recv, near
        rows = out.shape[1] // 2
        self.halves = (pl.ds(0, rows), pl.ds(rows, rows))

    def message(self, i, chip, half, to):
        c = self.c
        dst = self.out.at[c.device(chip), self.halves[half]]
        src = self.own.at[self.halves[half]] if i < 6 else dst
        return remote(src, dst, self.send.at[i], self.recv.at[chip, half], seq=c.device(to))

    def messages(self):
        c = self.c
        plan = [
            (c.own, 0, c.r), (c.own, 1, c.l), (c.own, 0, c.y), (c.own, 1, c.r), (c.own, 0, c.l), (c.own, 1, c.y),
            (c.l, 0, c.r), (c.r, 1, c.l), (c.y, 0, c.r), (c.y, 0, c.l), (c.y, 1, c.r), (c.y, 1, c.l),
            (c.f, 0, c.y), (c.f, 1, c.y),
        ]
        return [functools.partial(self.message, i, *p) for i, p in enumerate(plan)]

    def begin(self, *which):
        plan = self.messages()
        for i in which:
            plan[i]().start()

    def arrive(self, chip, half):
        self.message(6, chip, half, self.c.own).wait_recv()

    def hand(self, chip, first=False):
        block = self.c.device(chip)
        src = self.own if first else self.out.at[block]
        return remote(src, self.out.at[block], self.send.at[14 + chip], self.near_sem.at[chip], seq=self.c.sib)

    def near(self, chip):
        block = 2 * chip + 1 - self.c.core
        remote(
            self.out.at[block], self.out.at[block], self.send.at[0], self.near_sem.at[chip], seq=self.c.sib
        ).wait_recv()

    def start(self):
        self.begin(0, 1, 2, 3, 4, 5)
        self.hand(self.c.own, True).start()

    def pass_x(self):
        c = self.c
        self.arrive(c.l, 0)
        self.begin(6)
        self.arrive(c.r, 1)
        self.begin(7)

    def pass_y(self):
        c = self.c
        self.arrive(c.y, 0)
        self.begin(8, 9)
        self.arrive(c.y, 1)
        self.begin(10, 11)
        self.hand(c.y).start()

    def pass_f(self):
        c = self.c
        self.arrive(c.f, 0)
        self.begin(12)
        self.arrive(c.f, 1)
        self.begin(13)
        self.hand(c.f).start()

    def take(self, name):
        c = self.c
        chip = getattr(c, name)
        for half in {"r": (0,), "l": (1,)}.get(name, (0, 1)):
            self.arrive(chip, half)
        self.hand(chip).start()

    def step(self, k):
        @pl.when(k == 2)
        def _():
            self.take("r")

        @pl.when(k == 3)
        def _():
            self.pass_f()
            self.take("ry")

        @pl.when(k == 4)
        def _():
            self.take("l")

        @pl.when(k == 5)
        def _():
            self.take("ly")

        @pl.when(k == 7)
        def _():
            self.take("fy")

        self.near(self.c.at(k))

    def finish(self):
        for name in ("r", "ry", "l", "ly", "fy"):
            self.take(name)
        loop(0, NF, self.near)

    def drain(self):
        for message in self.messages():
            message().wait_send()
        loop(0, NF, lambda chip: self.hand(chip, True).wait_send())


class Reduce:
    def __init__(self, chips, part, pair, total, got, hop, hop_recv, send, recv):
        self.c, self.part, self.pair, self.total, self.got = chips, part, pair, total, got
        self.hop, self.hop_recv, self.send, self.recv = hop, hop_recv, send, recv
        rows = total.shape[1]
        self.low, self.high, self.all = pl.ds(0, rows // 2), pl.ds(rows // 2, rows // 2), pl.ds(0, rows)

    def pairing(self, chip):
        src = self.part.at[2 * chip + 1 - self.c.core]
        return remote(src, self.pair.at[chip], self.hop.at[chip], self.hop_recv.at[chip], seq=self.c.sib)

    def merge(self, chip):
        self.pairing(chip).wait_recv()
        both = self.part[self.c.device(chip)].astype(F32) + self.pair[chip].astype(F32)
        self.total[chip] = both.astype(BF16)

    def message(self, i):
        c = self.c
        chip, rows, slot, to = (
            (c.fy, self.low, 0, c.y), (c.fy, self.high, 0, c.y), (c.ly, self.all, 3, c.l), (c.ry, self.all, 2, c.r),
            (c.r, self.high, 4, c.r), (c.l, self.low, 5, c.l), (c.f, self.low, 1, c.r), (c.f, self.high, 1, c.l),
            (c.r, self.low, 4, c.r), (c.l, self.high, 5, c.l), (c.y, self.all, 6, c.y),
        )[i]
        return remote(
            self.total.at[chip, rows], self.got.at[slot, rows], self.send.at[i], self.recv.at[i], seq=c.device(to)
        )

    def begin(self, *which):
        for i in which:
            self.message(i).start()

    def add(self, i, chip, slot, rows):
        self.message(i).wait_recv()
        both = self.total[chip, rows].astype(F32) + self.got[slot, rows].astype(F32)
        self.total[chip, rows] = both.astype(BF16)

    def far(self):
        self.begin(0, 1)

    def sides(self):
        self.begin(2, 3, 4, 5)

    def turn(self):
        c = self.c
        self.add(0, c.f, 0, self.low)
        self.begin(6)
        self.add(1, c.f, 0, self.high)
        self.begin(7)

    def back(self):
        c = self.c
        self.add(6, c.r, 1, self.low)
        self.begin(8)
        self.add(7, c.l, 1, self.high)
        self.begin(9)

    def across(self):
        c = self.c
        self.add(2, c.y, 3, self.all)
        self.add(3, c.y, 2, self.all)
        self.begin(10)

    def finish(self):
        for i in (4, 5, 8, 9, 10):
            self.message(i).wait_recv()
        total = self.total[self.c.own].astype(F32)
        for slot in (4, 5, 6):
            total += self.got[slot].astype(F32)
        return total

    def drain(self, paired=True):
        if paired:
            loop(0, NF, lambda chip: self.pairing(chip).wait_send())
        for i in range(11):
            self.message(i).wait_send()


class Rows:
    def __init__(self, src, out, rows, send, recv):
        self.src, self.out, self.rows, self.send, self.recv = src, out, rows, send, recv
        self.row = lax.axis_index("fsdp")
        self.mate = self.row + 1 - 2 * lax.rem(self.row, 2)

    def message(self, k, second):
        if second:
            group = self.mate
            src = self.out.at[group, self.rows]
            slot = k + 3
        else:
            group = self.row
            src = self.src.at[self.rows]
            slot = k
        to = self.mate if k == 0 else lax.rem(self.row + 2 * k, NF)
        return remote(src, self.out.at[group, self.rows], self.send.at[slot], self.recv.at[group], fsdp=to)

    def wait(self, group):
        dst = self.out.at[group, self.rows]
        remote(dst, dst, self.send.at[0], self.recv.at[group], fsdp=self.mate).wait_recv()

    def start(self):
        for k in range(4):
            self.message(k, False).start()

    def pass_on(self):
        self.wait(self.mate)
        for k in range(1, 4):
            self.message(k, True).start()

    def finish(self):
        for k in range(1, 4):
            self.wait(lax.rem(self.row + 2 * k, NF))
            self.wait(lax.rem(self.mate + 2 * k, NF))

    def drain(self):
        for k in range(4):
            self.message(k, False).wait_send()
        for k in range(1, 4):
            self.message(k, True).wait_send()


class RowSums:
    def __init__(self, pack, got, part, cross, send, recv):
        self.pack, self.got, self.part, self.cross, self.send, self.recv = pack, got, part, cross, send, recv
        self.row = lax.axis_index("fsdp")
        self.high = lax.rem(self.row, 2)
        self.z = self.row // 2

    def message(self, k):
        to = lax.rem(self.row + 2 * k, NF)
        src = self.pack.at[pl.ds(2 * (to // 2), 2)]
        return remote(src, self.got.at[k], self.send.at[k], self.recv.at[k], fsdp=to)

    def last(self):
        to = self.row + 1 - 2 * self.high
        return remote(self.part.at[1], self.cross, self.send.at[0], self.recv.at[0], fsdp=to)

    def start(self):
        for k in range(1, 4):
            self.message(k).start()

    def middle(self, keep):
        for k in range(1, 4):
            self.message(k).wait_recv()

        def total(which):
            value = self.pack[2 * self.z + which].astype(F32)
            for k in range(1, 4):
                value += self.got[k, which].astype(F32)
            return value

        keep[...] = total(self.high)
        self.part[1] = total(1 - self.high).astype(BF16)
        self.last().start()

    def finish(self, keep):
        self.last().wait_recv()
        return keep[...] + self.cross[...].astype(F32)

    def drain(self):
        for k in range(1, 4):
            self.message(k).wait_send()
        self.last().wait_send()


def key_extras(rows):
    lane = lax.broadcasted_iota(jnp.int32, (rows, HD), 1)
    pos = lax.broadcasted_iota(jnp.int32, (rows, HD), 0)
    high = (pos // 256) * 256
    value = jnp.where(lane < 3, high, jnp.where(lane < 6, pos - high, 0))
    return value.astype(F32).astype(BF16)


def query_extras(me):
    row = lax.broadcasted_iota(jnp.int32, (HD, 256), 0)
    slope = jnp.exp2(jnp.full((HD, 256), 0.0, F32) + (-8.0 / H) * (me + 1).astype(F32))
    first = slope.astype(BF16).astype(F32)
    second = (slope - first).astype(BF16).astype(F32)
    third = slope - first - second
    part = lax.rem(row, 3)
    value = jnp.where(part == 0, first, jnp.where(part == 1, second, third))
    return jnp.where(row < 6, value, 0.0).astype(BF16)


def kernel_a(
    hid_ref, cot_ref, wqkv_ref, wproj_ref, wup_ref, wdown_ref, vec_ref,
    nrm, cota, qkvt, qkvr, lse, mid, n2, ctxr, wq, up, dn, pj, sm,
    hid, wf, smb, wqo, dno, pjo, kr, ctxo, ctxt, pack_ref, sml_ref,
    h_s, h_r, h_h, c_s, c_r, c_h, p_s, p_r, p_h, w_s, w_r, o_s, o_r, m_s, m_r, q_s, q_r, d_s, d_r, x_s, x_r, l_s,
):
    me, core, sib, row = places()
    sem = barrier_seq_all(me)
    barrier_fsdp(sem, row)
    vectors = vec_ref[...].astype(F32)
    pack_ref[0:192, :] = wqkv_ref[...].astype(F32).T.astype(BF16)
    pack_ref[192:256, :] = wproj_ref[...].astype(F32).T.astype(BF16)
    down_t = wdown_ref[...].astype(F32).T.astype(BF16)
    for piece in range(4):
        pack_ref[256 + piece * 64 : 320 + piece * 64, :] = down_t[:, piece * 128 : piece * 128 + 128]
    pack_ref[512:640, :] = wup_ref[:, 0:128]
    pack_ref[640:768, :] = wup_ref[:, 128:256]
    blank = jnp.zeros((16, HD), F32)
    left = jnp.concatenate([vectors, blank], axis=1)
    right = jnp.concatenate([blank, vectors], axis=1)
    sml_ref[...] = jnp.where(core == 0, left, right).astype(BF16)
    columns = vectors.T
    qvb = jnp.concatenate([columns[:, 6:7], jnp.zeros((HD, 1), F32), columns[:, 7:8]], axis=0)
    pl.semaphore_wait(sem, NS - 1 + NF - 1)
    chips = Chips()
    qkv_rows = Rows(pack_ref, wf, pl.ds(0, 192), w_s, w_r)
    other_rows = Rows(pack_ref, wf, pl.ds(192, PACK - 192), o_s, o_r)

    def small_to(k):
        return remote(sml_ref, smb.at[me], m_s.at[k], m_r.at[me], seq=lax.rem(me + k, NS))

    qkv_rows.start()
    hidden = Gather(chips, hid_ref, hid, h_s, h_r, h_h)
    hidden.start()
    loop(1, NS, lambda k: small_to(k).start())
    cot_own = pltpu.make_async_copy(cot_ref, cota.at[me], l_s)
    cot_own.start()
    wf[row] = pack_ref[...]
    smb[me] = sml_ref[...]
    hid[me] = hid_ref[...]
    kr[:, HD:] = key_extras(NS * TOK)
    qkv_rows.pass_on()
    other_rows.start()
    qkv_rows.finish()
    for f in range(NF):
        wqo[:, f * 128 : f * 128 + 128] = wf[f, 0:192, :]

    def q_block(j):
        block = 3 * me + j
        kind, head = block // H, lax.rem(block, H)
        src = wqo.at[pl.ds(j * HD, HD), :]
        dst = wq.at[pl.ds(pl.multiple_of(kind * HD, HD), HD), :]
        return head, kind, src, dst

    for j in range(3):
        head, kind, src, dst = q_block(j)

        @pl.when(head != me)
        def _():
            remote(src, dst, q_s.at[j], q_r.at[kind], seq=head).start()

        @pl.when(head == me)
        def _():
            dst[...] = src[...]

    def down_to(k):
        other = lax.rem(me + k, NS)
        return remote(
            dno.at[other], dn.at[pl.ds(pl.multiple_of(me * HD, HD), HD), :], d_s.at[k], d_r.at[me], seq=other
        )

    def down_from(k):
        other = lax.rem(me + k, NS)
        remote(
            dno.at[me], dn.at[pl.ds(pl.multiple_of(other * HD, HD), HD), :], d_s.at[k], d_r.at[other], seq=other
        ).wait_recv()

    hidden.pass_x()
    hidden.pass_y()
    other_rows.pass_on()

    def small_from(k):
        other = lax.rem(me + k, NS)
        remote(sml_ref, smb.at[other], m_s.at[k], m_r.at[other], seq=other).wait_recv()

    loop(1, NS, small_from)
    for t in range(NF):
        sm[:, t * 128 : t * 128 + 128] = smb[2 * t].astype(F32) + smb[2 * t + 1].astype(F32)

    for kind in range(3):

        @pl.when((kind * H + me) // 3 != me)
        def _():
            remote(
                wqo.at[pl.ds(0, HD), :], wq.at[pl.ds(kind * HD, HD), :], q_s.at[0], q_r.at[kind], seq=sib
            ).wait_recv()

    proj = Gather(chips, pjo, pj, p_s, p_r, p_h)
    cot = Gather(chips, cot_ref, cota, c_s, c_r, c_h)

    def send_rest():
        other_rows.finish()
        for f in range(NF):
            lanes = slice(f * 128, f * 128 + 128)
            pjo[:, lanes] = wf[f, 192:256, :]
            up[lanes, 0:128] = wf[f, 512:640, :]
            up[lanes, 128:256] = wf[f, 640:768, :]
            for half in range(2):
                for piece in range(2):
                    at = 256 + (2 * half + piece) * 64
                    dno[2 * f + half, :, piece * 128 : piece * 128 + 128] = wf[f, at : at + 64, :]
        proj.start()
        loop(1, NS, lambda k: down_to(k).start())
        dn[pl.ds(pl.multiple_of(me * HD, HD), HD), :] = dno[me]
        pj[me] = pjo[...]

    def norm_and_project(k):
        hidden.step(k)

        @pl.when(k == 4)
        def _():
            send_rest()

        @pl.when(k == 6)
        def _():
            cot.start()

        m = chips.at(k)
        values = hid[pl.ds(2 * m, 2)].reshape(2 * TOK, D).astype(F32)
        normed = layer_norm(values, sm[0:1, :], sm[1:2, :]).astype(BF16)
        nrm[pl.ds(2 * m, 2)] = normed.reshape(2, TOK, D)
        block = dot(wq[...], normed, 1, 1) + qvb
        qkvt[m] = block.astype(BF16)
        at = pl.ds(pl.multiple_of(m * 256, 256), 256)
        qkvr[0, at, :] = block[0:64].T.astype(BF16)
        keys = block[64:128].T.astype(BF16)
        qkvr[1, at, :] = keys
        kr[at, 0:HD] = keys
        qkvr[2, at, :] = block[128:192].T.astype(BF16)

    loop(0, NF, norm_and_project)
    extras = query_extras(me)

    def ctx_to(j):
        return remote(ctxo.at[j], ctxt.at[me], x_s.at[j], x_r.at[me], seq=j)

    between = {0: [proj.pass_x], 2: [proj.pass_y], 4: [proj.pass_f], 5: [cot.pass_x], 6: [cot.pass_y], 7: [proj.finish]}
    for j in range(NF):
        for relay in between.get(j, []):
            relay()
        n = (j + 1) * 256
        queries = jnp.concatenate([(qkvt[j, 0:64, :].astype(F32) * 0.125).astype(BF16), extras], axis=0)
        scores = dot(kr[0:n, :], queries)
        kpos = lax.broadcasted_iota(jnp.int32, (256, 256), 0)
        qpos = lax.broadcasted_iota(jnp.int32, (256, 256), 1)
        last = jnp.where(kpos <= qpos, scores[n - 256 :], -1e30)
        scores = last if j == 0 else jnp.concatenate([scores[: n - 256], last], axis=0)
        peak = jnp.max(scores, axis=0, keepdims=True)
        expo = jnp.exp(scores - peak)
        total = jnp.sum(expo, axis=0, keepdims=True)
        lse[j : j + 1, :] = peak + jnp.log(total)
        weights = expo.astype(BF16)
        acc = dot(qkvt[0, 128:192, :], weights[0:256])
        for i in range(1, j + 1):
            acc += dot(qkvt[i, 128:192, :], weights[i * 256 : i * 256 + 256])
        context = (acc / total).astype(BF16)
        for half in range(2):
            target = 2 * j + half
            ctxo[target] = context[:, half * 128 : half * 128 + 128]

            @pl.when(me != target)
            def _():
                ctx_to(target).start()

            @pl.when(me == target)
            def _():
                ctxt[target] = ctxo[target]

    def ctx_from(k):
        other = lax.rem(me + k, NS)
        remote(ctxo.at[other], ctxt.at[other], x_s.at[other], x_r.at[other], seq=other).wait_recv()

    loop(1, NS, ctx_from)
    context = ctxt[...].reshape(D, TOK).astype(F32).T.astype(BF16)
    ctxr[...] = context
    middle = hid_ref[...].astype(F32) + dot(context, pj[...].reshape(D, D), 1, 1) + sm[2:3, :]
    mid[...] = middle
    n2[...] = layer_norm(middle, sm[3:4, :], sm[4:5, :]).astype(BF16)

    cot.pass_f()
    loop(1, NS, down_from)
    cot.finish()
    cot_own.wait()
    hidden.drain()
    cot.drain()
    proj.drain()
    qkv_rows.drain()
    other_rows.drain()
    loop(1, NS, lambda k: small_to(k).wait_send())
    loop(1, NS, lambda k: down_to(k).wait_send())
    for j in range(3):
        head, kind, src, dst = q_block(j)

        @pl.when(head != me)
        def _():
            remote(src, dst, q_s.at[j], q_r.at[kind], seq=head).wait_send()

    def ctx_sent(k):
        other = lax.rem(me + k, NS)
        remote(ctxo.at[other], ctxt.at[me], x_s.at[other], x_r.at[me], seq=other).wait_send()

    loop(1, NS, ctx_sent)


def vm():
    return pl.BlockSpec(memory_space=pltpu.VMEM)


def hbm():
    return pl.BlockSpec(memory_space=pl.ANY)


def sems(*counts):
    return [pltpu.SemaphoreType.DMA(n if isinstance(n, tuple) else (n,)) for n in counts]


def params(number):
    return pltpu.CompilerParams(collective_id=number, has_side_effects=True, vmem_limit_bytes=56 * MIB)


def run_a(*operands):
    shapes = [
        ((NS, TOK, D), BF16), ((NS, TOK, D), BF16), ((NF, 192, 256), BF16), ((3, NS * TOK, HD), BF16),
        ((NF, 256), F32), ((TOK, D), F32), ((TOK, D), BF16), ((TOK, D), BF16), ((192, D), BF16),
        ((D, HID), BF16), ((D, HID), BF16), ((NS, HD, D), BF16), ((16, D), F32),
    ]
    specs = [vm() for _ in shapes]
    specs[1] = hbm()
    return pl.pallas_call(
        kernel_a,
        out_shape=[jax.ShapeDtypeStruct(*s) for s in shapes],
        in_specs=[hbm() if i == 1 else vm() for i in range(len(operands))],
        out_specs=specs,
        scratch_shapes=[
            pltpu.VMEM((NS, TOK, D), BF16),
            pltpu.VMEM((NF, PACK, 128), BF16),
            pltpu.VMEM((NS, 16, 128), BF16),
            pltpu.VMEM((192, D), BF16),
            pltpu.VMEM((NS, HD, HID), BF16),
            pltpu.VMEM((HD, D), BF16),
            pltpu.VMEM((NS * TOK, 128), BF16),
            pltpu.VMEM((NS, HD, TOK), BF16),
            pltpu.VMEM((NS, HD, TOK), BF16),
            pltpu.VMEM((PACK, 128), BF16),
            pltpu.VMEM((16, 128), BF16),
        ]
        + sems(22, (8, 2), 8) * 3
        + sems(8, 8, 8, 8, 16, 16, 3, 3, 16, 16, 16, 16)
        + [pltpu.SemaphoreType.DMA],
        compiler_params=params(0),
        name="gather_attend",
    )(*operands)


def kernel_m(
    n2_ref, cot_ref, up_ref, dn_ref, ub_ref, mid_ref, sm_ref, pj_ref,
    gmid, branch, gct, tok, dtot, gup, gdn, gub,
    xa, act, gu, g_part, g_pair, g_total, g_got, d_part, d_pair,
    n_s, n_r, n_h, g1s, g1r, g2s, g2r, d1s, d1r,
):
    chips = Chips()
    sem = pltpu.get_barrier_semaphore()
    for other in (chips.sib, chips.device(chips.r), chips.device(chips.l), chips.device(chips.y)):
        pl.semaphore_signal(sem, inc=1, device_id={"seq": other}, device_id_type=MESH)
    pl.semaphore_wait(sem, 4)
    tokens = Gather(chips, n2_ref, xa, n_s, n_r, n_h)
    tokens.start()
    xa[chips.me] = n2_ref[...]
    grads = Reduce(chips, g_part, g_pair, g_total, g_got, g1s, g1r, g2s, g2r)
    downs = Reduce(chips, d_part, d_pair, dtot, None, d1s, d1r, None, None)
    gub[...] = jnp.zeros_like(gub)

    def put(side, chip, values):
        side.part[pl.ds(2 * chip, 2)] = values.astype(BF16).reshape(2, TOK, D)
        side.pairing(chip).start()

    def step(k):
        @pl.when(k == 1)
        def _():
            tokens.pass_x()
            tokens.pass_y()

        tokens.step(k)
        m = chips.at(k)
        rows = xa[pl.ds(2 * m, 2)].reshape(2 * TOK, D)
        upper = dot(rows, up_ref[...]) + ub_ref[...].astype(F32)
        square = upper * upper
        bend = jnp.tanh(0.7978845608 * upper * (1.0 + 0.044715 * square))
        half = 0.5 * (1.0 + bend)
        active = (upper * half).astype(BF16)
        slope = half + 0.5 * upper * (1.0 - bend * bend) * (0.7978845608 * (1.0 + 0.134145 * square))
        cots = cot_ref[pl.ds(2 * m, 2)].reshape(2 * TOK, D)
        grad = (dot(cots, dn_ref[...]) * slope).astype(BF16)
        at = pl.ds(pl.multiple_of(m * 256, 256), 256)
        act[at, :] = active
        gu[at, :] = grad
        gub[0:1, :] += jnp.sum(grad.astype(F32), axis=0, keepdims=True)
        put(grads, m, dot(grad, up_ref[...], 1, 1))
        put(downs, m, dot(active, dn_ref[...], 1, 1))

        @pl.when(k > 0)
        def _():
            grads.merge(chips.at(k - 1))
            downs.merge(chips.at(k - 1))

    loop(0, NF, step)
    grads.merge(chips.fy)
    grads.far()
    grads.sides()
    downs.merge(chips.fy)
    gup[...] = dot(xa[...].reshape(NS * TOK, D), gu[...], 0, 0).astype(BF16)
    grads.turn()
    gdn[...] = dot(cot_ref[...].reshape(NS * TOK, D), act[...], 0, 0).astype(BF16)
    grads.back()
    grads.across()
    tok[...] = jnp.zeros_like(tok)
    cot = cot_ref[chips.me].astype(F32)
    tok[5:6, :] = jnp.sum(cot, axis=0, keepdims=True)
    back, tok[3:4, :], tok[4:5, :] = norm_back(mid_ref[...], sm_ref[3:4, :], grads.finish())
    total = cot + back
    gmid[...] = total
    low = total.astype(BF16)
    branch[...] = low
    tok[2:3, :] = jnp.sum(low.astype(F32), axis=0, keepdims=True)
    gct[...] = dot(low, pj_ref[...].reshape(D, D)).T.astype(BF16).reshape(NS, HD, TOK)
    tokens.drain()
    grads.drain()
    loop(0, NF, lambda chip: downs.pairing(chip).wait_send())


def reduce_scratch(rows):
    return [pltpu.VMEM((NF, rows, D), BF16), pltpu.VMEM((NF, rows, D), BF16), pltpu.VMEM((7, rows, D), BF16)]


def run_m(*operands):
    shapes = [
        ((TOK, D), F32), ((TOK, D), BF16), ((NS, HD, TOK), BF16), ((8, D), F32), ((NF, TOK, D), BF16),
        ((D, HID), BF16), ((D, HID), BF16), ((8, HID), F32),
    ]
    return pl.pallas_call(
        kernel_m,
        out_shape=[jax.ShapeDtypeStruct(*s) for s in shapes],
        in_specs=[vm() for _ in operands],
        out_specs=[vm() for _ in shapes],
        scratch_shapes=[
            pltpu.VMEM((NS, TOK, D), BF16),
            pltpu.VMEM((NS * TOK, HID), BF16),
            pltpu.VMEM((NS * TOK, HID), BF16),
        ]
        + [pltpu.VMEM((NS, TOK, D), BF16)]
        + reduce_scratch(TOK)
        + [pltpu.VMEM((NS, TOK, D), BF16), pltpu.VMEM((NF, TOK, D), BF16)]
        + sems(22, (8, 2), 8, 8, 8, 16, 16, 8, 8),
        compiler_params=params(1),
        name="feed_forward",
    )(*operands)


def kernel_b(
    gc_ref, qkvt, qkvr, lse, wq, nrm, branch, dtot, ctx_ref, gdn_ref, gup_ref, hid_ref, gmid, mid, sm, tok, gub,
    layer_out, input_grad, weights, small,
    dct, gjt, kr, dk, dv, part, pair, total, got, d_total, d_got, gpj, p_pair, p_total, p_got, d1,
    u_pack, u_got, u_part, u_cross, u_keep, t_pack, t_got, t_part, t_cross, t_keep, gqkv, q1, tiles, m1, m2, sgot,
    x_s, x_r, r1s, r1r, r2s, r2r, d2s, d2r, p1s, p1r, p2s, p2r, y_s, y_r, u_s, u_r, t_s, t_r, q_s, q_r, m_s, m_r,
    v_s, v_r, l_s,
):
    me, core, sib, row = places()
    chips = Chips()
    local = pltpu.make_async_copy(dtot, d_total, l_s)
    local.start()
    sem = barrier_seq_all(me)
    barrier_fsdp(sem, row)
    pl.semaphore_wait(sem, NS - 1 + NF - 1)
    downs = Reduce(chips, None, None, d_total, d_got, None, None, d2s, d2r)
    projs = Reduce(chips, gpj, p_pair, p_total, p_got, p1s, p1r, p2s, p2r)
    ups = RowSums(u_pack, u_got, u_part, u_cross, u_s, u_r)
    rest = RowSums(t_pack, t_got, t_part, t_cross, t_s, t_r)

    def block(other):
        return pl.ds(pl.multiple_of(other * HD, HD), HD)

    def down_to(k):
        other = lax.rem(me + k, NS)
        return remote(gdn_ref.at[block(other), :], d1.at[me], y_s.at[k], y_r.at[me], seq=other)

    def down_from(k):
        other = lax.rem(me + k, NS)
        remote(gdn_ref.at[block(me), :], d1.at[other], y_s.at[k], y_r.at[other], seq=other).wait_recv()

    def send_weights():
        loop(1, NS, down_from)
        for f in range(NF):
            lanes = slice(f * 128, f * 128 + 128)
            for half in range(2):
                for piece in range(2):
                    at = (2 * half + piece) * 64
                    u_pack[f, at : at + 64, :] = d1[2 * f + half, :, piece * 128 : piece * 128 + 128]
            u_pack[f, 256:384, :] = gup_ref[lanes, 0:128]
            u_pack[f, 384:512, :] = gup_ref[lanes, 128:256]
        ups.start()

    def merge_projs():
        loop(0, NF, projs.merge)
        projs.far()
        projs.sides()

    def q_block(kind):
        index = kind * H + me
        holder, slot = index // 3, lax.rem(index, 3)
        return holder, slot, gqkv.at[pl.ds(kind * HD, HD), :], q1.at[block(slot), :]

    def tokens(k):
        other = lax.rem(me + k, NS)
        return remote(tiles.at[other // 2], m1.at[me], m_s.at[k], m_r.at[me], seq=other)

    def tokens_from(k):
        other = lax.rem(me + k, NS)
        remote(tiles.at[0], m1.at[other], m_s.at[k], m_r.at[other], seq=other).wait_recv()

    def vectors(k):
        return remote(m2, sgot.at[row], v_s.at[k], v_r.at[row], fsdp=lax.rem(row + k, NF))

    def vectors_from(k):
        other = lax.rem(row + k, NF)
        remote(m2, sgot.at[other], v_s.at[k], v_r.at[other], fsdp=other).wait_recv()

    def ctx_to(k):
        other = lax.rem(me + k, NS)
        return remote(gc_ref.at[other], dct.at[me], x_s.at[k], x_r.at[me], seq=other)

    def ctx_from(k):
        other = lax.rem(me + k, NS)
        remote(gc_ref.at[me], dct.at[other], x_s.at[k], x_r.at[other], seq=other).wait_recv()

    loop(1, NS, lambda k: ctx_to(k).start())
    dct[me] = gc_ref[me]
    d1[me] = gdn_ref[block(me), :]
    kr[:, HD:] = key_extras(NS * TOK)
    kr[:, 0:HD] = qkvr[1]
    dk[...] = jnp.zeros_like(dk)
    dv[...] = jnp.zeros_like(dv)
    extras = query_extras(me)
    for f in range(NF):
        lanes = slice(f * 128, f * 128 + 128)
        columns = branch[:, lanes].astype(F32).T.astype(BF16)
        gpj[2 * f : 2 * f + 2] = dot(columns, ctx_ref[...]).astype(BF16).reshape(2, HD, D)
    loop(1, NS, ctx_from)
    local.wait()
    downs.far()
    downs.sides()
    loop(0, NF, lambda chip: projs.pairing(chip).start())
    loop(1, NS, lambda k: down_to(k).start())
    between = {5: [merge_projs], 7: [downs.turn]}
    for j in range(NF):
        for relay in between.get(j, []):
            relay()
        n = (j + 1) * 256
        at = slice(j * 256, n)
        queries = jnp.concatenate([(qkvt[j, 0:64, :].astype(F32) * 0.125).astype(BF16), extras], axis=0)
        scores = dot(kr[0:n, :], queries)
        probs = jnp.exp(scores - lse[j : j + 1, :])
        kpos = lax.broadcasted_iota(jnp.int32, (256, 256), 0)
        qpos = lax.broadcasted_iota(jnp.int32, (256, 256), 1)
        last = jnp.where(kpos <= qpos, probs[n - 256 :], 0.0)
        probs = last if j == 0 else jnp.concatenate([probs[: n - 256], last], axis=0)
        gctx = jnp.concatenate([dct[2 * j], dct[2 * j + 1]], axis=1)
        gprobs = dot(qkvr[2, 0:n, :], gctx)
        inner = jnp.sum(probs * gprobs, axis=0, keepdims=True)
        gscores = (probs * (gprobs - inner) * 0.125).astype(BF16)
        gq = dot(qkvt[0, 64:128, :], gscores[0:256])
        for i in range(1, j + 1):
            gq += dot(qkvt[i, 64:128, :], gscores[i * 256 : i * 256 + 256])
        gjt[j, 0:64, :] = gq.astype(BF16)
        dk[0:n, :] += dot(gscores, qkvr[0, at, :])
        dv[0:n, :] += dot(probs.astype(BF16), gctx.astype(F32).T.astype(BF16))
    for j in range(NF):
        at = slice(j * 256, j * 256 + 256)
        gjt[j, 64:128, :] = dk[at, :].T.astype(BF16)
        gjt[j, 128:192, :] = dv[at, :].T.astype(BF16)

    send_weights()
    acc = jnp.zeros((192, D), F32)
    sums = jnp.zeros((192, 1), F32)
    for j in range(NF):
        acc += dot(gjt[j], nrm[2 * j : 2 * j + 2].reshape(2 * TOK, D))
        sums += jnp.sum(gjt[j].astype(F32), axis=1, keepdims=True)
    gqkv[...] = acc.astype(BF16)
    m2[...] = jnp.zeros_like(m2)
    line = jnp.broadcast_to(sums, (192, 128)).T
    m2[8:9, 0:64] = line[0:1, 0:64]
    m2[8:9, 64:128] = line[0:1, 128:192]
    m2[9:10, :] = gub[0:1, 0:128]
    m2[10:11, :] = gub[0:1, 128:256]
    for kind in range(3):
        holder, slot, src, dst = q_block(kind)

        @pl.when(holder != me)
        def _():
            remote(src, dst, q_s.at[kind], q_r.at[slot], seq=holder).start()

        @pl.when(holder == me)
        def _():
            dst[...] = src[...]

    norms = Reduce(chips, part, pair, total, got, r1s, r1r, r2s, r2r)
    downs.back()
    projs.turn()
    during = {
        1: [lambda: norms.begin(0, 1)],
        2: [downs.across, projs.back],
        3: [lambda: norms.begin(2)],
        4: [projs.across],
        5: [lambda: norms.begin(5), norms.turn],
        6: [lambda: norms.begin(3)],
    }

    def step(k):
        m = chips.at(NF - 1 - k)
        rows = gjt[m].astype(F32).T.astype(BF16)
        part[pl.ds(2 * m, 2)] = dot(rows, wq[...]).astype(BF16).reshape(2, TOK, D)
        norms.pairing(m).start()

        @pl.when(k > 0)
        def _():
            norms.merge(chips.at(NF - k))

        for at, events in during.items():

            @pl.when(k == at)
            def _():
                for event in events:
                    event()

    loop(0, NF, step)
    norms.begin(4)
    norms.merge(chips.own)
    norms.back()
    ups.middle(u_keep)
    for slot in range(3):

        @pl.when(lax.rem(3 * me + slot, H) != me)
        def _():
            remote(
                gqkv.at[pl.ds(0, HD), :], q1.at[pl.ds(slot * HD, HD), :], q_s.at[0], q_r.at[slot], seq=sib
            ).wait_recv()

    proj_sum = projs.finish().astype(BF16)
    for f in range(NF):
        lanes = slice(f * 128, f * 128 + 128)
        t_pack[f, 0:192, :] = q1[:, lanes]
        t_pack[f, 192:256, :] = proj_sum[:, lanes]
    rest.start()
    norms.across()
    layer_out[...] = (mid[...] + downs.finish() + sm[5:6, :]).astype(BF16)
    back, gain, shift = norm_back(hid_ref[...].astype(F32), sm[0:1, :], norms.finish())
    input_grad[...] = (gmid[...] + back).astype(BF16)
    line = jnp.concatenate([gain, shift, tok[2:8, :]], axis=0)
    for t in range(NF):
        tiles[t] = line[:, t * 128 : t * 128 + 128]
    loop(1, NS, lambda k: tokens(k).start())
    m1[me] = tiles[me // 2]
    rest.middle(t_keep)
    weights[256:768, :] = ups.finish(u_keep)
    loop(1, NS, tokens_from)
    vector = m1[0]
    for p in range(1, NS):
        vector += m1[p]
    m2[0:8, :] = vector
    loop(1, NF, lambda k: vectors(k).start())
    sgot[row] = m2[...]
    weights[0:256, :] = rest.finish(t_keep)
    loop(1, NF, vectors_from)
    vector = sgot[0]
    for f in range(1, NF):
        vector += sgot[f]
    small[...] = vector
    norms.drain()
    downs.drain(False)
    projs.drain()
    ups.drain()
    rest.drain()
    loop(1, NS, lambda k: ctx_to(k).wait_send())
    loop(1, NS, lambda k: down_to(k).wait_send())
    loop(1, NS, lambda k: tokens(k).wait_send())
    loop(1, NF, lambda k: vectors(k).wait_send())
    for kind in range(3):
        holder, slot, src, dst = q_block(kind)

        @pl.when(holder != me)
        def _():
            remote(src, dst, q_s.at[kind], q_r.at[slot], seq=holder).wait_send()


def row_scratch(rows):
    return [
        pltpu.VMEM((NF, rows, 128), BF16),
        pltpu.VMEM((4, 2, rows, 128), BF16),
        pltpu.VMEM((2, rows, 128), BF16),
        pltpu.VMEM((rows, 128), BF16),
        pltpu.VMEM((rows, 128), F32),
    ]


def run_b(*operands):
    shapes = [((TOK, D), BF16), ((TOK, D), BF16), ((PACK, 128), F32), ((16, 128), F32)]
    return pl.pallas_call(
        kernel_b,
        out_shape=[jax.ShapeDtypeStruct(*s) for s in shapes],
        in_specs=[hbm() if i == 7 else vm() for i in range(len(operands))],
        out_specs=[vm() for _ in shapes],
        scratch_shapes=[
            pltpu.VMEM((NS, HD, TOK), BF16),
            pltpu.VMEM((NF, 192, 256), BF16),
            pltpu.VMEM((NS * TOK, 128), BF16),
            pltpu.VMEM((NS * TOK, HD), F32),
            pltpu.VMEM((NS * TOK, HD), F32),
            pltpu.VMEM((NS, TOK, D), BF16),
        ]
        + reduce_scratch(TOK)
        + [pltpu.VMEM((NF, TOK, D), BF16), pltpu.VMEM((7, TOK, D), BF16), pltpu.VMEM((NS, HD, D), BF16)]
        + reduce_scratch(HD)
        + [pltpu.VMEM((NS, HD, HID), BF16)]
        + row_scratch(512)
        + row_scratch(256)
        + [
            pltpu.VMEM((192, D), BF16),
            pltpu.VMEM((192, D), BF16),
            pltpu.VMEM((NF, 8, 128), F32),
            pltpu.VMEM((NS, 8, 128), F32),
            pltpu.VMEM((16, 128), F32),
            pltpu.VMEM((NF, 16, 128), F32),
        ]
        + sems(16, 16, 8, 8, 16, 16, 16, 16, 8, 8, 16, 16, 16, 16, 4, 4, 4, 4, 3, 3, 16, 16, 8, 8)
        + [pltpu.SemaphoreType.DMA],
        compiler_params=params(2),
        name="attend_back",
    )(*operands)


def per_device(
    hidden_in, norm1_gain, norm1_shift, qkv_weight, query_bias, value_bias, proj_weight, proj_bias,
    norm2_gain, norm2_shift, up_weight, up_bias, down_weight, down_bias, out_cotangent,
):
    hid, cot = hidden_in[0], out_cotangent[0]
    me = lax.axis_index("seq")
    nothing = jnp.zeros_like(norm1_gain)
    vectors = jnp.stack(
        [norm1_gain, norm1_shift, proj_bias, norm2_gain, norm2_shift, down_bias, query_bias, value_bias]
        + [nothing] * 8
    )
    (nrm, cota, qkvt, qkvr, lse, middle, n2, ctx, wq, up, dn, pj, sm) = run_a(
        hid, cot, qkv_weight, proj_weight, up_weight, down_weight, vectors
    )
    gmid, branch, gctx, tok, downs, gup, gdn, gub = run_m(n2, cota, up, dn, up_bias[None], middle, sm, pj)
    layer_out, input_grad, out, vecs = run_b(
        gctx, qkvt, qkvr, lse, wq, nrm, branch, downs, ctx, gdn, gup, hid, gmid, middle, sm, tok, gub
    )
    mine = jnp.where(lax.rem(me, 2) == 0, vecs[:6, :64], vecs[:6, 64:])
    return (
        layer_out[None],
        input_grad[None],
        mine[0],
        mine[1],
        out[0:192].T,
        vecs[8, :64],
        vecs[8, 64:],
        out[192:256].T,
        mine[2],
        mine[3],
        mine[4],
        out[512:768].reshape(2, 128, 128).transpose(1, 0, 2).reshape(128, 256),
        vecs[9:11].reshape(256),
        out[256:512].reshape(4, HD, 128).transpose(0, 2, 1).reshape(512, HD),
        mine[5],
    )


def solution(mesh):
    act, vec, mat = P("fsdp", "seq", None), P("seq"), P("fsdp", "seq")
    return jax.shard_map(
        per_device,
        mesh=mesh,
        in_specs=(act, vec, vec, mat, vec, vec, mat, vec, vec, vec, mat, vec, mat, vec, act),
        out_specs=(act, act, vec, vec, mat, vec, vec, mat, vec, vec, vec, mat, vec, mat, vec),
        check_vma=False,
    )
```

```python
import functools

import jax
import jax.numpy as jnp
from jax import lax
from jax.experimental import pallas as pl
from jax.experimental.pallas import tpu as pltpu
from jax.sharding import PartitionSpec as P

H = 16
HD = 64
D = 1024
HID = 256
TOK = 128
NS = 16
NF = 8
PACK = 768
MESH = pl.DeviceIdType.MESH
F32 = jnp.float32
BF16 = jnp.bfloat16
MIB = 1024 * 1024


def dot(left, right, lc=1, rc=0):
    return lax.dot_general(left, right, (((lc,), (rc,)), ((), ())), preferred_element_type=F32)


def layer_norm(values, gain, shift):
    average = jnp.mean(values, axis=-1, keepdims=True)
    centered = values - average
    spread = jnp.mean(centered * centered, axis=-1, keepdims=True)
    return centered * lax.rsqrt(spread + 1e-05) * gain + shift


def norm_back(values, gain, grad):
    average = jnp.mean(values, axis=-1, keepdims=True)
    centered = values - average
    spread = jnp.mean(centered * centered, axis=-1, keepdims=True)
    inverse = lax.rsqrt(spread + 1e-05)
    normed = centered * inverse
    scaled = grad * gain
    mean = jnp.mean(scaled, axis=-1, keepdims=True)
    slant = jnp.mean(scaled * normed, axis=-1, keepdims=True)
    back = inverse * (scaled - mean - normed * slant)
    return back, jnp.sum(grad * normed, axis=0, keepdims=True), jnp.sum(grad, axis=0, keepdims=True)


def remote(src, dst, send, recv, **where):
    return pltpu.make_async_remote_copy(
        src_ref=src, dst_ref=dst, send_sem=send, recv_sem=recv, device_id=where, device_id_type=MESH
    )


def places():
    me = lax.axis_index("seq")
    core = lax.rem(me, 2)
    return me, core, me + 1 - 2 * core, lax.axis_index("fsdp")


def barrier_seq_all(me):
    sem = pltpu.get_barrier_semaphore()

    def body(k, carry):
        pl.semaphore_signal(sem, inc=1, device_id={"seq": lax.rem(me + k, NS)}, device_id_type=MESH)
        return carry

    lax.fori_loop(1, NS, body, 0)
    return sem


def barrier_fsdp(sem, row):
    def body(k, carry):
        pl.semaphore_signal(sem, inc=1, device_id={"fsdp": lax.rem(row + k, NF)}, device_id_type=MESH)
        return carry

    lax.fori_loop(1, NF, body, 0)


def loop(low, high, body):
    def step(k, carry):
        body(k)
        return carry

    lax.fori_loop(low, high, step, 0)


class Chips:
    def __init__(self):
        self.me, self.core, self.sib, self.row = places()
        self.own = self.me // 2
        step = 1 - 2 * lax.rem(self.own, 2)
        self.y = self.own + step
        self.r, self.f, self.l = (lax.rem(self.own + d, NF) for d in (2, 4, 6))
        self.ry, self.fy, self.ly = self.r + step, self.f + step, self.l + step

    def at(self, k):
        j = k // 2
        ring = lax.rem(self.own // 2 + j + (j // 2) * (5 - 2 * j), 4)
        return 2 * ring + lax.rem(self.own + k, 2)

    def device(self, chip):
        return 2 * chip + self.core


class Gather:
    def __init__(self, chips, own, out, send, recv, near):
        self.c, self.own, self.out, self.send, self.recv, self.near_sem = chips, own, out, send, recv, near
        rows = out.shape[1] // 2
        self.halves = (pl.ds(0, rows), pl.ds(rows, rows))

    def message(self, i, chip, half, to):
        c = self.c
        dst = self.out.at[c.device(chip), self.halves[half]]
        src = self.own.at[self.halves[half]] if i < 6 else dst
        return remote(src, dst, self.send.at[i], self.recv.at[chip, half], seq=c.device(to))

    def messages(self):
        c = self.c
        plan = [
            (c.own, 0, c.r), (c.own, 1, c.l), (c.own, 0, c.y), (c.own, 1, c.r), (c.own, 0, c.l), (c.own, 1, c.y),
            (c.l, 0, c.r), (c.r, 1, c.l), (c.y, 0, c.r), (c.y, 0, c.l), (c.y, 1, c.r), (c.y, 1, c.l),
            (c.f, 0, c.y), (c.f, 1, c.y),
        ]
        return [functools.partial(self.message, i, *p) for i, p in enumerate(plan)]

    def begin(self, *which):
        plan = self.messages()
        for i in which:
            plan[i]().start()

    def arrive(self, chip, half):
        self.message(6, chip, half, self.c.own).wait_recv()

    def hand(self, chip, first=False):
        block = self.c.device(chip)
        src = self.own if first else self.out.at[block]
        return remote(src, self.out.at[block], self.send.at[14 + chip], self.near_sem.at[chip], seq=self.c.sib)

    def near(self, chip):
        block = 2 * chip + 1 - self.c.core
        remote(
            self.out.at[block], self.out.at[block], self.send.at[0], self.near_sem.at[chip], seq=self.c.sib
        ).wait_recv()

    def start(self):
        self.begin(0, 1, 2, 3, 4, 5)
        self.hand(self.c.own, True).start()

    def pass_x(self):
        c = self.c
        self.arrive(c.l, 0)
        self.begin(6)
        self.arrive(c.r, 1)
        self.begin(7)

    def pass_y(self):
        c = self.c
        self.arrive(c.y, 0)
        self.begin(8, 9)
        self.arrive(c.y, 1)
        self.begin(10, 11)
        self.hand(c.y).start()

    def pass_f(self):
        c = self.c
        self.arrive(c.f, 0)
        self.begin(12)
        self.arrive(c.f, 1)
        self.begin(13)
        self.hand(c.f).start()

    def take(self, name):
        c = self.c
        chip = getattr(c, name)
        for half in {"r": (0,), "l": (1,)}.get(name, (0, 1)):
            self.arrive(chip, half)
        self.hand(chip).start()

    def step(self, k):
        @pl.when(k == 2)
        def _():
            self.take("r")

        @pl.when(k == 3)
        def _():
            self.pass_f()
            self.take("ry")

        @pl.when(k == 4)
        def _():
            self.take("l")

        @pl.when(k == 5)
        def _():
            self.take("ly")

        @pl.when(k == 7)
        def _():
            self.take("fy")

        self.near(self.c.at(k))

    def finish(self):
        for name in ("r", "ry", "l", "ly", "fy"):
            self.take(name)
        loop(0, NF, self.near)

    def drain(self):
        for message in self.messages():
            message().wait_send()
        loop(0, NF, lambda chip: self.hand(chip, True).wait_send())


class Reduce:
    def __init__(self, chips, part, pair, total, got, hop, hop_recv, send, recv):
        self.c, self.part, self.pair, self.total, self.got = chips, part, pair, total, got
        self.hop, self.hop_recv, self.send, self.recv = hop, hop_recv, send, recv
        rows = total.shape[1]
        self.low, self.high, self.all = pl.ds(0, rows // 2), pl.ds(rows // 2, rows // 2), pl.ds(0, rows)

    def pairing(self, chip):
        src = self.part.at[2 * chip + 1 - self.c.core]
        return remote(src, self.pair.at[chip], self.hop.at[chip], self.hop_recv.at[chip], seq=self.c.sib)

    def merge(self, chip):
        self.pairing(chip).wait_recv()
        both = self.part[self.c.device(chip)].astype(F32) + self.pair[chip].astype(F32)
        self.total[chip] = both.astype(BF16)

    def message(self, i):
        c = self.c
        chip, rows, slot, to = (
            (c.fy, self.low, 0, c.y), (c.fy, self.high, 0, c.y), (c.ly, self.all, 3, c.l), (c.ry, self.all, 2, c.r),
            (c.r, self.high, 4, c.r), (c.l, self.low, 5, c.l), (c.f, self.low, 1, c.r), (c.f, self.high, 1, c.l),
            (c.r, self.low, 4, c.r), (c.l, self.high, 5, c.l), (c.y, self.all, 6, c.y),
        )[i]
        return remote(
            self.total.at[chip, rows], self.got.at[slot, rows], self.send.at[i], self.recv.at[i], seq=c.device(to)
        )

    def begin(self, *which):
        for i in which:
            self.message(i).start()

    def add(self, i, chip, slot, rows):
        self.message(i).wait_recv()
        both = self.total[chip, rows].astype(F32) + self.got[slot, rows].astype(F32)
        self.total[chip, rows] = both.astype(BF16)

    def far(self):
        self.begin(0, 1)

    def sides(self):
        self.begin(2, 3, 4, 5)

    def turn(self):
        c = self.c
        self.add(0, c.f, 0, self.low)
        self.begin(6)
        self.add(1, c.f, 0, self.high)
        self.begin(7)

    def back(self):
        c = self.c
        self.add(6, c.r, 1, self.low)
        self.begin(8)
        self.add(7, c.l, 1, self.high)
        self.begin(9)

    def across(self):
        c = self.c
        self.add(2, c.y, 3, self.all)
        self.add(3, c.y, 2, self.all)
        self.begin(10)

    def finish(self):
        for i in (4, 5, 8, 9, 10):
            self.message(i).wait_recv()
        total = self.total[self.c.own].astype(F32)
        for slot in (4, 5, 6):
            total += self.got[slot].astype(F32)
        return total

    def drain(self, paired=True):
        if paired:
            loop(0, NF, lambda chip: self.pairing(chip).wait_send())
        for i in range(11):
            self.message(i).wait_send()


class Rows:
    def __init__(self, src, out, rows, send, recv):
        self.src, self.out, self.rows, self.send, self.recv = src, out, rows, send, recv
        self.row = lax.axis_index("fsdp")
        self.mate = self.row + 1 - 2 * lax.rem(self.row, 2)

    def message(self, k, second):
        if second:
            group = self.mate
            src = self.out.at[group, self.rows]
            slot = k + 3
        else:
            group = self.row
            src = self.src.at[self.rows]
            slot = k
        to = self.mate if k == 0 else lax.rem(self.row + 2 * k, NF)
        return remote(src, self.out.at[group, self.rows], self.send.at[slot], self.recv.at[group], fsdp=to)

    def wait(self, group):
        dst = self.out.at[group, self.rows]
        remote(dst, dst, self.send.at[0], self.recv.at[group], fsdp=self.mate).wait_recv()

    def start(self):
        for k in range(4):
            self.message(k, False).start()

    def pass_on(self):
        self.wait(self.mate)
        for k in range(1, 4):
            self.message(k, True).start()

    def finish(self):
        for k in range(1, 4):
            self.wait(lax.rem(self.row + 2 * k, NF))
            self.wait(lax.rem(self.mate + 2 * k, NF))

    def drain(self):
        for k in range(4):
            self.message(k, False).wait_send()
        for k in range(1, 4):
            self.message(k, True).wait_send()


class RowSums:
    def __init__(self, pack, got, part, cross, send, recv):
        self.pack, self.got, self.part, self.cross, self.send, self.recv = pack, got, part, cross, send, recv
        self.row = lax.axis_index("fsdp")
        self.high = lax.rem(self.row, 2)
        self.z = self.row // 2

    def message(self, k):
        to = lax.rem(self.row + 2 * k, NF)
        src = self.pack.at[pl.ds(2 * (to // 2), 2)]
        return remote(src, self.got.at[k], self.send.at[k], self.recv.at[k], fsdp=to)

    def last(self):
        to = self.row + 1 - 2 * self.high
        return remote(self.part.at[1], self.cross, self.send.at[0], self.recv.at[0], fsdp=to)

    def start(self):
        for k in range(1, 4):
            self.message(k).start()

    def middle(self, keep):
        for k in range(1, 4):
            self.message(k).wait_recv()

        def total(which):
            value = self.pack[2 * self.z + which].astype(F32)
            for k in range(1, 4):
                value += self.got[k, which].astype(F32)
            return value

        keep[...] = total(self.high)
        self.part[1] = total(1 - self.high).astype(BF16)
        self.last().start()

    def finish(self, keep):
        self.last().wait_recv()
        return keep[...] + self.cross[...].astype(F32)

    def drain(self):
        for k in range(1, 4):
            self.message(k).wait_send()
        self.last().wait_send()


def key_extras(rows):
    lane = lax.broadcasted_iota(jnp.int32, (rows, HD), 1)
    pos = lax.broadcasted_iota(jnp.int32, (rows, HD), 0)
    high = (pos // 256) * 256
    value = jnp.where(lane < 3, high, jnp.where(lane < 6, pos - high, 0))
    return value.astype(F32).astype(BF16)


def query_extras(me):
    row = lax.broadcasted_iota(jnp.int32, (HD, 256), 0)
    slope = jnp.exp2(jnp.full((HD, 256), 0.0, F32) + (-8.0 / H) * (me + 1).astype(F32))
    first = slope.astype(BF16).astype(F32)
    second = (slope - first).astype(BF16).astype(F32)
    third = slope - first - second
    part = lax.rem(row, 3)
    value = jnp.where(part == 0, first, jnp.where(part == 1, second, third))
    return jnp.where(row < 6, value, 0.0).astype(BF16)


def kernel_a(
    hid_ref, cot_ref, wqkv_ref, wproj_ref, wup_ref, wdown_ref, vec_ref,
    nrm, cota, qkvt, qkvr, lse, mid, n2, ctxr, wq, up, dn, pj, sm, ub,
    hid, wf, smb, wqo, dno, pjo, kr, ctxo, ctxt, pack_ref, sml_ref, normed_all,
    h_s, h_r, h_h, c_s, c_r, c_h, p_s, p_r, p_h, w_s, w_r, o_s, o_r, m_s, m_r, q_s, q_r, d_s, d_r, x_s, x_r, n_c, l_s,
):
    me, core, sib, row = places()
    sem = barrier_seq_all(me)
    barrier_fsdp(sem, row)
    rows = vec_ref[...].astype(F32)
    vectors = jnp.concatenate([rows[0:8], jnp.zeros((8, HD), F32)], axis=0)
    for i in range(4):
        ub[0:1, i * HD : i * HD + HD] = rows[8 + i : 9 + i]
    pack_ref[0:192, :] = wqkv_ref[...]
    pack_ref[192:256, :] = wproj_ref[...]
    for piece in range(4):
        pack_ref[256 + piece * 64 : 320 + piece * 64, :] = wdown_ref[:, piece * 128 : piece * 128 + 128]
    pack_ref[512:640, :] = wup_ref[:, 0:128]
    pack_ref[640:768, :] = wup_ref[:, 128:256]
    blank = jnp.zeros((16, HD), F32)
    left = jnp.concatenate([vectors, blank], axis=1)
    right = jnp.concatenate([blank, vectors], axis=1)
    sml_ref[...] = jnp.where(core == 0, left, right).astype(BF16)
    columns = vectors.T
    qvb = jnp.concatenate([columns[:, 6:7], jnp.zeros((HD, 1), F32), columns[:, 7:8]], axis=0)
    pl.semaphore_wait(sem, NS - 1 + NF - 1)
    chips = Chips()
    qkv_rows = Rows(pack_ref, wf, pl.ds(0, 192), w_s, w_r)
    other_rows = Rows(pack_ref, wf, pl.ds(192, PACK - 192), o_s, o_r)

    def small_to(k):
        return remote(sml_ref, smb.at[me], m_s.at[k], m_r.at[me], seq=lax.rem(me + k, NS))

    qkv_rows.start()
    hidden = Gather(chips, hid_ref, hid, h_s, h_r, h_h)
    hidden.start()
    loop(1, NS, lambda k: small_to(k).start())
    cot_own = pltpu.make_async_copy(cot_ref, cota.at[me], l_s)
    cot_own.start()
    wf[row] = pack_ref[...]
    smb[me] = sml_ref[...]
    hid[me] = hid_ref[...]
    kr[:, HD:] = key_extras(NS * TOK)
    qkv_rows.pass_on()
    other_rows.start()
    qkv_rows.finish()
    for f in range(NF):
        wqo[:, f * 128 : f * 128 + 128] = wf[f, 0:192, :]

    def q_block(j):
        block = 3 * me + j
        kind, head = block // H, lax.rem(block, H)
        src = wqo.at[pl.ds(j * HD, HD), :]
        dst = wq.at[pl.ds(pl.multiple_of(kind * HD, HD), HD), :]
        return head, kind, src, dst

    for j in range(3):
        head, kind, src, dst = q_block(j)

        @pl.when(head != me)
        def _():
            remote(src, dst, q_s.at[j], q_r.at[kind], seq=head).start()

        @pl.when(head == me)
        def _():
            dst[...] = src[...]

    def down_to(k):
        other = lax.rem(me + k, NS)
        return remote(
            dno.at[other], dn.at[pl.ds(pl.multiple_of(me * HD, HD), HD), :], d_s.at[k], d_r.at[me], seq=other
        )

    def down_from(k):
        other = lax.rem(me + k, NS)
        remote(
            dno.at[me], dn.at[pl.ds(pl.multiple_of(other * HD, HD), HD), :], d_s.at[k], d_r.at[other], seq=other
        ).wait_recv()

    hidden.pass_x()
    hidden.pass_y()
    other_rows.pass_on()

    def small_from(k):
        other = lax.rem(me + k, NS)
        remote(sml_ref, smb.at[other], m_s.at[k], m_r.at[other], seq=other).wait_recv()

    loop(1, NS, small_from)
    for t in range(NF):
        sm[:, t * 128 : t * 128 + 128] = smb[2 * t].astype(F32) + smb[2 * t + 1].astype(F32)

    for kind in range(3):

        @pl.when((kind * H + me) // 3 != me)
        def _():
            remote(
                wqo.at[pl.ds(0, HD), :], wq.at[pl.ds(kind * HD, HD), :], q_s.at[0], q_r.at[kind], seq=sib
            ).wait_recv()

    proj = Gather(chips, pjo, pj, p_s, p_r, p_h)
    cot = Gather(chips, cot_ref, cota, c_s, c_r, c_h)

    def send_rest():
        other_rows.finish()
        for f in range(NF):
            lanes = slice(f * 128, f * 128 + 128)
            pjo[:, lanes] = wf[f, 192:256, :]
            up[lanes, 0:128] = wf[f, 512:640, :]
            up[lanes, 128:256] = wf[f, 640:768, :]
            for half in range(2):
                for piece in range(2):
                    at = 256 + (2 * half + piece) * 64
                    dno[2 * f + half, :, piece * 128 : piece * 128 + 128] = wf[f, at : at + 64, :]
        proj.start()
        loop(1, NS, lambda k: down_to(k).start())
        dn[pl.ds(pl.multiple_of(me * HD, HD), HD), :] = dno[me]
        pj[me] = pjo[...]

    def keep(m):
        pair = pl.ds(2 * m, 2)
        return pltpu.make_async_copy(normed_all.at[pair], nrm.at[pair], n_c.at[m])

    def norm_and_project(k):
        hidden.step(k)

        @pl.when(k == 4)
        def _():
            send_rest()

        @pl.when(k == 3)
        def _():
            cot.start()

        m = chips.at(k)
        values = hid[pl.ds(2 * m, 2)].reshape(2 * TOK, D).astype(F32)
        standard = layer_norm(values, 1.0, 0.0)
        normed = (standard * sm[0:1, :] + sm[1:2, :]).astype(BF16)
        normed_all[pl.ds(2 * m, 2)] = standard.astype(BF16).reshape(2, TOK, D)
        keep(m).start()
        block = dot(wq[...], normed, 1, 1) + qvb
        qkvt[m] = block.astype(BF16)
        at = pl.ds(pl.multiple_of(m * 256, 256), 256)
        qkvr[0, at, :] = block[0:64].T.astype(BF16)
        keys = block[64:128].T.astype(BF16)
        qkvr[1, at, :] = keys
        kr[at, 0:HD] = keys
        qkvr[2, at, :] = block[128:192].T.astype(BF16)

    loop(0, NF, norm_and_project)
    extras = query_extras(me)

    def ctx_to(j):
        return remote(ctxo.at[j], ctxt.at[me], x_s.at[j], x_r.at[me], seq=j)

    between = {0: [proj.pass_x, proj.pass_y], 4: [proj.pass_f, cot.pass_x], 5: [cot.pass_y]}
    for j in range(NF):
        for relay in between.get(j, []):
            relay()
        n = (j + 1) * 256
        queries = jnp.concatenate([(qkvt[j, 0:64, :].astype(F32) * 0.125).astype(BF16), extras], axis=0)
        scores = dot(kr[0:n, :], queries)
        kpos = lax.broadcasted_iota(jnp.int32, (256, 256), 0)
        qpos = lax.broadcasted_iota(jnp.int32, (256, 256), 1)
        last = jnp.where(kpos <= qpos, scores[n - 256 :], -1e30)
        scores = last if j == 0 else jnp.concatenate([scores[: n - 256], last], axis=0)
        peak = jnp.max(scores, axis=0, keepdims=True)
        expo = jnp.exp(scores - peak)
        total = jnp.sum(expo, axis=0, keepdims=True)
        lse[j : j + 1, :] = peak + jnp.log(total)
        weights = expo.astype(BF16)
        acc = dot(qkvt[0, 128:192, :], weights[0:256])
        for i in range(1, j + 1):
            acc += dot(qkvt[i, 128:192, :], weights[i * 256 : i * 256 + 256])
        context = (acc / total).astype(BF16)
        for half in range(2):
            target = 2 * j + half
            ctxo[target] = context[:, half * 128 : half * 128 + 128]

            @pl.when(me != target)
            def _():
                ctx_to(target).start()

            @pl.when(me == target)
            def _():
                ctxt[target] = ctxo[target]

    cot.pass_f()
    proj.finish()

    def ctx_from(k):
        other = lax.rem(me + k, NS)
        remote(ctxo.at[other], ctxt.at[other], x_s.at[other], x_r.at[other], seq=other).wait_recv()

    loop(1, NS, ctx_from)
    context = ctxt[...].reshape(D, TOK).astype(F32).T.astype(BF16)
    ctxr[...] = context
    middle = hid_ref[...].astype(F32) + dot(context, pj[...].reshape(D, D), 1, 1) + sm[2:3, :]
    mid[...] = middle
    n2[...] = layer_norm(middle, sm[3:4, :], sm[4:5, :]).astype(BF16)

    loop(1, NS, down_from)
    cot.finish()
    cot_own.wait()
    loop(0, NF, lambda m: keep(m).wait())
    hidden.drain()
    cot.drain()
    proj.drain()
    qkv_rows.drain()
    other_rows.drain()
    loop(1, NS, lambda k: small_to(k).wait_send())
    loop(1, NS, lambda k: down_to(k).wait_send())
    for j in range(3):
        head, kind, src, dst = q_block(j)

        @pl.when(head != me)
        def _():
            remote(src, dst, q_s.at[j], q_r.at[kind], seq=head).wait_send()

    def ctx_sent(k):
        other = lax.rem(me + k, NS)
        remote(ctxo.at[other], ctxt.at[me], x_s.at[other], x_r.at[me], seq=other).wait_send()

    loop(1, NS, ctx_sent)


def vm():
    return pl.BlockSpec(memory_space=pltpu.VMEM)


def hbm():
    return pl.BlockSpec(memory_space=pl.ANY)


def sems(*counts):
    return [pltpu.SemaphoreType.DMA(n if isinstance(n, tuple) else (n,)) for n in counts]


def params(number):
    return pltpu.CompilerParams(collective_id=number, has_side_effects=True, vmem_limit_bytes=56 * MIB)


def run_a(*operands):
    shapes = [
        ((NS, TOK, D), BF16), ((NS, TOK, D), BF16), ((NF, 192, 256), BF16), ((3, NS * TOK, HD), BF16),
        ((NF, 256), F32), ((TOK, D), F32), ((TOK, D), BF16), ((TOK, D), BF16), ((192, D), BF16),
        ((D, HID), BF16), ((D, HID), BF16), ((NS, HD, D), BF16), ((16, D), F32), ((8, HID), F32),
    ]
    specs = [hbm() if i < 2 else vm() for i in range(len(shapes))]
    return pl.pallas_call(
        kernel_a,
        out_shape=[jax.ShapeDtypeStruct(*s) for s in shapes],
        in_specs=[hbm() if i == 1 else vm() for i in range(len(operands))],
        out_specs=specs,
        scratch_shapes=[
            pltpu.VMEM((NS, TOK, D), BF16),
            pltpu.VMEM((NF, PACK, 128), BF16),
            pltpu.VMEM((NS, 16, 128), BF16),
            pltpu.VMEM((192, D), BF16),
            pltpu.VMEM((NS, HD, HID), BF16),
            pltpu.VMEM((HD, D), BF16),
            pltpu.VMEM((NS * TOK, 128), BF16),
            pltpu.VMEM((NS, HD, TOK), BF16),
            pltpu.VMEM((NS, HD, TOK), BF16),
            pltpu.VMEM((PACK, 128), BF16),
            pltpu.VMEM((16, 128), BF16),
            pltpu.VMEM((NS, TOK, D), BF16),
        ]
        + sems(22, (8, 2), 8) * 3
        + sems(8, 8, 8, 8, 16, 16, 3, 3, 16, 16, 16, 16, 8)
        + [pltpu.SemaphoreType.DMA],
        compiler_params=params(0),
        name="gather_attend",
    )(*operands)


def kernel_m(
    n2_ref, cot_hbm, up_ref, dn_ref, ub_ref, mid_ref, sm_ref, pj_ref,
    gmid, branch, gct, tok, dtot, gup, gdn, gub,
    xa, act, gu, g_part, g_pair, g_total, g_got, d_part, d_pair, cot_ref,
    n_s, n_r, n_h, g1s, g1r, g2s, g2r, d1s, d1r, l_s,
):
    chips = Chips()
    cots_in = pltpu.make_async_copy(cot_hbm, cot_ref, l_s)
    cots_in.start()
    sem = pltpu.get_barrier_semaphore()
    for other in (chips.sib, chips.device(chips.r), chips.device(chips.l), chips.device(chips.y)):
        pl.semaphore_signal(sem, inc=1, device_id={"seq": other}, device_id_type=MESH)
    pl.semaphore_wait(sem, 4)
    tokens = Gather(chips, n2_ref, xa, n_s, n_r, n_h)
    tokens.start()
    xa[chips.me] = n2_ref[...]
    grads = Reduce(chips, g_part, g_pair, g_total, g_got, g1s, g1r, g2s, g2r)
    downs = Reduce(chips, d_part, d_pair, dtot, None, d1s, d1r, None, None)
    gub[...] = jnp.zeros_like(gub)
    cots_in.wait()

    def put(side, chip, values):
        side.part[pl.ds(2 * chip, 2)] = values.astype(BF16).reshape(2, TOK, D)
        side.pairing(chip).start()

    def step(k):
        @pl.when(k == 1)
        def _():
            tokens.pass_x()
            tokens.pass_y()

        tokens.step(k)
        m = chips.at(k)
        rows = xa[pl.ds(2 * m, 2)].reshape(2 * TOK, D)
        upper = dot(rows, up_ref[...]) + ub_ref[0:1, :]
        square = upper * upper
        bend = jnp.tanh(0.7978845608 * upper * (1.0 + 0.044715 * square))
        half = 0.5 * (1.0 + bend)
        active = (upper * half).astype(BF16)
        slope = half + 0.5 * upper * (1.0 - bend * bend) * (0.7978845608 * (1.0 + 0.134145 * square))
        cots = cot_ref[pl.ds(2 * m, 2)].reshape(2 * TOK, D)
        grad = (dot(cots, dn_ref[...]) * slope).astype(BF16)
        at = pl.ds(pl.multiple_of(m * 256, 256), 256)
        act[at, :] = active
        gu[at, :] = grad
        gub[0:1, :] += jnp.sum(grad.astype(F32), axis=0, keepdims=True)
        put(grads, m, dot(grad, up_ref[...], 1, 1))
        put(downs, m, dot(active, dn_ref[...], 1, 1))

        @pl.when(k > 0)
        def _():
            grads.merge(chips.at(k - 1))
            downs.merge(chips.at(k - 1))

        for at, message in ((3, 4), (4, 3), (5, 5), (6, 2)):

            @pl.when(k == at)
            def _():
                grads.begin(message)

    loop(0, NF, step)
    grads.merge(chips.fy)
    grads.far()
    downs.merge(chips.fy)
    gup[...] = dot(xa[...].reshape(NS * TOK, D), gu[...], 0, 0).astype(BF16)
    grads.turn()
    gdn[...] = dot(cot_ref[...].reshape(NS * TOK, D), act[...], 0, 0).astype(BF16)
    grads.back()
    grads.across()
    tok[...] = jnp.zeros_like(tok)
    cot = cot_ref[chips.me].astype(F32)
    tok[5:6, :] = jnp.sum(cot, axis=0, keepdims=True)
    back, tok[3:4, :], tok[4:5, :] = norm_back(mid_ref[...], sm_ref[3:4, :], grads.finish())
    total = cot + back
    gmid[...] = total
    low = total.astype(BF16)
    branch[...] = low
    tok[2:3, :] = jnp.sum(low.astype(F32), axis=0, keepdims=True)
    gct[...] = dot(low, pj_ref[...].reshape(D, D)).T.astype(BF16).reshape(NS, HD, TOK)
    tokens.drain()
    grads.drain()
    loop(0, NF, lambda chip: downs.pairing(chip).wait_send())


def reduce_scratch(rows):
    return [pltpu.VMEM((NF, rows, D), BF16), pltpu.VMEM((NF, rows, D), BF16), pltpu.VMEM((7, rows, D), BF16)]


def run_m(*operands):
    shapes = [
        ((TOK, D), F32), ((TOK, D), BF16), ((NS, HD, TOK), BF16), ((8, D), F32), ((NF, TOK, D), BF16),
        ((D, HID), BF16), ((D, HID), BF16), ((8, HID), F32),
    ]
    return pl.pallas_call(
        kernel_m,
        out_shape=[jax.ShapeDtypeStruct(*s) for s in shapes],
        in_specs=[hbm() if i == 1 else vm() for i in range(len(operands))],
        out_specs=[vm() for _ in shapes],
        scratch_shapes=[
            pltpu.VMEM((NS, TOK, D), BF16),
            pltpu.VMEM((NS * TOK, HID), BF16),
            pltpu.VMEM((NS * TOK, HID), BF16),
        ]
        + [pltpu.VMEM((NS, TOK, D), BF16)]
        + reduce_scratch(TOK)
        + [pltpu.VMEM((NS, TOK, D), BF16), pltpu.VMEM((NF, TOK, D), BF16), pltpu.VMEM((NS, TOK, D), BF16)]
        + sems(22, (8, 2), 8, 8, 8, 16, 16, 8, 8)
        + [pltpu.SemaphoreType.DMA],
        compiler_params=params(1),
        name="feed_forward",
    )(*operands)


def kernel_b(
    gc_ref, qkvt, qkvr, lse, wq, nrm_hbm, branch, dtot, ctx_ref, gdn_ref, gup_ref, hid_ref, gmid, mid, sm, tok, gub,
    layer_out, input_grad, w_qkv, w_proj, w_up, w_down, small,
    dct, gjt, kr, dk, dv, part, pair, total, got, d_total, d_got, gpj, p_pair, p_total, p_got, d1,
    u_pack, u_got, u_part, u_cross, u_keep, t_pack, t_got, t_part, t_cross, t_keep, gqkv, q1, tiles, m1, m2, sgot, nrm,
    x_s, x_r, r1s, r1r, r2s, r2r, d2s, d2r, p1s, p1r, p2s, p2r, y_s, y_r, u_s, u_r, t_s, t_r, q_s, q_r, m_s, m_r,
    v_s, v_r, l_s, n_c,
):
    me, core, sib, row = places()
    chips = Chips()
    local = pltpu.make_async_copy(dtot, d_total, l_s)
    local.start()
    normed_in = pltpu.make_async_copy(nrm_hbm, nrm, n_c)
    normed_in.start()
    sem = barrier_seq_all(me)
    barrier_fsdp(sem, row)
    pl.semaphore_wait(sem, NS - 1 + NF - 1)
    downs = Reduce(chips, None, None, d_total, d_got, None, None, d2s, d2r)
    projs = Reduce(chips, gpj, p_pair, p_total, p_got, p1s, p1r, p2s, p2r)
    ups = RowSums(u_pack, u_got, u_part, u_cross, u_s, u_r)
    rest = RowSums(t_pack, t_got, t_part, t_cross, t_s, t_r)

    def block(other):
        return pl.ds(pl.multiple_of(other * HD, HD), HD)

    def down_to(k):
        other = lax.rem(me + k, NS)
        return remote(gdn_ref.at[block(other), :], d1.at[me], y_s.at[k], y_r.at[me], seq=other)

    def down_from(k):
        other = lax.rem(me + k, NS)
        remote(gdn_ref.at[block(me), :], d1.at[other], y_s.at[k], y_r.at[other], seq=other).wait_recv()

    def send_weights():
        loop(1, NS, down_from)
        for f in range(NF):
            lanes = slice(f * 128, f * 128 + 128)
            for half in range(2):
                for piece in range(2):
                    at = (2 * half + piece) * 64
                    u_pack[f, at : at + 64, :] = d1[2 * f + half, :, piece * 128 : piece * 128 + 128]
            u_pack[f, 256:384, :] = gup_ref[lanes, 0:128]
            u_pack[f, 384:512, :] = gup_ref[lanes, 128:256]
        ups.start()

    def merge_projs():
        loop(0, NF, projs.merge)
        projs.far()
        projs.sides()

    def q_block(kind):
        index = kind * H + me
        holder, slot = index // 3, lax.rem(index, 3)
        return holder, slot, gqkv.at[pl.ds(kind * HD, HD), :], q1.at[block(slot), :]

    def tokens(k):
        other = lax.rem(me + k, NS)
        return remote(tiles.at[other // 2], m1.at[me], m_s.at[k], m_r.at[me], seq=other)

    def tokens_from(k):
        other = lax.rem(me + k, NS)
        remote(tiles.at[0], m1.at[other], m_s.at[k], m_r.at[other], seq=other).wait_recv()

    def vectors(k):
        return remote(m2, sgot.at[row], v_s.at[k], v_r.at[row], fsdp=lax.rem(row + k, NF))

    def vectors_from(k):
        other = lax.rem(row + k, NF)
        remote(m2, sgot.at[other], v_s.at[k], v_r.at[other], fsdp=other).wait_recv()

    def ctx_to(k):
        other = lax.rem(me + k, NS)
        return remote(gc_ref.at[other], dct.at[me], x_s.at[k], x_r.at[me], seq=other)

    def ctx_from(k):
        other = lax.rem(me + k, NS)
        remote(gc_ref.at[me], dct.at[other], x_s.at[k], x_r.at[other], seq=other).wait_recv()

    loop(1, NS, lambda k: ctx_to(k).start())
    dct[me] = gc_ref[me]
    d1[me] = gdn_ref[block(me), :]
    kr[:, HD:] = key_extras(NS * TOK)
    kr[:, 0:HD] = qkvr[1]
    dk[...] = jnp.zeros_like(dk)
    dv[...] = jnp.zeros_like(dv)
    extras = query_extras(me)
    for f in range(NF):
        lanes = slice(f * 128, f * 128 + 128)
        columns = branch[:, lanes].astype(F32).T.astype(BF16)
        gpj[2 * f : 2 * f + 2] = dot(columns, ctx_ref[...]).astype(BF16).reshape(2, HD, D)
    loop(1, NS, lambda k: down_to(k).start())
    loop(0, NF, lambda chip: projs.pairing(chip).start())
    local.wait()
    normed_in.wait()
    loop(1, NS, ctx_from)
    downs.far()
    downs.sides()
    between = {3: [send_weights], 5: [merge_projs], 7: [downs.turn]}
    for j in range(NF):
        for relay in between.get(j, []):
            relay()
        n = (j + 1) * 256
        at = slice(j * 256, n)
        queries = jnp.concatenate([(qkvt[j, 0:64, :].astype(F32) * 0.125).astype(BF16), extras], axis=0)
        scores = dot(kr[0:n, :], queries)
        probs = jnp.exp(scores - lse[j : j + 1, :])
        kpos = lax.broadcasted_iota(jnp.int32, (256, 256), 0)
        qpos = lax.broadcasted_iota(jnp.int32, (256, 256), 1)
        last = jnp.where(kpos <= qpos, probs[n - 256 :], 0.0)
        probs = last if j == 0 else jnp.concatenate([probs[: n - 256], last], axis=0)
        gctx = jnp.concatenate([dct[2 * j], dct[2 * j + 1]], axis=1)
        gprobs = dot(qkvr[2, 0:n, :], gctx)
        inner = jnp.sum(probs * gprobs, axis=0, keepdims=True)
        gscores = (probs * (gprobs - inner) * 0.125).astype(BF16)
        gq = dot(qkvt[0, 64:128, :], gscores[0:256])
        for i in range(1, j + 1):
            gq += dot(qkvt[i, 64:128, :], gscores[i * 256 : i * 256 + 256])
        gjt[j, 0:64, :] = gq.astype(BF16)
        dk[0:n, :] += dot(gscores, qkvr[0, at, :])
        dv[0:n, :] += dot(probs.astype(BF16), gctx.astype(F32).T.astype(BF16))
    for j in range(NF):
        at = slice(j * 256, j * 256 + 256)
        gjt[j, 64:128, :] = dk[at, :].T.astype(BF16)
        gjt[j, 128:192, :] = dv[at, :].T.astype(BF16)

    acc = jnp.zeros((192, D), F32)
    sums = jnp.zeros((192, 1), F32)
    for j in range(NF):
        acc += dot(gjt[j], nrm[2 * j : 2 * j + 2].reshape(2 * TOK, D))
        sums += jnp.sum(gjt[j].astype(F32), axis=1, keepdims=True)
    gqkv[...] = (acc * sm[0:1, :] + sums * sm[1:2, :]).astype(BF16)
    head = wq[...].astype(F32)
    gain = jnp.sum(acc * head, axis=0, keepdims=True)
    shift = jnp.sum(sums * head, axis=0, keepdims=True)
    line = jnp.concatenate([gain, shift, tok[2:8, :]], axis=0)
    for t in range(NF):
        tiles[t] = line[:, t * 128 : t * 128 + 128]
    loop(1, NS, lambda k: tokens(k).start())
    m1[me] = tiles[me // 2]
    m2[...] = jnp.zeros_like(m2)
    line = jnp.broadcast_to(sums, (192, 128)).T
    m2[8:9, 0:64] = line[0:1, 0:64]
    m2[8:9, 64:128] = line[0:1, 128:192]
    m2[9:10, :] = gub[0:1, 0:128]
    m2[10:11, :] = gub[0:1, 128:256]
    for kind in range(3):
        holder, slot, src, dst = q_block(kind)

        @pl.when(holder != me)
        def _():
            remote(src, dst, q_s.at[kind], q_r.at[slot], seq=holder).start()

        @pl.when(holder == me)
        def _():
            dst[...] = src[...]

    norms = Reduce(chips, part, pair, total, got, r1s, r1r, r2s, r2r)
    downs.back()
    during = {
        1: [lambda: norms.begin(0, 1), projs.turn],
        2: [downs.across],
        3: [lambda: norms.begin(2), projs.back],
        4: [projs.across],
        5: [lambda: norms.begin(5), norms.turn],
        6: [lambda: norms.begin(3)],
    }

    def step(k):
        m = chips.at(NF - 1 - k)
        rows = gjt[m].astype(F32).T.astype(BF16)
        part[pl.ds(2 * m, 2)] = dot(rows, wq[...]).astype(BF16).reshape(2, TOK, D)
        norms.pairing(m).start()

        @pl.when(k > 0)
        def _():
            norms.merge(chips.at(NF - k))

        for at, events in during.items():

            @pl.when(k == at)
            def _():
                for event in events:
                    event()

    loop(0, NF, step)
    norms.begin(4)
    norms.merge(chips.own)
    ups.middle(u_keep)
    loop(1, NS, tokens_from)
    vector = m1[0]
    for p in range(1, NS):
        vector += m1[p]
    m2[0:8, :] = vector
    loop(1, NF, lambda k: vectors(k).start())
    sgot[row] = m2[...]
    norms.back()
    for slot in range(3):

        @pl.when(lax.rem(3 * me + slot, H) != me)
        def _():
            remote(
                gqkv.at[pl.ds(0, HD), :], q1.at[pl.ds(slot * HD, HD), :], q_s.at[0], q_r.at[slot], seq=sib
            ).wait_recv()

    proj_sum = projs.finish().astype(BF16)
    for f in range(NF):
        lanes = slice(f * 128, f * 128 + 128)
        t_pack[f, 0:192, :] = q1[:, lanes]
        t_pack[f, 192:256, :] = proj_sum[:, lanes]
    rest.start()
    norms.across()
    layer_out[...] = (mid[...] + downs.finish() + sm[5:6, :]).astype(BF16)
    rest.middle(t_keep)
    rows = ups.finish(u_keep)
    for piece in range(4):
        w_down[:, piece * 128 : piece * 128 + 128] = rows[piece * HD : piece * HD + HD]
    w_up[:, 0:128] = rows[256:384]
    w_up[:, 128:256] = rows[384:512]
    rows = rest.finish(t_keep)
    w_qkv[...] = rows[0:192]
    w_proj[...] = rows[192:256]
    loop(1, NF, vectors_from)
    vector = sgot[0]
    for f in range(1, NF):
        vector += sgot[f]
    small[...] = vector
    back, _, _ = norm_back(hid_ref[...].astype(F32), sm[0:1, :], norms.finish())
    input_grad[...] = (gmid[...] + back).astype(BF16)
    norms.drain()
    downs.drain(False)
    projs.drain()
    ups.drain()
    rest.drain()
    loop(1, NS, lambda k: ctx_to(k).wait_send())
    loop(1, NS, lambda k: down_to(k).wait_send())
    loop(1, NS, lambda k: tokens(k).wait_send())
    loop(1, NF, lambda k: vectors(k).wait_send())
    for kind in range(3):
        holder, slot, src, dst = q_block(kind)

        @pl.when(holder != me)
        def _():
            remote(src, dst, q_s.at[kind], q_r.at[slot], seq=holder).wait_send()


def row_scratch(rows):
    return [
        pltpu.VMEM((NF, rows, 128), BF16),
        pltpu.VMEM((4, 2, rows, 128), BF16),
        pltpu.VMEM((2, rows, 128), BF16),
        pltpu.VMEM((rows, 128), BF16),
        pltpu.VMEM((rows, 128), F32),
    ]


def run_b(*operands):
    shapes = [
        ((TOK, D), BF16), ((TOK, D), BF16), ((192, 128), F32), ((HD, 128), F32), ((128, HID), F32), ((HD, 512), F32),
        ((16, 128), F32),
    ]
    return pl.pallas_call(
        kernel_b,
        out_shape=[jax.ShapeDtypeStruct(*s) for s in shapes],
        in_specs=[hbm() if i in (5, 7) else vm() for i in range(len(operands))],
        out_specs=[vm() for _ in shapes],
        scratch_shapes=[
            pltpu.VMEM((NS, HD, TOK), BF16),
            pltpu.VMEM((NF, 192, 256), BF16),
            pltpu.VMEM((NS * TOK, 128), BF16),
            pltpu.VMEM((NS * TOK, HD), F32),
            pltpu.VMEM((NS * TOK, HD), F32),
            pltpu.VMEM((NS, TOK, D), BF16),
        ]
        + reduce_scratch(TOK)
        + [pltpu.VMEM((NF, TOK, D), BF16), pltpu.VMEM((7, TOK, D), BF16), pltpu.VMEM((NS, HD, D), BF16)]
        + reduce_scratch(HD)
        + [pltpu.VMEM((NS, HD, HID), BF16)]
        + row_scratch(512)
        + row_scratch(256)
        + [
            pltpu.VMEM((192, D), BF16),
            pltpu.VMEM((192, D), BF16),
            pltpu.VMEM((NF, 8, 128), F32),
            pltpu.VMEM((NS, 8, 128), F32),
            pltpu.VMEM((16, 128), F32),
            pltpu.VMEM((NF, 16, 128), F32),
            pltpu.VMEM((NS, TOK, D), BF16),
        ]
        + sems(16, 16, 8, 8, 16, 16, 16, 16, 8, 8, 16, 16, 16, 16, 4, 4, 4, 4, 3, 3, 16, 16, 8, 8)
        + [pltpu.SemaphoreType.DMA, pltpu.SemaphoreType.DMA],
        compiler_params=params(2),
        name="attend_back",
    )(*operands)


def per_device(
    hidden_in, norm1_gain, norm1_shift, qkv_weight, query_bias, value_bias, proj_weight, proj_bias,
    norm2_gain, norm2_shift, up_weight, up_bias, down_weight, down_bias, out_cotangent,
):
    hid, cot = hidden_in[0], out_cotangent[0]
    me = lax.axis_index("seq")
    vectors = [norm1_gain, norm1_shift, proj_bias, norm2_gain, norm2_shift, down_bias, query_bias, value_bias]
    vectors = jnp.concatenate([v[None] for v in vectors] + [up_bias.reshape(4, HD)], axis=0)
    (nrm, cota, qkvt, qkvr, lse, middle, n2, ctx, wq, up, dn, pj, sm, ub) = run_a(
        hid, cot, qkv_weight.T, proj_weight.T, up_weight, down_weight.T, vectors
    )
    gmid, branch, gctx, tok, downs, gup, gdn, gub = run_m(n2, cota, up, dn, ub, middle, sm, pj)
    layer_out, input_grad, w_qkv, w_proj, w_up, w_down, vecs = run_b(
        gctx, qkvt, qkvr, lse, wq, nrm, branch, downs, ctx, gdn, gup, hid, gmid, middle, sm, tok, gub
    )
    mine = jnp.where(lax.rem(me, 2) == 0, vecs[:6, :64], vecs[:6, 64:])
    return (
        layer_out[None],
        input_grad[None],
        mine[0],
        mine[1],
        w_qkv.T,
        vecs[8, :64],
        vecs[8, 64:],
        w_proj.T,
        mine[2],
        mine[3],
        mine[4],
        w_up,
        vecs[9:11].reshape(256),
        w_down.T,
        mine[5],
    )


def solution(mesh):
    act, vec, mat = P("fsdp", "seq", None), P("seq"), P("fsdp", "seq")
    return jax.shard_map(
        per_device,
        mesh=mesh,
        in_specs=(act, vec, vec, mat, vec, vec, mat, vec, vec, vec, mat, vec, mat, vec, act),
        out_specs=(act, act, vec, vec, mat, vec, vec, mat, vec, vec, vec, mat, vec, mat, vec),
        check_vma=False,
    )
```

```python
import functools

import jax
import jax.numpy as jnp
from jax import lax
from jax.experimental import pallas as pl
from jax.experimental.pallas import tpu as pltpu
from jax.sharding import PartitionSpec as P

H = 16
HD = 64
D = 1024
HID = 256
TOK = 128
NS = 16
NF = 8
PACK = 768
MESH = pl.DeviceIdType.MESH
F32 = jnp.float32
BF16 = jnp.bfloat16
MIB = 1024 * 1024


def dot(left, right, lc=1, rc=0):
    return lax.dot_general(left, right, (((lc,), (rc,)), ((), ())), preferred_element_type=F32)


def layer_norm(values, gain, shift):
    average = jnp.mean(values, axis=-1, keepdims=True)
    centered = values - average
    spread = jnp.mean(centered * centered, axis=-1, keepdims=True)
    return centered * lax.rsqrt(spread + 1e-05) * gain + shift


def norm_back(values, gain, grad):
    average = jnp.mean(values, axis=-1, keepdims=True)
    centered = values - average
    spread = jnp.mean(centered * centered, axis=-1, keepdims=True)
    inverse = lax.rsqrt(spread + 1e-05)
    normed = centered * inverse
    scaled = grad * gain
    mean = jnp.mean(scaled, axis=-1, keepdims=True)
    slant = jnp.mean(scaled * normed, axis=-1, keepdims=True)
    back = inverse * (scaled - mean - normed * slant)
    return back, jnp.sum(grad * normed, axis=0, keepdims=True), jnp.sum(grad, axis=0, keepdims=True)


def remote(src, dst, send, recv, **where):
    return pltpu.make_async_remote_copy(
        src_ref=src, dst_ref=dst, send_sem=send, recv_sem=recv, device_id=where, device_id_type=MESH
    )


def places():
    me = lax.axis_index("seq")
    core = lax.rem(me, 2)
    return me, core, me + 1 - 2 * core, lax.axis_index("fsdp")


def barrier_seq_all(me):
    sem = pltpu.get_barrier_semaphore()

    def body(k, carry):
        pl.semaphore_signal(sem, inc=1, device_id={"seq": lax.rem(me + k, NS)}, device_id_type=MESH)
        return carry

    lax.fori_loop(1, NS, body, 0)
    return sem


def barrier_fsdp(sem, row):
    def body(k, carry):
        pl.semaphore_signal(sem, inc=1, device_id={"fsdp": lax.rem(row + k, NF)}, device_id_type=MESH)
        return carry

    lax.fori_loop(1, NF, body, 0)


def loop(low, high, body):
    def step(k, carry):
        body(k)
        return carry

    lax.fori_loop(low, high, step, 0)


class Chips:
    def __init__(self):
        self.me, self.core, self.sib, self.row = places()
        self.own = self.me // 2
        step = 1 - 2 * lax.rem(self.own, 2)
        self.y = self.own + step
        self.r, self.f, self.l = (lax.rem(self.own + d, NF) for d in (2, 4, 6))
        self.ry, self.fy, self.ly = self.r + step, self.f + step, self.l + step

    def at(self, k):
        j = k // 2
        ring = lax.rem(self.own // 2 + j + (j // 2) * (5 - 2 * j), 4)
        return 2 * ring + lax.rem(self.own + k, 2)

    def device(self, chip):
        return 2 * chip + self.core


class Gather:
    def __init__(self, chips, own, out, send, recv, near):
        self.c, self.own, self.out, self.send, self.recv, self.near_sem = chips, own, out, send, recv, near
        rows = out.shape[1] // 2
        self.halves = (pl.ds(0, rows), pl.ds(rows, rows))

    def message(self, i, chip, half, to):
        c = self.c
        dst = self.out.at[c.device(chip), self.halves[half]]
        src = self.own.at[self.halves[half]] if i < 6 else dst
        return remote(src, dst, self.send.at[i], self.recv.at[chip, half], seq=c.device(to))

    def messages(self):
        c = self.c
        plan = [
            (c.own, 0, c.r), (c.own, 1, c.l), (c.own, 0, c.y), (c.own, 1, c.r), (c.own, 0, c.l), (c.own, 1, c.y),
            (c.l, 0, c.r), (c.r, 1, c.l), (c.y, 0, c.r), (c.y, 0, c.l), (c.y, 1, c.r), (c.y, 1, c.l),
            (c.f, 0, c.y), (c.f, 1, c.y),
        ]
        return [functools.partial(self.message, i, *p) for i, p in enumerate(plan)]

    def begin(self, *which):
        plan = self.messages()
        for i in which:
            plan[i]().start()

    def arrive(self, chip, half):
        self.message(6, chip, half, self.c.own).wait_recv()

    def hand(self, chip, first=False):
        block = self.c.device(chip)
        src = self.own if first else self.out.at[block]
        return remote(src, self.out.at[block], self.send.at[14 + chip], self.near_sem.at[chip], seq=self.c.sib)

    def near(self, chip):
        block = 2 * chip + 1 - self.c.core
        remote(
            self.out.at[block], self.out.at[block], self.send.at[0], self.near_sem.at[chip], seq=self.c.sib
        ).wait_recv()

    def start(self):
        self.begin(0, 1, 2, 3, 4, 5)
        self.hand(self.c.own, True).start()

    def pass_x(self):
        c = self.c
        self.arrive(c.l, 0)
        self.begin(6)
        self.arrive(c.r, 1)
        self.begin(7)

    def pass_y(self):
        c = self.c
        self.arrive(c.y, 0)
        self.begin(8, 9)
        self.arrive(c.y, 1)
        self.begin(10, 11)
        self.hand(c.y).start()

    def pass_f(self):
        c = self.c
        self.arrive(c.f, 0)
        self.begin(12)
        self.arrive(c.f, 1)
        self.begin(13)
        self.hand(c.f).start()

    def take(self, name):
        c = self.c
        chip = getattr(c, name)
        for half in {"r": (0,), "l": (1,)}.get(name, (0, 1)):
            self.arrive(chip, half)
        self.hand(chip).start()

    def step(self, k):
        @pl.when(k == 2)
        def _():
            self.take("r")

        @pl.when(k == 3)
        def _():
            self.pass_f()
            self.take("ry")

        @pl.when(k == 4)
        def _():
            self.take("l")

        @pl.when(k == 5)
        def _():
            self.take("ly")

        @pl.when(k == 7)
        def _():
            self.take("fy")

        self.near(self.c.at(k))

    def finish(self):
        for name in ("r", "ry", "l", "ly", "fy"):
            self.take(name)
        loop(0, NF, self.near)

    def drain(self):
        for message in self.messages():
            message().wait_send()
        loop(0, NF, lambda chip: self.hand(chip, True).wait_send())


class Reduce:
    def __init__(self, chips, part, pair, total, got, hop, hop_recv, send, recv):
        self.c, self.part, self.pair, self.total, self.got = chips, part, pair, total, got
        self.hop, self.hop_recv, self.send, self.recv = hop, hop_recv, send, recv
        rows = total.shape[1]
        self.low, self.high, self.all = pl.ds(0, rows // 2), pl.ds(rows // 2, rows // 2), pl.ds(0, rows)

    def pairing(self, chip):
        src = self.part.at[2 * chip + 1 - self.c.core]
        return remote(src, self.pair.at[chip], self.hop.at[chip], self.hop_recv.at[chip], seq=self.c.sib)

    def merge(self, chip):
        self.pairing(chip).wait_recv()
        both = self.part[self.c.device(chip)].astype(F32) + self.pair[chip].astype(F32)
        self.total[chip] = both.astype(BF16)

    def message(self, i):
        c = self.c
        chip, rows, slot, to = (
            (c.fy, self.low, 0, c.y), (c.fy, self.high, 0, c.y), (c.ly, self.all, 3, c.l), (c.ry, self.all, 2, c.r),
            (c.r, self.high, 4, c.r), (c.l, self.low, 5, c.l), (c.f, self.low, 1, c.r), (c.f, self.high, 1, c.l),
            (c.r, self.low, 4, c.r), (c.l, self.high, 5, c.l), (c.y, self.all, 6, c.y),
        )[i]
        return remote(
            self.total.at[chip, rows], self.got.at[slot, rows], self.send.at[i], self.recv.at[i], seq=c.device(to)
        )

    def begin(self, *which):
        for i in which:
            self.message(i).start()

    def add(self, i, chip, slot, rows):
        self.message(i).wait_recv()
        both = self.total[chip, rows].astype(F32) + self.got[slot, rows].astype(F32)
        self.total[chip, rows] = both.astype(BF16)

    def far(self):
        self.begin(0, 1)

    def sides(self):
        self.begin(2, 3, 4, 5)

    def turn(self):
        c = self.c
        self.add(0, c.f, 0, self.low)
        self.begin(6)
        self.add(1, c.f, 0, self.high)
        self.begin(7)

    def back(self):
        c = self.c
        self.add(6, c.r, 1, self.low)
        self.begin(8)
        self.add(7, c.l, 1, self.high)
        self.begin(9)

    def across(self):
        c = self.c
        self.add(2, c.y, 3, self.all)
        self.add(3, c.y, 2, self.all)
        self.begin(10)

    def finish(self):
        for i in (4, 5, 8, 9, 10):
            self.message(i).wait_recv()
        total = self.total[self.c.own].astype(F32)
        for slot in (4, 5, 6):
            total += self.got[slot].astype(F32)
        return total

    def drain(self, paired=True):
        if paired:
            loop(0, NF, lambda chip: self.pairing(chip).wait_send())
        for i in range(11):
            self.message(i).wait_send()


class Rows:
    def __init__(self, src, out, rows, send, recv):
        self.src, self.out, self.rows, self.send, self.recv = src, out, rows, send, recv
        self.row = lax.axis_index("fsdp")
        self.mate = self.row + 1 - 2 * lax.rem(self.row, 2)

    def message(self, k, second):
        if second:
            group = self.mate
            src = self.out.at[group, self.rows]
            slot = k + 3
        else:
            group = self.row
            src = self.src.at[self.rows]
            slot = k
        to = self.mate if k == 0 else lax.rem(self.row + 2 * k, NF)
        return remote(src, self.out.at[group, self.rows], self.send.at[slot], self.recv.at[group], fsdp=to)

    def wait(self, group):
        dst = self.out.at[group, self.rows]
        remote(dst, dst, self.send.at[0], self.recv.at[group], fsdp=self.mate).wait_recv()

    def start(self):
        for k in range(4):
            self.message(k, False).start()

    def pass_on(self):
        self.wait(self.mate)
        for k in range(1, 4):
            self.message(k, True).start()

    def finish(self):
        for k in range(1, 4):
            self.wait(lax.rem(self.row + 2 * k, NF))
            self.wait(lax.rem(self.mate + 2 * k, NF))

    def drain(self):
        for k in range(4):
            self.message(k, False).wait_send()
        for k in range(1, 4):
            self.message(k, True).wait_send()


class RowSums:
    def __init__(self, pack, got, part, cross, send, recv):
        self.pack, self.got, self.part, self.cross, self.send, self.recv = pack, got, part, cross, send, recv
        self.row = lax.axis_index("fsdp")
        self.high = lax.rem(self.row, 2)
        self.z = self.row // 2

    def message(self, k):
        to = lax.rem(self.row + 2 * k, NF)
        src = self.pack.at[pl.ds(2 * (to // 2), 2)]
        return remote(src, self.got.at[k], self.send.at[k], self.recv.at[k], fsdp=to)

    def last(self):
        to = self.row + 1 - 2 * self.high
        return remote(self.part.at[1], self.cross, self.send.at[0], self.recv.at[0], fsdp=to)

    def start(self):
        for k in range(1, 4):
            self.message(k).start()

    def middle(self, keep):
        for k in range(1, 4):
            self.message(k).wait_recv()

        def total(which):
            value = self.pack[2 * self.z + which].astype(F32)
            for k in range(1, 4):
                value += self.got[k, which].astype(F32)
            return value

        keep[...] = total(self.high)
        self.part[1] = total(1 - self.high).astype(BF16)
        self.last().start()

    def finish(self, keep):
        self.last().wait_recv()
        return keep[...] + self.cross[...].astype(F32)

    def drain(self):
        for k in range(1, 4):
            self.message(k).wait_send()
        self.last().wait_send()


def key_extras(rows):
    lane = lax.broadcasted_iota(jnp.int32, (rows, HD), 1)
    pos = lax.broadcasted_iota(jnp.int32, (rows, HD), 0)
    high = (pos // 256) * 256
    value = jnp.where(lane < 3, high, jnp.where(lane < 6, pos - high, 0))
    return value.astype(F32).astype(BF16)


def query_extras(me):
    row = lax.broadcasted_iota(jnp.int32, (HD, 256), 0)
    slope = jnp.exp2(jnp.full((HD, 256), 0.0, F32) + (-8.0 / H) * (me + 1).astype(F32))
    first = slope.astype(BF16).astype(F32)
    second = (slope - first).astype(BF16).astype(F32)
    third = slope - first - second
    part = lax.rem(row, 3)
    value = jnp.where(part == 0, first, jnp.where(part == 1, second, third))
    return jnp.where(row < 6, value, 0.0).astype(BF16)


def kernel_a(
    hid_ref, cot_ref, wqkv_ref, wproj_ref, wup_ref, wdown_ref, vec_ref,
    nrm, qkvt, qkvr, lse, mid, ctxr, wq, sm, gmid, branch, gct, tok, dtot, gup, gdn, gub,
    hid, wf, smb, wqo, dno, pjo, kr, ctxo, ctxt, pack_ref, sml_ref, normed_all, cota, n2, up, dn, pj, ub,
    xa, act, gu, g_part, g_pair, g_total, g_got, d_part, d_pair,
    h_s, h_r, h_h, c_s, c_r, c_h, p_s, p_r, p_h, n_s, n_r, n_h,
    w_s, w_r, o_s, o_r, m_s, m_r, q_s, q_r, d_s, d_r, x_s, x_r, n_c,
    g1s, g1r, g2s, g2r, d1s, d1r,
):
    me, core, sib, row = places()
    sem = barrier_seq_all(me)
    barrier_fsdp(sem, row)
    rows = vec_ref[...].astype(F32)
    vectors = jnp.concatenate([rows[0:8], jnp.zeros((8, HD), F32)], axis=0)
    for i in range(4):
        ub[0:1, i * HD : i * HD + HD] = rows[8 + i : 9 + i]
    pack_ref[0:192, :] = wqkv_ref[...]
    pack_ref[192:256, :] = wproj_ref[...]
    for piece in range(4):
        pack_ref[256 + piece * 64 : 320 + piece * 64, :] = wdown_ref[:, piece * 128 : piece * 128 + 128]
    pack_ref[512:640, :] = wup_ref[:, 0:128]
    pack_ref[640:768, :] = wup_ref[:, 128:256]
    blank = jnp.zeros((16, HD), F32)
    left = jnp.concatenate([vectors, blank], axis=1)
    right = jnp.concatenate([blank, vectors], axis=1)
    sml_ref[...] = jnp.where(core == 0, left, right).astype(BF16)
    columns = vectors.T
    qvb = jnp.concatenate([columns[:, 6:7], jnp.zeros((HD, 1), F32), columns[:, 7:8]], axis=0)
    pl.semaphore_wait(sem, NS - 1 + NF - 1)
    chips = Chips()
    qkv_rows = Rows(pack_ref, wf, pl.ds(0, 192), w_s, w_r)
    other_rows = Rows(pack_ref, wf, pl.ds(192, PACK - 192), o_s, o_r)

    def small_to(k):
        return remote(sml_ref, smb.at[me], m_s.at[k], m_r.at[me], seq=lax.rem(me + k, NS))

    qkv_rows.start()
    hidden = Gather(chips, hid_ref, hid, h_s, h_r, h_h)
    hidden.start()
    loop(1, NS, lambda k: small_to(k).start())
    wf[row] = pack_ref[...]
    smb[me] = sml_ref[...]
    hid[me] = hid_ref[...]
    cota[me] = cot_ref[...]
    kr[:, HD:] = key_extras(NS * TOK)
    qkv_rows.pass_on()
    other_rows.start()
    qkv_rows.finish()
    for f in range(NF):
        wqo[:, f * 128 : f * 128 + 128] = wf[f, 0:192, :]

    def q_block(j):
        block = 3 * me + j
        kind, head = block // H, lax.rem(block, H)
        src = wqo.at[pl.ds(j * HD, HD), :]
        dst = wq.at[pl.ds(pl.multiple_of(kind * HD, HD), HD), :]
        return head, kind, src, dst

    for j in range(3):
        head, kind, src, dst = q_block(j)

        @pl.when(head != me)
        def _():
            remote(src, dst, q_s.at[j], q_r.at[kind], seq=head).start()

        @pl.when(head == me)
        def _():
            dst[...] = src[...]

    def down_to(k):
        other = lax.rem(me + k, NS)
        return remote(
            dno.at[other], dn.at[pl.ds(pl.multiple_of(me * HD, HD), HD), :], d_s.at[k], d_r.at[me], seq=other
        )

    def down_from(k):
        other = lax.rem(me + k, NS)
        remote(
            dno.at[me], dn.at[pl.ds(pl.multiple_of(other * HD, HD), HD), :], d_s.at[k], d_r.at[other], seq=other
        ).wait_recv()

    hidden.pass_x()
    hidden.pass_y()
    other_rows.pass_on()

    def small_from(k):
        other = lax.rem(me + k, NS)
        remote(sml_ref, smb.at[other], m_s.at[k], m_r.at[other], seq=other).wait_recv()

    loop(1, NS, small_from)
    for t in range(NF):
        sm[:, t * 128 : t * 128 + 128] = smb[2 * t].astype(F32) + smb[2 * t + 1].astype(F32)

    for kind in range(3):

        @pl.when((kind * H + me) // 3 != me)
        def _():
            remote(
                wqo.at[pl.ds(0, HD), :], wq.at[pl.ds(kind * HD, HD), :], q_s.at[0], q_r.at[kind], seq=sib
            ).wait_recv()

    proj = Gather(chips, pjo, pj, p_s, p_r, p_h)
    cot = Gather(chips, cot_ref, cota, c_s, c_r, c_h)

    def send_rest():
        other_rows.finish()
        for f in range(NF):
            lanes = slice(f * 128, f * 128 + 128)
            pjo[:, lanes] = wf[f, 192:256, :]
            up[lanes, 0:128] = wf[f, 512:640, :]
            up[lanes, 128:256] = wf[f, 640:768, :]
            for half in range(2):
                for piece in range(2):
                    at = 256 + (2 * half + piece) * 64
                    dno[2 * f + half, :, piece * 128 : piece * 128 + 128] = wf[f, at : at + 64, :]
        proj.start()
        loop(1, NS, lambda k: down_to(k).start())
        dn[pl.ds(pl.multiple_of(me * HD, HD), HD), :] = dno[me]
        pj[me] = pjo[...]

    def keep(m):
        pair = pl.ds(2 * m, 2)
        return pltpu.make_async_copy(normed_all.at[pair], nrm.at[pair], n_c.at[m])

    def norm_and_project(k):
        hidden.step(k)

        @pl.when(k == 4)
        def _():
            send_rest()

        @pl.when(k == 3)
        def _():
            cot.start()

        m = chips.at(k)
        values = hid[pl.ds(2 * m, 2)].reshape(2 * TOK, D).astype(F32)
        standard = layer_norm(values, 1.0, 0.0)
        normed = (standard * sm[0:1, :] + sm[1:2, :]).astype(BF16)
        normed_all[pl.ds(2 * m, 2)] = standard.astype(BF16).reshape(2, TOK, D)
        keep(m).start()
        block = dot(wq[...], normed, 1, 1) + qvb
        qkvt[m] = block.astype(BF16)
        at = pl.ds(pl.multiple_of(m * 256, 256), 256)
        qkvr[0, at, :] = block[0:64].T.astype(BF16)
        keys = block[64:128].T.astype(BF16)
        qkvr[1, at, :] = keys
        kr[at, 0:HD] = keys
        qkvr[2, at, :] = block[128:192].T.astype(BF16)

    loop(0, NF, norm_and_project)
    extras = query_extras(me)

    def ctx_to(j):
        return remote(ctxo.at[j], ctxt.at[me], x_s.at[j], x_r.at[me], seq=j)

    between = {0: [proj.pass_x, proj.pass_y], 3: [cot.pass_x], 4: [proj.pass_f, cot.pass_y]}
    for j in range(NF):
        for relay in between.get(j, []):
            relay()
        n = (j + 1) * 256
        queries = jnp.concatenate([(qkvt[j, 0:64, :].astype(F32) * 0.125).astype(BF16), extras], axis=0)
        scores = dot(kr[0:n, :], queries)
        kpos = lax.broadcasted_iota(jnp.int32, (256, 256), 0)
        qpos = lax.broadcasted_iota(jnp.int32, (256, 256), 1)
        last = jnp.where(kpos <= qpos, scores[n - 256 :], -1e30)
        scores = last if j == 0 else jnp.concatenate([scores[: n - 256], last], axis=0)
        peak = jnp.max(scores, axis=0, keepdims=True)
        expo = jnp.exp(scores - peak)
        total = jnp.sum(expo, axis=0, keepdims=True)
        lse[j : j + 1, :] = peak + jnp.log(total)
        weights = expo.astype(BF16)
        acc = dot(qkvt[0, 128:192, :], weights[0:256])
        for i in range(1, j + 1):
            acc += dot(qkvt[i, 128:192, :], weights[i * 256 : i * 256 + 256])
        context = (acc / total).astype(BF16)
        for half in range(2):
            target = 2 * j + half
            ctxo[target] = context[:, half * 128 : half * 128 + 128]

            @pl.when(me != target)
            def _():
                ctx_to(target).start()

            @pl.when(me == target)
            def _():
                ctxt[target] = ctxo[target]

    cot.pass_f()
    proj.finish()

    def ctx_from(k):
        other = lax.rem(me + k, NS)
        remote(ctxo.at[other], ctxt.at[other], x_s.at[other], x_r.at[other], seq=other).wait_recv()

    loop(1, NS, ctx_from)
    context = ctxt[...].reshape(D, TOK).astype(F32).T.astype(BF16)
    ctxr[...] = context
    middle = hid_ref[...].astype(F32) + dot(context, pj[...].reshape(D, D), 1, 1) + sm[2:3, :]
    mid[...] = middle
    n2[...] = layer_norm(middle, sm[3:4, :], sm[4:5, :]).astype(BF16)

    tokens = Gather(chips, n2, xa, n_s, n_r, n_h)
    tokens.start()
    xa[chips.me] = n2[...]
    grads = Reduce(chips, g_part, g_pair, g_total, g_got, g1s, g1r, g2s, g2r)
    downs = Reduce(chips, d_part, d_pair, dtot, None, d1s, d1r, None, None)
    gub[...] = jnp.zeros_like(gub)
    loop(1, NS, down_from)
    cot.finish()

    def put(side, chip, values):
        side.part[pl.ds(2 * chip, 2)] = values.astype(BF16).reshape(2, TOK, D)
        side.pairing(chip).start()

    def feed(k):
        @pl.when(k == 1)
        def _():
            tokens.pass_x()
            tokens.pass_y()

        tokens.step(k)
        m = chips.at(k)
        rows = xa[pl.ds(2 * m, 2)].reshape(2 * TOK, D)
        upper = dot(rows, up[...]) + ub[0:1, :]
        square = upper * upper
        bend = jnp.tanh(0.7978845608 * upper * (1.0 + 0.044715 * square))
        half = 0.5 * (1.0 + bend)
        active = (upper * half).astype(BF16)
        slope = half + 0.5 * upper * (1.0 - bend * bend) * (0.7978845608 * (1.0 + 0.134145 * square))
        cots = cota[pl.ds(2 * m, 2)].reshape(2 * TOK, D)
        grad = (dot(cots, dn[...]) * slope).astype(BF16)
        at = pl.ds(pl.multiple_of(m * 256, 256), 256)
        act[at, :] = active
        gu[at, :] = grad
        gub[0:1, :] += jnp.sum(grad.astype(F32), axis=0, keepdims=True)
        put(grads, m, dot(grad, up[...], 1, 1))
        put(downs, m, dot(active, dn[...], 1, 1))

        @pl.when(k > 0)
        def _():
            grads.merge(chips.at(k - 1))
            downs.merge(chips.at(k - 1))

        for at, message in ((3, 4), (4, 3), (5, 5), (6, 2)):

            @pl.when(k == at)
            def _():
                grads.begin(message)

    loop(0, NF, feed)
    grads.merge(chips.fy)
    grads.far()
    downs.merge(chips.fy)
    gup[...] = dot(xa[...].reshape(NS * TOK, D), gu[...], 0, 0).astype(BF16)
    grads.turn()
    gdn[...] = dot(cota[...].reshape(NS * TOK, D), act[...], 0, 0).astype(BF16)
    grads.back()
    grads.across()
    tok[...] = jnp.zeros_like(tok)
    own_cot = cota[chips.me].astype(F32)
    tok[5:6, :] = jnp.sum(own_cot, axis=0, keepdims=True)
    back, tok[3:4, :], tok[4:5, :] = norm_back(mid[...], sm[3:4, :], grads.finish())
    total = own_cot + back
    gmid[...] = total
    low = total.astype(BF16)
    branch[...] = low
    tok[2:3, :] = jnp.sum(low.astype(F32), axis=0, keepdims=True)
    gct[...] = dot(low, pj[...].reshape(D, D)).T.astype(BF16).reshape(NS, HD, TOK)
    loop(0, NF, lambda m: keep(m).wait())
    hidden.drain()
    cot.drain()
    proj.drain()
    qkv_rows.drain()
    other_rows.drain()
    loop(1, NS, lambda k: small_to(k).wait_send())
    loop(1, NS, lambda k: down_to(k).wait_send())
    for j in range(3):
        head, kind, src, dst = q_block(j)

        @pl.when(head != me)
        def _():
            remote(src, dst, q_s.at[j], q_r.at[kind], seq=head).wait_send()

    def ctx_sent(k):
        other = lax.rem(me + k, NS)
        remote(ctxo.at[other], ctxt.at[me], x_s.at[other], x_r.at[me], seq=other).wait_send()

    loop(1, NS, ctx_sent)
    tokens.drain()
    grads.drain()
    loop(0, NF, lambda chip: downs.pairing(chip).wait_send())


def vm():
    return pl.BlockSpec(memory_space=pltpu.VMEM)


def hbm():
    return pl.BlockSpec(memory_space=pl.ANY)


def sems(*counts):
    return [pltpu.SemaphoreType.DMA(n if isinstance(n, tuple) else (n,)) for n in counts]


def params(number):
    return pltpu.CompilerParams(collective_id=number, has_side_effects=True, vmem_limit_bytes=62 * MIB)


def reduce_scratch(rows):
    return [pltpu.VMEM((NF, rows, D), BF16), pltpu.VMEM((NF, rows, D), BF16), pltpu.VMEM((7, rows, D), BF16)]


def run_a(*operands):
    shapes = [
        ((NS, TOK, D), BF16), ((NF, 192, 256), BF16), ((3, NS * TOK, HD), BF16), ((NF, 256), F32), ((TOK, D), F32),
        ((TOK, D), BF16), ((192, D), BF16), ((16, D), F32), ((TOK, D), F32), ((TOK, D), BF16), ((NS, HD, TOK), BF16),
        ((8, D), F32), ((NF, TOK, D), BF16), ((D, HID), BF16), ((D, HID), BF16), ((8, HID), F32),
    ]
    return pl.pallas_call(
        kernel_a,
        out_shape=[jax.ShapeDtypeStruct(*s) for s in shapes],
        in_specs=[vm() for _ in operands],
        out_specs=[hbm() if i == 0 else vm() for i in range(len(shapes))],
        scratch_shapes=[
            pltpu.VMEM((NS, TOK, D), BF16),
            pltpu.VMEM((NF, PACK, 128), BF16),
            pltpu.VMEM((NS, 16, 128), BF16),
            pltpu.VMEM((192, D), BF16),
            pltpu.VMEM((NS, HD, HID), BF16),
            pltpu.VMEM((HD, D), BF16),
            pltpu.VMEM((NS * TOK, 128), BF16),
            pltpu.VMEM((NS, HD, TOK), BF16),
            pltpu.VMEM((NS, HD, TOK), BF16),
            pltpu.VMEM((PACK, 128), BF16),
            pltpu.VMEM((16, 128), BF16),
            pltpu.VMEM((NS, TOK, D), BF16),
            pltpu.VMEM((NS, TOK, D), BF16),
            pltpu.VMEM((TOK, D), BF16),
            pltpu.VMEM((D, HID), BF16),
            pltpu.VMEM((D, HID), BF16),
            pltpu.VMEM((NS, HD, D), BF16),
            pltpu.VMEM((8, HID), F32),
            pltpu.VMEM((NS, TOK, D), BF16),
            pltpu.VMEM((NS * TOK, HID), BF16),
            pltpu.VMEM((NS * TOK, HID), BF16),
            pltpu.VMEM((NS, TOK, D), BF16),
        ]
        + reduce_scratch(TOK)
        + [pltpu.VMEM((NS, TOK, D), BF16), pltpu.VMEM((NF, TOK, D), BF16)]
        + sems(22, (8, 2), 8) * 4
        + sems(8, 8, 8, 8, 16, 16, 3, 3, 16, 16, 16, 16, 8, 8, 8, 16, 16, 8, 8),
        compiler_params=params(0),
        name="forward_and_feed",
    )(*operands)


def kernel_b(
    gc_ref, qkvt, qkvr, lse, wq, nrm_hbm, branch, dtot, ctx_ref, gdn_ref, gup_ref, hid_ref, gmid, mid, sm, tok, gub,
    layer_out, input_grad, w_qkv, w_proj, w_up, w_down, small,
    dct, gjt, kr, dk, dv, part, pair, total, got, d_total, d_got, gpj, p_pair, p_total, p_got, d1,
    u_pack, u_got, u_part, u_cross, u_keep, t_pack, t_got, t_part, t_cross, t_keep, gqkv, q1, tiles, m1, m2, sgot, nrm,
    x_s, x_r, r1s, r1r, r2s, r2r, d2s, d2r, p1s, p1r, p2s, p2r, y_s, y_r, u_s, u_r, t_s, t_r, q_s, q_r, m_s, m_r,
    v_s, v_r, l_s, n_c,
):
    me, core, sib, row = places()
    chips = Chips()
    local = pltpu.make_async_copy(dtot, d_total, l_s)
    local.start()
    normed_in = pltpu.make_async_copy(nrm_hbm, nrm, n_c)
    normed_in.start()
    sem = barrier_seq_all(me)
    barrier_fsdp(sem, row)
    pl.semaphore_wait(sem, NS - 1 + NF - 1)
    downs = Reduce(chips, None, None, d_total, d_got, None, None, d2s, d2r)
    projs = Reduce(chips, gpj, p_pair, p_total, p_got, p1s, p1r, p2s, p2r)
    ups = RowSums(u_pack, u_got, u_part, u_cross, u_s, u_r)
    rest = RowSums(t_pack, t_got, t_part, t_cross, t_s, t_r)

    def block(other):
        return pl.ds(pl.multiple_of(other * HD, HD), HD)

    def down_to(k):
        other = lax.rem(me + k, NS)
        return remote(gdn_ref.at[block(other), :], d1.at[me], y_s.at[k], y_r.at[me], seq=other)

    def down_from(k):
        other = lax.rem(me + k, NS)
        remote(gdn_ref.at[block(me), :], d1.at[other], y_s.at[k], y_r.at[other], seq=other).wait_recv()

    def send_weights():
        loop(1, NS, down_from)
        for f in range(NF):
            lanes = slice(f * 128, f * 128 + 128)
            for half in range(2):
                for piece in range(2):
                    at = (2 * half + piece) * 64
                    u_pack[f, at : at + 64, :] = d1[2 * f + half, :, piece * 128 : piece * 128 + 128]
            u_pack[f, 256:384, :] = gup_ref[lanes, 0:128]
            u_pack[f, 384:512, :] = gup_ref[lanes, 128:256]
        ups.start()

    def merge_projs():
        loop(0, NF, projs.merge)
        projs.far()
        projs.sides()

    def q_block(kind):
        index = kind * H + me
        holder, slot = index // 3, lax.rem(index, 3)
        return holder, slot, gqkv.at[pl.ds(kind * HD, HD), :], q1.at[block(slot), :]

    def tokens(k):
        other = lax.rem(me + k, NS)
        return remote(tiles.at[other // 2], m1.at[me], m_s.at[k], m_r.at[me], seq=other)

    def tokens_from(k):
        other = lax.rem(me + k, NS)
        remote(tiles.at[0], m1.at[other], m_s.at[k], m_r.at[other], seq=other).wait_recv()

    def vectors(k):
        return remote(m2, sgot.at[row], v_s.at[k], v_r.at[row], fsdp=lax.rem(row + k, NF))

    def vectors_from(k):
        other = lax.rem(row + k, NF)
        remote(m2, sgot.at[other], v_s.at[k], v_r.at[other], fsdp=other).wait_recv()

    def ctx_to(k):
        other = lax.rem(me + k, NS)
        return remote(gc_ref.at[other], dct.at[me], x_s.at[k], x_r.at[me], seq=other)

    def ctx_from(k):
        other = lax.rem(me + k, NS)
        remote(gc_ref.at[me], dct.at[other], x_s.at[k], x_r.at[other], seq=other).wait_recv()

    loop(1, NS, lambda k: ctx_to(k).start())
    dct[me] = gc_ref[me]
    d1[me] = gdn_ref[block(me), :]
    kr[:, HD:] = key_extras(NS * TOK)
    kr[:, 0:HD] = qkvr[1]
    dk[...] = jnp.zeros_like(dk)
    dv[...] = jnp.zeros_like(dv)
    extras = query_extras(me)
    for f in range(NF):
        lanes = slice(f * 128, f * 128 + 128)
        columns = branch[:, lanes].astype(F32).T.astype(BF16)
        gpj[2 * f : 2 * f + 2] = dot(columns, ctx_ref[...]).astype(BF16).reshape(2, HD, D)
    loop(1, NS, lambda k: down_to(k).start())
    loop(0, NF, lambda chip: projs.pairing(chip).start())
    local.wait()
    normed_in.wait()
    loop(1, NS, ctx_from)
    downs.far()
    downs.sides()
    between = {3: [send_weights], 5: [merge_projs], 7: [downs.turn]}
    for j in range(NF):
        for relay in between.get(j, []):
            relay()
        n = (j + 1) * 256
        at = slice(j * 256, n)
        queries = jnp.concatenate([(qkvt[j, 0:64, :].astype(F32) * 0.125).astype(BF16), extras], axis=0)
        scores = dot(kr[0:n, :], queries)
        probs = jnp.exp(scores - lse[j : j + 1, :])
        kpos = lax.broadcasted_iota(jnp.int32, (256, 256), 0)
        qpos = lax.broadcasted_iota(jnp.int32, (256, 256), 1)
        last = jnp.where(kpos <= qpos, probs[n - 256 :], 0.0)
        probs = last if j == 0 else jnp.concatenate([probs[: n - 256], last], axis=0)
        gctx = jnp.concatenate([dct[2 * j], dct[2 * j + 1]], axis=1)
        gprobs = dot(qkvr[2, 0:n, :], gctx)
        inner = jnp.sum(probs * gprobs, axis=0, keepdims=True)
        gscores = (probs * (gprobs - inner) * 0.125).astype(BF16)
        gq = dot(qkvt[0, 64:128, :], gscores[0:256])
        for i in range(1, j + 1):
            gq += dot(qkvt[i, 64:128, :], gscores[i * 256 : i * 256 + 256])
        gjt[j, 0:64, :] = gq.astype(BF16)
        dk[0:n, :] += dot(gscores, qkvr[0, at, :])
        dv[0:n, :] += dot(probs.astype(BF16), gctx.astype(F32).T.astype(BF16))
    for j in range(NF):
        at = slice(j * 256, j * 256 + 256)
        gjt[j, 64:128, :] = dk[at, :].T.astype(BF16)
        gjt[j, 128:192, :] = dv[at, :].T.astype(BF16)

    acc = jnp.zeros((192, D), F32)
    sums = jnp.zeros((192, 1), F32)
    for j in range(NF):
        acc += dot(gjt[j], nrm[2 * j : 2 * j + 2].reshape(2 * TOK, D))
        sums += jnp.sum(gjt[j].astype(F32), axis=1, keepdims=True)
    gqkv[...] = (acc * sm[0:1, :] + sums * sm[1:2, :]).astype(BF16)
    head = wq[...].astype(F32)
    gain = jnp.sum(acc * head, axis=0, keepdims=True)
    shift = jnp.sum(sums * head, axis=0, keepdims=True)
    line = jnp.concatenate([gain, shift, tok[2:8, :]], axis=0)
    for t in range(NF):
        tiles[t] = line[:, t * 128 : t * 128 + 128]
    loop(1, NS, lambda k: tokens(k).start())
    m1[me] = tiles[me // 2]
    m2[...] = jnp.zeros_like(m2)
    line = jnp.broadcast_to(sums, (192, 128)).T
    m2[8:9, 0:64] = line[0:1, 0:64]
    m2[8:9, 64:128] = line[0:1, 128:192]
    m2[9:10, :] = gub[0:1, 0:128]
    m2[10:11, :] = gub[0:1, 128:256]
    for kind in range(3):
        holder, slot, src, dst = q_block(kind)

        @pl.when(holder != me)
        def _():
            remote(src, dst, q_s.at[kind], q_r.at[slot], seq=holder).start()

        @pl.when(holder == me)
        def _():
            dst[...] = src[...]

    norms = Reduce(chips, part, pair, total, got, r1s, r1r, r2s, r2r)
    downs.back()
    during = {
        1: [lambda: norms.begin(0, 1), projs.turn],
        2: [downs.across],
        3: [lambda: norms.begin(2), projs.back],
        4: [projs.across],
        5: [lambda: norms.begin(5), norms.turn],
        6: [lambda: norms.begin(3)],
    }

    def step(k):
        m = chips.at(NF - 1 - k)
        rows = gjt[m].astype(F32).T.astype(BF16)
        part[pl.ds(2 * m, 2)] = dot(rows, wq[...]).astype(BF16).reshape(2, TOK, D)
        norms.pairing(m).start()

        @pl.when(k > 0)
        def _():
            norms.merge(chips.at(NF - k))

        for at, events in during.items():

            @pl.when(k == at)
            def _():
                for event in events:
                    event()

    loop(0, NF, step)
    norms.begin(4)
    norms.merge(chips.own)
    ups.middle(u_keep)
    loop(1, NS, tokens_from)
    vector = m1[0]
    for p in range(1, NS):
        vector += m1[p]
    m2[0:8, :] = vector
    loop(1, NF, lambda k: vectors(k).start())
    sgot[row] = m2[...]
    norms.back()
    for slot in range(3):

        @pl.when(lax.rem(3 * me + slot, H) != me)
        def _():
            remote(
                gqkv.at[pl.ds(0, HD), :], q1.at[pl.ds(slot * HD, HD), :], q_s.at[0], q_r.at[slot], seq=sib
            ).wait_recv()

    proj_sum = projs.finish().astype(BF16)
    for f in range(NF):
        lanes = slice(f * 128, f * 128 + 128)
        t_pack[f, 0:192, :] = q1[:, lanes]
        t_pack[f, 192:256, :] = proj_sum[:, lanes]
    rest.start()
    norms.across()
    layer_out[...] = (mid[...] + downs.finish() + sm[5:6, :]).astype(BF16)
    rest.middle(t_keep)
    rows = ups.finish(u_keep)
    for piece in range(4):
        w_down[:, piece * 128 : piece * 128 + 128] = rows[piece * HD : piece * HD + HD]
    w_up[:, 0:128] = rows[256:384]
    w_up[:, 128:256] = rows[384:512]
    rows = rest.finish(t_keep)
    w_qkv[...] = rows[0:192]
    w_proj[...] = rows[192:256]
    loop(1, NF, vectors_from)
    vector = sgot[0]
    for f in range(1, NF):
        vector += sgot[f]
    small[...] = vector
    back, _, _ = norm_back(hid_ref[...].astype(F32), sm[0:1, :], norms.finish())
    input_grad[...] = (gmid[...] + back).astype(BF16)
    norms.drain()
    downs.drain(False)
    projs.drain()
    ups.drain()
    rest.drain()
    loop(1, NS, lambda k: ctx_to(k).wait_send())
    loop(1, NS, lambda k: down_to(k).wait_send())
    loop(1, NS, lambda k: tokens(k).wait_send())
    loop(1, NF, lambda k: vectors(k).wait_send())
    for kind in range(3):
        holder, slot, src, dst = q_block(kind)

        @pl.when(holder != me)
        def _():
            remote(src, dst, q_s.at[kind], q_r.at[slot], seq=holder).wait_send()


def row_scratch(rows):
    return [
        pltpu.VMEM((NF, rows, 128), BF16),
        pltpu.VMEM((4, 2, rows, 128), BF16),
        pltpu.VMEM((2, rows, 128), BF16),
        pltpu.VMEM((rows, 128), BF16),
        pltpu.VMEM((rows, 128), F32),
    ]


def run_b(*operands):
    shapes = [
        ((TOK, D), BF16), ((TOK, D), BF16), ((192, 128), F32), ((HD, 128), F32), ((128, HID), F32), ((HD, 512), F32),
        ((16, 128), F32),
    ]
    return pl.pallas_call(
        kernel_b,
        out_shape=[jax.ShapeDtypeStruct(*s) for s in shapes],
        in_specs=[hbm() if i in (5, 7) else vm() for i in range(len(operands))],
        out_specs=[vm() for _ in shapes],
        scratch_shapes=[
            pltpu.VMEM((NS, HD, TOK), BF16),
            pltpu.VMEM((NF, 192, 256), BF16),
            pltpu.VMEM((NS * TOK, 128), BF16),
            pltpu.VMEM((NS * TOK, HD), F32),
            pltpu.VMEM((NS * TOK, HD), F32),
            pltpu.VMEM((NS, TOK, D), BF16),
        ]
        + reduce_scratch(TOK)
        + [pltpu.VMEM((NF, TOK, D), BF16), pltpu.VMEM((7, TOK, D), BF16), pltpu.VMEM((NS, HD, D), BF16)]
        + reduce_scratch(HD)
        + [pltpu.VMEM((NS, HD, HID), BF16)]
        + row_scratch(512)
        + row_scratch(256)
        + [
            pltpu.VMEM((192, D), BF16),
            pltpu.VMEM((192, D), BF16),
            pltpu.VMEM((NF, 8, 128), F32),
            pltpu.VMEM((NS, 8, 128), F32),
            pltpu.VMEM((16, 128), F32),
            pltpu.VMEM((NF, 16, 128), F32),
            pltpu.VMEM((NS, TOK, D), BF16),
        ]
        + sems(16, 16, 8, 8, 16, 16, 16, 16, 8, 8, 16, 16, 16, 16, 4, 4, 4, 4, 3, 3, 16, 16, 8, 8)
        + [pltpu.SemaphoreType.DMA, pltpu.SemaphoreType.DMA],
        compiler_params=params(2),
        name="attend_back",
    )(*operands)


def kernel_f(*refs):
    half = len(refs) // 2
    for src, dst in zip(refs[: half - 1], refs[half:-1]):
        dst[...] = src[...]
    values = refs[half - 1][...]
    mine = jnp.where(lax.rem(lax.axis_index("seq"), 2) == 0, values[0:8, 0:HD], values[0:8, HD:])
    refs[-1][...] = values
    refs[-1][0:8, 0:HD] = mine


def run_f(*operands):
    return pl.pallas_call(
        kernel_f,
        out_shape=[jax.ShapeDtypeStruct(o.shape, o.dtype) for o in operands],
        in_specs=[vm() for _ in operands],
        out_specs=[vm() for _ in operands],
        name="finish",
    )(*operands)


def per_device(
    hidden_in, norm1_gain, norm1_shift, qkv_weight, query_bias, value_bias, proj_weight, proj_bias,
    norm2_gain, norm2_shift, up_weight, up_bias, down_weight, down_bias, out_cotangent,
):
    hid, cot = hidden_in[0], out_cotangent[0]
    vectors = [norm1_gain, norm1_shift, proj_bias, norm2_gain, norm2_shift, down_bias, query_bias, value_bias]
    vectors = jnp.concatenate([v[None] for v in vectors] + [up_bias.reshape(4, HD)], axis=0)
    (nrm, qkvt, qkvr, lse, middle, ctx, wq, sm, gmid, branch, gctx, tok, downs, gup, gdn, gub) = run_a(
        hid, cot, qkv_weight.T, proj_weight.T, up_weight, down_weight.T, vectors
    )
    results = run_b(
        gctx, qkvt, qkvr, lse, wq, nrm, branch, downs, ctx, gdn, gup, hid, gmid, middle, sm, tok, gub
    )
    layer_out, input_grad, w_qkv, w_proj, w_up, w_down, vecs = run_f(*results)
    return (
        layer_out[None],
        input_grad[None],
        vecs[0, :64],
        vecs[1, :64],
        w_qkv.T,
        vecs[8, :64],
        vecs[8, 64:],
        w_proj.T,
        vecs[2, :64],
        vecs[3, :64],
        vecs[4, :64],
        w_up,
        vecs[9:11].reshape(256),
        w_down.T,
        vecs[5, :64],
    )


def solution(mesh):
    act, vec, mat = P("fsdp", "seq", None), P("seq"), P("fsdp", "seq")
    return jax.shard_map(
        per_device,
        mesh=mesh,
        in_specs=(act, vec, vec, mat, vec, vec, mat, vec, vec, vec, mat, vec, mat, vec, act),
        out_specs=(act, act, vec, vec, mat, vec, vec, mat, vec, vec, vec, mat, vec, mat, vec),
        check_vma=False,
    )
```

```python
import functools

import jax
import jax.numpy as jnp
from jax import lax
from jax.experimental import pallas as pl
from jax.experimental.pallas import tpu as pltpu
from jax.sharding import PartitionSpec as P

H = 16
HD = 64
D = 1024
HID = 256
TOK = 128
NS = 16
NF = 8
PACK = 768
MESH = pl.DeviceIdType.MESH
F32 = jnp.float32
BF16 = jnp.bfloat16
MIB = 1024 * 1024


def dot(left, right, lc=1, rc=0):
    return lax.dot_general(left, right, (((lc,), (rc,)), ((), ())), preferred_element_type=F32)


def layer_norm(values, gain, shift):
    average = jnp.mean(values, axis=-1, keepdims=True)
    centered = values - average
    spread = jnp.mean(centered * centered, axis=-1, keepdims=True)
    return centered * lax.rsqrt(spread + 1e-05) * gain + shift


def norm_back(values, gain, grad):
    average = jnp.mean(values, axis=-1, keepdims=True)
    centered = values - average
    spread = jnp.mean(centered * centered, axis=-1, keepdims=True)
    inverse = lax.rsqrt(spread + 1e-05)
    normed = centered * inverse
    scaled = grad * gain
    mean = jnp.mean(scaled, axis=-1, keepdims=True)
    slant = jnp.mean(scaled * normed, axis=-1, keepdims=True)
    back = inverse * (scaled - mean - normed * slant)
    return back, jnp.sum(grad * normed, axis=0, keepdims=True), jnp.sum(grad, axis=0, keepdims=True)


def remote(src, dst, send, recv, **where):
    return pltpu.make_async_remote_copy(
        src_ref=src, dst_ref=dst, send_sem=send, recv_sem=recv, device_id=where, device_id_type=MESH
    )


def places():
    me = lax.axis_index("seq")
    core = lax.rem(me, 2)
    return me, core, me + 1 - 2 * core, lax.axis_index("fsdp")


def barrier_seq_all(me):
    sem = pltpu.get_barrier_semaphore()

    def body(k, carry):
        pl.semaphore_signal(sem, inc=1, device_id={"seq": lax.rem(me + k, NS)}, device_id_type=MESH)
        return carry

    lax.fori_loop(1, NS, body, 0)
    return sem


def barrier_fsdp(sem, row):
    def body(k, carry):
        pl.semaphore_signal(sem, inc=1, device_id={"fsdp": lax.rem(row + k, NF)}, device_id_type=MESH)
        return carry

    lax.fori_loop(1, NF, body, 0)


def loop(low, high, body):
    def step(k, carry):
        body(k)
        return carry

    lax.fori_loop(low, high, step, 0)


class Chips:
    def __init__(self):
        self.me, self.core, self.sib, self.row = places()
        self.own = self.me // 2
        step = 1 - 2 * lax.rem(self.own, 2)
        self.y = self.own + step
        self.r, self.f, self.l = (lax.rem(self.own + d, NF) for d in (2, 4, 6))
        self.ry, self.fy, self.ly = self.r + step, self.f + step, self.l + step

    def at(self, k):
        j = k // 2
        ring = lax.rem(self.own // 2 + j + (j // 2) * (5 - 2 * j), 4)
        return 2 * ring + lax.rem(self.own + k, 2)

    def device(self, chip):
        return 2 * chip + self.core


class Gather:
    def __init__(self, chips, own, out, send, recv, near):
        self.c, self.own, self.out, self.send, self.recv, self.near_sem = chips, own, out, send, recv, near
        rows = out.shape[1] // 2
        self.halves = (pl.ds(0, rows), pl.ds(rows, rows))

    def message(self, i, chip, half, to):
        c = self.c
        dst = self.out.at[c.device(chip), self.halves[half]]
        src = self.own.at[self.halves[half]] if i < 6 else dst
        return remote(src, dst, self.send.at[i], self.recv.at[chip, half], seq=c.device(to))

    def messages(self):
        c = self.c
        plan = [
            (c.own, 0, c.r), (c.own, 1, c.l), (c.own, 0, c.y), (c.own, 1, c.r), (c.own, 0, c.l), (c.own, 1, c.y),
            (c.l, 0, c.r), (c.r, 1, c.l), (c.y, 0, c.r), (c.y, 0, c.l), (c.y, 1, c.r), (c.y, 1, c.l),
            (c.f, 0, c.y), (c.f, 1, c.y),
        ]
        return [functools.partial(self.message, i, *p) for i, p in enumerate(plan)]

    def begin(self, *which):
        plan = self.messages()
        for i in which:
            plan[i]().start()

    def arrive(self, chip, half):
        self.message(6, chip, half, self.c.own).wait_recv()

    def hand(self, chip, first=False):
        block = self.c.device(chip)
        src = self.own if first else self.out.at[block]
        return remote(src, self.out.at[block], self.send.at[14 + chip], self.near_sem.at[chip], seq=self.c.sib)

    def near(self, chip):
        block = 2 * chip + 1 - self.c.core
        remote(
            self.out.at[block], self.out.at[block], self.send.at[0], self.near_sem.at[chip], seq=self.c.sib
        ).wait_recv()

    def start(self):
        self.begin(0, 1, 2, 3, 4, 5)
        self.hand(self.c.own, True).start()

    def pass_x(self):
        c = self.c
        self.arrive(c.l, 0)
        self.begin(6)
        self.arrive(c.r, 1)
        self.begin(7)

    def pass_y(self):
        c = self.c
        self.arrive(c.y, 0)
        self.begin(8, 9)
        self.arrive(c.y, 1)
        self.begin(10, 11)
        self.hand(c.y).start()

    def pass_f(self):
        c = self.c
        self.arrive(c.f, 0)
        self.begin(12)
        self.arrive(c.f, 1)
        self.begin(13)
        self.hand(c.f).start()

    def take(self, name):
        c = self.c
        chip = getattr(c, name)
        for half in {"r": (0,), "l": (1,)}.get(name, (0, 1)):
            self.arrive(chip, half)
        self.hand(chip).start()

    def step(self, k):
        @pl.when(k == 2)
        def _():
            self.take("r")

        @pl.when(k == 3)
        def _():
            self.pass_f()
            self.take("ry")

        @pl.when(k == 4)
        def _():
            self.take("l")

        @pl.when(k == 5)
        def _():
            self.take("ly")

        @pl.when(k == 7)
        def _():
            self.take("fy")

        self.near(self.c.at(k))

    def finish(self):
        for name in ("r", "ry", "l", "ly", "fy"):
            self.take(name)
        loop(0, NF, self.near)

    def drain(self):
        for message in self.messages():
            message().wait_send()
        loop(0, NF, lambda chip: self.hand(chip, True).wait_send())


class Reduce:
    def __init__(self, chips, part, pair, total, got, hop, hop_recv, send, recv):
        self.c, self.part, self.pair, self.total, self.got = chips, part, pair, total, got
        self.hop, self.hop_recv, self.send, self.recv = hop, hop_recv, send, recv
        rows = total.shape[1]
        self.low, self.high, self.all = pl.ds(0, rows // 2), pl.ds(rows // 2, rows // 2), pl.ds(0, rows)

    def pairing(self, chip):
        src = self.part.at[2 * chip + 1 - self.c.core]
        return remote(src, self.pair.at[chip], self.hop.at[chip], self.hop_recv.at[chip], seq=self.c.sib)

    def merge(self, chip):
        self.pairing(chip).wait_recv()
        both = self.part[self.c.device(chip)].astype(F32) + self.pair[chip].astype(F32)
        self.total[chip] = both.astype(BF16)

    def message(self, i):
        c = self.c
        chip, rows, slot, to = (
            (c.fy, self.low, 0, c.y), (c.fy, self.high, 0, c.y), (c.ly, self.all, 3, c.l), (c.ry, self.all, 2, c.r),
            (c.r, self.high, 4, c.r), (c.l, self.low, 5, c.l), (c.f, self.low, 1, c.r), (c.f, self.high, 1, c.l),
            (c.r, self.low, 4, c.r), (c.l, self.high, 5, c.l), (c.y, self.all, 6, c.y),
        )[i]
        return remote(
            self.total.at[chip, rows], self.got.at[slot, rows], self.send.at[i], self.recv.at[i], seq=c.device(to)
        )

    def begin(self, *which):
        for i in which:
            self.message(i).start()

    def add(self, i, chip, slot, rows):
        self.message(i).wait_recv()
        both = self.total[chip, rows].astype(F32) + self.got[slot, rows].astype(F32)
        self.total[chip, rows] = both.astype(BF16)

    def far(self):
        self.begin(0, 1)

    def sides(self):
        self.begin(2, 3, 4, 5)

    def turn(self):
        c = self.c
        self.add(0, c.f, 0, self.low)
        self.begin(6)
        self.add(1, c.f, 0, self.high)
        self.begin(7)

    def back(self):
        c = self.c
        self.add(6, c.r, 1, self.low)
        self.begin(8)
        self.add(7, c.l, 1, self.high)
        self.begin(9)

    def across(self):
        c = self.c
        self.add(2, c.y, 3, self.all)
        self.add(3, c.y, 2, self.all)
        self.begin(10)

    def finish(self):
        for i in (4, 5, 8, 9, 10):
            self.message(i).wait_recv()
        total = self.total[self.c.own].astype(F32)
        for slot in (4, 5, 6):
            total += self.got[slot].astype(F32)
        return total

    def drain(self, paired=True):
        if paired:
            loop(0, NF, lambda chip: self.pairing(chip).wait_send())
        for i in range(11):
            self.message(i).wait_send()


class Rows:
    def __init__(self, src, out, rows, send, recv):
        self.src, self.out, self.rows, self.send, self.recv = src, out, rows, send, recv
        self.row = lax.axis_index("fsdp")
        self.mate = self.row + 1 - 2 * lax.rem(self.row, 2)

    def message(self, k, second):
        if second:
            group = self.mate
            src = self.out.at[group, self.rows]
            slot = k + 3
        else:
            group = self.row
            src = self.src.at[self.rows]
            slot = k
        to = self.mate if k == 0 else lax.rem(self.row + 2 * k, NF)
        return remote(src, self.out.at[group, self.rows], self.send.at[slot], self.recv.at[group], fsdp=to)

    def wait(self, group):
        dst = self.out.at[group, self.rows]
        remote(dst, dst, self.send.at[0], self.recv.at[group], fsdp=self.mate).wait_recv()

    def start(self):
        for k in range(4):
            self.message(k, False).start()

    def pass_on(self):
        self.wait(self.mate)
        for k in range(1, 4):
            self.message(k, True).start()

    def finish(self):
        for k in range(1, 4):
            self.wait(lax.rem(self.row + 2 * k, NF))
            self.wait(lax.rem(self.mate + 2 * k, NF))

    def drain(self):
        for k in range(4):
            self.message(k, False).wait_send()
        for k in range(1, 4):
            self.message(k, True).wait_send()


class RowSums:
    def __init__(self, pack, got, part, cross, send, recv):
        self.pack, self.got, self.part, self.cross, self.send, self.recv = pack, got, part, cross, send, recv
        self.row = lax.axis_index("fsdp")
        self.high = lax.rem(self.row, 2)
        self.z = self.row // 2

    def message(self, k):
        to = lax.rem(self.row + 2 * k, NF)
        src = self.pack.at[pl.ds(2 * (to // 2), 2)]
        return remote(src, self.got.at[k], self.send.at[k], self.recv.at[k], fsdp=to)

    def last(self):
        to = self.row + 1 - 2 * self.high
        return remote(self.part.at[1], self.cross, self.send.at[0], self.recv.at[0], fsdp=to)

    def start(self):
        for k in range(1, 4):
            self.message(k).start()

    def middle(self, keep):
        for k in range(1, 4):
            self.message(k).wait_recv()

        def total(which):
            value = self.pack[2 * self.z + which].astype(F32)
            for k in range(1, 4):
                value += self.got[k, which].astype(F32)
            return value

        keep[...] = total(self.high)
        self.part[1] = total(1 - self.high).astype(BF16)
        self.last().start()

    def finish(self, keep):
        self.last().wait_recv()
        return keep[...] + self.cross[...].astype(F32)

    def drain(self):
        for k in range(1, 4):
            self.message(k).wait_send()
        self.last().wait_send()


def key_extras(rows):
    lane = lax.broadcasted_iota(jnp.int32, (rows, HD), 1)
    pos = lax.broadcasted_iota(jnp.int32, (rows, HD), 0)
    high = (pos // 256) * 256
    value = jnp.where(lane < 3, high, jnp.where(lane < 6, pos - high, 0))
    return value.astype(F32).astype(BF16)


def query_extras(me):
    row = lax.broadcasted_iota(jnp.int32, (HD, 256), 0)
    slope = jnp.exp2(jnp.full((HD, 256), 0.0, F32) + (-8.0 / H) * (me + 1).astype(F32))
    first = slope.astype(BF16).astype(F32)
    second = (slope - first).astype(BF16).astype(F32)
    third = slope - first - second
    part = lax.rem(row, 3)
    value = jnp.where(part == 0, first, jnp.where(part == 1, second, third))
    return jnp.where(row < 6, value, 0.0).astype(BF16)


def kernel_a(
    hid_ref, cot_ref, wqkv_ref, wproj_ref, wup_ref, wdown_ref, vec_ref,
    nrm, qkvt, qkvr, lse, mid, ctxr, wq, sm, gmid, branch, gct, tok, dtot, gup, gdn, gub,
    hid, wf, smb, wqo, dno, pjo, kr, ctxo, ctxt, pack_ref, sml_ref, normed_all, cota, n2, up, dn, pj, ub,
    xa, act, gu, g_part, g_pair, g_total, g_got, d_part, d_pair,
    h_s, h_r, h_h, c_s, c_r, c_h, p_s, p_r, p_h, n_s, n_r, n_h,
    w_s, w_r, o_s, o_r, m_s, m_r, q_s, q_r, d_s, d_r, x_s, x_r, n_c,
    g1s, g1r, g2s, g2r, d1s, d1r,
):
    me, core, sib, row = places()
    sem = barrier_seq_all(me)
    barrier_fsdp(sem, row)
    rows = vec_ref[...].astype(F32)
    vectors = jnp.concatenate([rows[0:8], jnp.zeros((8, HD), F32)], axis=0)
    for i in range(4):
        ub[0:1, i * HD : i * HD + HD] = rows[8 + i : 9 + i]
    pack_ref[0:192, :] = wqkv_ref[...]
    pack_ref[192:256, :] = wproj_ref[...]
    for piece in range(4):
        pack_ref[256 + piece * 64 : 320 + piece * 64, :] = wdown_ref[:, piece * 128 : piece * 128 + 128]
    pack_ref[512:640, :] = wup_ref[:, 0:128]
    pack_ref[640:768, :] = wup_ref[:, 128:256]
    blank = jnp.zeros((16, HD), F32)
    left = jnp.concatenate([vectors, blank], axis=1)
    right = jnp.concatenate([blank, vectors], axis=1)
    sml_ref[...] = jnp.where(core == 0, left, right).astype(BF16)
    columns = vectors.T
    qvb = jnp.concatenate([columns[:, 6:7], jnp.zeros((HD, 1), F32), columns[:, 7:8]], axis=0)
    pl.semaphore_wait(sem, NS - 1 + NF - 1)
    chips = Chips()
    qkv_rows = Rows(pack_ref, wf, pl.ds(0, 192), w_s, w_r)
    other_rows = Rows(pack_ref, wf, pl.ds(192, PACK - 192), o_s, o_r)

    def small_to(k):
        return remote(sml_ref, smb.at[me], m_s.at[k], m_r.at[me], seq=lax.rem(me + k, NS))

    qkv_rows.start()
    hidden = Gather(chips, hid_ref, hid, h_s, h_r, h_h)
    hidden.start()
    loop(1, NS, lambda k: small_to(k).start())
    wf[row] = pack_ref[...]
    smb[me] = sml_ref[...]
    hid[me] = hid_ref[...]
    cota[me] = cot_ref[...]
    kr[:, HD:] = key_extras(NS * TOK)
    qkv_rows.pass_on()
    other_rows.start()
    qkv_rows.finish()
    for f in range(NF):
        wqo[:, f * 128 : f * 128 + 128] = wf[f, 0:192, :]

    def q_block(j):
        block = 3 * me + j
        kind, head = block // H, lax.rem(block, H)
        src = wqo.at[pl.ds(j * HD, HD), :]
        dst = wq.at[pl.ds(pl.multiple_of(kind * HD, HD), HD), :]
        return head, kind, src, dst

    for j in range(3):
        head, kind, src, dst = q_block(j)

        @pl.when(head != me)
        def _():
            remote(src, dst, q_s.at[j], q_r.at[kind], seq=head).start()

        @pl.when(head == me)
        def _():
            dst[...] = src[...]

    def down_to(k):
        other = lax.rem(me + k, NS)
        return remote(
            dno.at[other], dn.at[pl.ds(pl.multiple_of(me * HD, HD), HD), :], d_s.at[k], d_r.at[me], seq=other
        )

    def down_from(k):
        other = lax.rem(me + k, NS)
        remote(
            dno.at[me], dn.at[pl.ds(pl.multiple_of(other * HD, HD), HD), :], d_s.at[k], d_r.at[other], seq=other
        ).wait_recv()

    hidden.pass_x()
    hidden.pass_y()
    other_rows.pass_on()

    def small_from(k):
        other = lax.rem(me + k, NS)
        remote(sml_ref, smb.at[other], m_s.at[k], m_r.at[other], seq=other).wait_recv()

    loop(1, NS, small_from)
    for t in range(NF):
        sm[:, t * 128 : t * 128 + 128] = smb[2 * t].astype(F32) + smb[2 * t + 1].astype(F32)

    for kind in range(3):

        @pl.when((kind * H + me) // 3 != me)
        def _():
            remote(
                wqo.at[pl.ds(0, HD), :], wq.at[pl.ds(kind * HD, HD), :], q_s.at[0], q_r.at[kind], seq=sib
            ).wait_recv()

    proj = Gather(chips, pjo, pj, p_s, p_r, p_h)
    cot = Gather(chips, cot_ref, cota, c_s, c_r, c_h)

    def send_rest():
        other_rows.finish()
        for f in range(NF):
            lanes = slice(f * 128, f * 128 + 128)
            pjo[:, lanes] = wf[f, 192:256, :]
            up[lanes, 0:128] = wf[f, 512:640, :]
            up[lanes, 128:256] = wf[f, 640:768, :]
            for half in range(2):
                for piece in range(2):
                    at = 256 + (2 * half + piece) * 64
                    dno[2 * f + half, :, piece * 128 : piece * 128 + 128] = wf[f, at : at + 64, :]
        proj.start()
        loop(1, NS, lambda k: down_to(k).start())
        dn[pl.ds(pl.multiple_of(me * HD, HD), HD), :] = dno[me]
        pj[me] = pjo[...]

    def keep(m):
        pair = pl.ds(2 * m, 2)
        return pltpu.make_async_copy(normed_all.at[pair], nrm.at[pair], n_c.at[m])

    def norm_and_project(k):
        hidden.step(k)

        @pl.when(k == 4)
        def _():
            send_rest()

        @pl.when(k == 3)
        def _():
            cot.start()

        m = chips.at(k)
        values = hid[pl.ds(2 * m, 2)].reshape(2 * TOK, D).astype(F32)
        standard = layer_norm(values, 1.0, 0.0)
        normed = (standard * sm[0:1, :] + sm[1:2, :]).astype(BF16)
        normed_all[pl.ds(2 * m, 2)] = standard.astype(BF16).reshape(2, TOK, D)
        keep(m).start()
        block = dot(wq[...], normed, 1, 1) + qvb
        qkvt[m] = block.astype(BF16)
        at = pl.ds(pl.multiple_of(m * 256, 256), 256)
        qkvr[0, at, :] = block[0:64].T.astype(BF16)
        keys = block[64:128].T.astype(BF16)
        qkvr[1, at, :] = keys
        kr[at, 0:HD] = keys
        qkvr[2, at, :] = block[128:192].T.astype(BF16)

    loop(0, NF, norm_and_project)
    extras = query_extras(me)

    def ctx_to(j):
        return remote(ctxo.at[j], ctxt.at[me], x_s.at[j], x_r.at[me], seq=j)

    between = {0: [proj.pass_x, proj.pass_y], 3: [cot.pass_x], 4: [proj.pass_f, cot.pass_y]}
    for j in range(NF):
        for relay in between.get(j, []):
            relay()
        n = (j + 1) * 256
        queries = jnp.concatenate([(qkvt[j, 0:64, :].astype(F32) * 0.125).astype(BF16), extras], axis=0)
        scores = dot(kr[0:n, :], queries)
        kpos = lax.broadcasted_iota(jnp.int32, (256, 256), 0)
        qpos = lax.broadcasted_iota(jnp.int32, (256, 256), 1)
        last = jnp.where(kpos <= qpos, scores[n - 256 :], -1e30)
        scores = last if j == 0 else jnp.concatenate([scores[: n - 256], last], axis=0)
        peak = jnp.max(scores, axis=0, keepdims=True)
        expo = jnp.exp(scores - peak)
        total = jnp.sum(expo, axis=0, keepdims=True)
        lse[j : j + 1, :] = peak + jnp.log(total)
        weights = expo.astype(BF16)
        acc = dot(qkvt[0, 128:192, :], weights[0:256])
        for i in range(1, j + 1):
            acc += dot(qkvt[i, 128:192, :], weights[i * 256 : i * 256 + 256])
        context = (acc / total).astype(BF16)
        for half in range(2):
            target = 2 * j + half
            ctxo[target] = context[:, half * 128 : half * 128 + 128]

            @pl.when(me != target)
            def _():
                ctx_to(target).start()

            @pl.when(me == target)
            def _():
                ctxt[target] = ctxo[target]

    cot.pass_f()
    proj.finish()

    def ctx_from(k):
        other = lax.rem(me + k, NS)
        remote(ctxo.at[other], ctxt.at[other], x_s.at[other], x_r.at[other], seq=other).wait_recv()

    loop(1, NS, ctx_from)
    context = ctxt[...].reshape(D, TOK).astype(F32).T.astype(BF16)
    ctxr[...] = context
    middle = hid_ref[...].astype(F32) + dot(context, pj[...].reshape(D, D), 1, 1) + sm[2:3, :]
    mid[...] = middle
    n2[...] = layer_norm(middle, sm[3:4, :], sm[4:5, :]).astype(BF16)

    tokens = Gather(chips, n2, xa, n_s, n_r, n_h)
    tokens.start()
    xa[chips.me] = n2[...]
    grads = Reduce(chips, g_part, g_pair, g_total, g_got, g1s, g1r, g2s, g2r)
    downs = Reduce(chips, d_part, d_pair, dtot, None, d1s, d1r, None, None)
    gub[...] = jnp.zeros_like(gub)
    loop(1, NS, down_from)
    cot.finish()

    def put(side, chip, values):
        side.part[pl.ds(2 * chip, 2)] = values.astype(BF16).reshape(2, TOK, D)
        side.pairing(chip).start()

    def feed(k):
        @pl.when(k == 1)
        def _():
            tokens.pass_x()
            tokens.pass_y()

        tokens.step(k)
        m = chips.at(k)
        rows = xa[pl.ds(2 * m, 2)].reshape(2 * TOK, D)
        upper = dot(rows, up[...]) + ub[0:1, :]
        square = upper * upper
        bend = jnp.tanh(0.7978845608 * upper * (1.0 + 0.044715 * square))
        half = 0.5 * (1.0 + bend)
        active = (upper * half).astype(BF16)
        slope = half + 0.5 * upper * (1.0 - bend * bend) * (0.7978845608 * (1.0 + 0.134145 * square))
        cots = cota[pl.ds(2 * m, 2)].reshape(2 * TOK, D)
        grad = (dot(cots, dn[...]) * slope).astype(BF16)
        at = pl.ds(pl.multiple_of(m * 256, 256), 256)
        act[at, :] = active
        gu[at, :] = grad
        gub[0:1, :] += jnp.sum(grad.astype(F32), axis=0, keepdims=True)
        put(grads, m, dot(grad, up[...], 1, 1))
        put(downs, m, dot(active, dn[...], 1, 1))

        @pl.when(k > 0)
        def _():
            grads.merge(chips.at(k - 1))
            downs.merge(chips.at(k - 1))

        for at, message in ((3, 4), (4, 3), (5, 5), (6, 2)):

            @pl.when(k == at)
            def _():
                grads.begin(message)

    loop(0, NF, feed)
    grads.merge(chips.fy)
    grads.far()
    downs.merge(chips.fy)
    gup[...] = dot(xa[...].reshape(NS * TOK, D), gu[...], 0, 0).astype(BF16)
    grads.turn()
    gdn[...] = dot(cota[...].reshape(NS * TOK, D), act[...], 0, 0).astype(BF16)
    grads.back()
    grads.across()
    tok[...] = jnp.zeros_like(tok)
    own_cot = cota[chips.me].astype(F32)
    tok[5:6, :] = jnp.sum(own_cot, axis=0, keepdims=True)
    back, tok[3:4, :], tok[4:5, :] = norm_back(mid[...], sm[3:4, :], grads.finish())
    total = own_cot + back
    gmid[...] = total
    low = total.astype(BF16)
    branch[...] = low
    tok[2:3, :] = jnp.sum(low.astype(F32), axis=0, keepdims=True)
    gct[...] = dot(low, pj[...].reshape(D, D)).T.astype(BF16).reshape(NS, HD, TOK)
    loop(0, NF, lambda m: keep(m).wait())
    hidden.drain()
    cot.drain()
    proj.drain()
    qkv_rows.drain()
    other_rows.drain()
    loop(1, NS, lambda k: small_to(k).wait_send())
    loop(1, NS, lambda k: down_to(k).wait_send())
    for j in range(3):
        head, kind, src, dst = q_block(j)

        @pl.when(head != me)
        def _():
            remote(src, dst, q_s.at[j], q_r.at[kind], seq=head).wait_send()

    def ctx_sent(k):
        other = lax.rem(me + k, NS)
        remote(ctxo.at[other], ctxt.at[me], x_s.at[other], x_r.at[me], seq=other).wait_send()

    loop(1, NS, ctx_sent)
    tokens.drain()
    grads.drain()
    loop(0, NF, lambda chip: downs.pairing(chip).wait_send())


def vm():
    return pl.BlockSpec(memory_space=pltpu.VMEM)


def hbm():
    return pl.BlockSpec(memory_space=pl.ANY)


def sems(*counts):
    return [pltpu.SemaphoreType.DMA(n if isinstance(n, tuple) else (n,)) for n in counts]


def params(number):
    return pltpu.CompilerParams(collective_id=number, has_side_effects=True, vmem_limit_bytes=62 * MIB)


def reduce_scratch(rows):
    return [pltpu.VMEM((NF, rows, D), BF16), pltpu.VMEM((NF, rows, D), BF16), pltpu.VMEM((7, rows, D), BF16)]


def run_a(*operands):
    shapes = [
        ((NS, TOK, D), BF16), ((NF, 192, 256), BF16), ((3, NS * TOK, HD), BF16), ((NF, 256), F32), ((TOK, D), F32),
        ((TOK, D), BF16), ((192, D), BF16), ((16, D), F32), ((TOK, D), F32), ((TOK, D), BF16), ((NS, HD, TOK), BF16),
        ((8, D), F32), ((NF, TOK, D), BF16), ((D, HID), BF16), ((D, HID), BF16), ((8, HID), F32),
    ]
    return pl.pallas_call(
        kernel_a,
        out_shape=[jax.ShapeDtypeStruct(*s) for s in shapes],
        in_specs=[vm() for _ in operands],
        out_specs=[hbm() if i == 0 else vm() for i in range(len(shapes))],
        scratch_shapes=[
            pltpu.VMEM((NS, TOK, D), BF16),
            pltpu.VMEM((NF, PACK, 128), BF16),
            pltpu.VMEM((NS, 16, 128), BF16),
            pltpu.VMEM((192, D), BF16),
            pltpu.VMEM((NS, HD, HID), BF16),
            pltpu.VMEM((HD, D), BF16),
            pltpu.VMEM((NS * TOK, 128), BF16),
            pltpu.VMEM((NS, HD, TOK), BF16),
            pltpu.VMEM((NS, HD, TOK), BF16),
            pltpu.VMEM((PACK, 128), BF16),
            pltpu.VMEM((16, 128), BF16),
            pltpu.VMEM((NS, TOK, D), BF16),
            pltpu.VMEM((NS, TOK, D), BF16),
            pltpu.VMEM((TOK, D), BF16),
            pltpu.VMEM((D, HID), BF16),
            pltpu.VMEM((D, HID), BF16),
            pltpu.VMEM((NS, HD, D), BF16),
            pltpu.VMEM((8, HID), F32),
            pltpu.VMEM((NS, TOK, D), BF16),
            pltpu.VMEM((NS * TOK, HID), BF16),
            pltpu.VMEM((NS * TOK, HID), BF16),
            pltpu.VMEM((NS, TOK, D), BF16),
        ]
        + reduce_scratch(TOK)
        + [pltpu.VMEM((NS, TOK, D), BF16), pltpu.VMEM((NF, TOK, D), BF16)]
        + sems(22, (8, 2), 8) * 4
        + sems(8, 8, 8, 8, 16, 16, 3, 3, 16, 16, 16, 16, 8, 8, 8, 16, 16, 8, 8),
        compiler_params=params(0),
        name="forward_and_feed",
    )(*operands)


def kernel_b(
    gc_ref, qkvt_hbm, qkvr_hbm, lse, wq, nrm_hbm, branch, dtot, ctx_ref, gdn_ref, gup_ref, hid_ref, gmid, mid, sm, tok, gub,
    layer_out, input_grad, w_qkv, w_proj, w_up, w_down, small,
    dct, gjt, kr, dk, dv, part, pair, total, got, d_total, d_got, gpj, p_pair, p_total, p_got, d1,
    u_pack, u_got, u_part, u_cross, u_keep, t_pack, t_got, t_part, t_cross, t_keep, gqkv, q1, tiles, m1, m2, sgot, nrm, qkvt, qkvr,
    x_s, x_r, r1s, r1r, r2s, r2r, d2s, d2r, p1s, p1r, p2s, p2r, y_s, y_r, u_s, u_r, t_s, t_r, q_s, q_r, m_s, m_r,
    v_s, v_r, l_s, n_c, f_c, r_c,
):
    me, core, sib, row = places()
    chips = Chips()
    local = pltpu.make_async_copy(dtot, d_total, l_s)
    local.start()
    normed_in = pltpu.make_async_copy(nrm_hbm, nrm, n_c)
    flat_in = pltpu.make_async_copy(qkvt_hbm, qkvt, f_c)
    rows_in = pltpu.make_async_copy(qkvr_hbm, qkvr, r_c)
    rows_in.start()
    flat_in.start()
    normed_in.start()
    sem = barrier_seq_all(me)
    barrier_fsdp(sem, row)
    pl.semaphore_wait(sem, NS - 1 + NF - 1)
    downs = Reduce(chips, None, None, d_total, d_got, None, None, d2s, d2r)
    projs = Reduce(chips, gpj, p_pair, p_total, p_got, p1s, p1r, p2s, p2r)
    ups = RowSums(u_pack, u_got, u_part, u_cross, u_s, u_r)
    rest = RowSums(t_pack, t_got, t_part, t_cross, t_s, t_r)

    def block(other):
        return pl.ds(pl.multiple_of(other * HD, HD), HD)

    def down_to(k):
        other = lax.rem(me + k, NS)
        return remote(gdn_ref.at[block(other), :], d1.at[me], y_s.at[k], y_r.at[me], seq=other)

    def down_from(k):
        other = lax.rem(me + k, NS)
        remote(gdn_ref.at[block(me), :], d1.at[other], y_s.at[k], y_r.at[other], seq=other).wait_recv()

    def send_weights():
        loop(1, NS, down_from)
        for f in range(NF):
            lanes = slice(f * 128, f * 128 + 128)
            for half in range(2):
                for piece in range(2):
                    at = (2 * half + piece) * 64
                    u_pack[f, at : at + 64, :] = d1[2 * f + half, :, piece * 128 : piece * 128 + 128]
            u_pack[f, 256:384, :] = gup_ref[lanes, 0:128]
            u_pack[f, 384:512, :] = gup_ref[lanes, 128:256]
        ups.start()

    def merge_projs():
        loop(0, NF, projs.merge)
        projs.far()
        projs.sides()

    def q_block(kind):
        index = kind * H + me
        holder, slot = index // 3, lax.rem(index, 3)
        return holder, slot, gqkv.at[pl.ds(kind * HD, HD), :], q1.at[block(slot), :]

    def tokens(k):
        other = lax.rem(me + k, NS)
        return remote(tiles.at[other // 2], m1.at[me], m_s.at[k], m_r.at[me], seq=other)

    def tokens_from(k):
        other = lax.rem(me + k, NS)
        remote(tiles.at[0], m1.at[other], m_s.at[k], m_r.at[other], seq=other).wait_recv()

    def vectors(k):
        return remote(m2, sgot.at[row], v_s.at[k], v_r.at[row], fsdp=lax.rem(row + k, NF))

    def vectors_from(k):
        other = lax.rem(row + k, NF)
        remote(m2, sgot.at[other], v_s.at[k], v_r.at[other], fsdp=other).wait_recv()

    def ctx_to(k):
        other = lax.rem(me + k, NS)
        return remote(gc_ref.at[other], dct.at[me], x_s.at[k], x_r.at[me], seq=other)

    def ctx_from(k):
        other = lax.rem(me + k, NS)
        remote(gc_ref.at[me], dct.at[other], x_s.at[k], x_r.at[other], seq=other).wait_recv()

    loop(1, NS, lambda k: ctx_to(k).start())
    dct[me] = gc_ref[me]
    d1[me] = gdn_ref[block(me), :]
    kr[:, HD:] = key_extras(NS * TOK)
    rows_in.wait()
    flat_in.wait()
    kr[:, 0:HD] = qkvr[1]
    dk[...] = jnp.zeros_like(dk)
    dv[...] = jnp.zeros_like(dv)
    extras = query_extras(me)
    for f in range(NF):
        lanes = slice(f * 128, f * 128 + 128)
        columns = branch[:, lanes].astype(F32).T.astype(BF16)
        gpj[2 * f : 2 * f + 2] = dot(columns, ctx_ref[...]).astype(BF16).reshape(2, HD, D)
    loop(1, NS, lambda k: down_to(k).start())
    loop(0, NF, lambda chip: projs.pairing(chip).start())
    local.wait()
    normed_in.wait()
    loop(1, NS, ctx_from)
    downs.far()
    downs.sides()
    between = {3: [send_weights], 5: [merge_projs], 7: [downs.turn]}
    for j in range(NF):
        for relay in between.get(j, []):
            relay()
        n = (j + 1) * 256
        at = slice(j * 256, n)
        queries = jnp.concatenate([(qkvt[j, 0:64, :].astype(F32) * 0.125).astype(BF16), extras], axis=0)
        scores = dot(kr[0:n, :], queries)
        probs = jnp.exp(scores - lse[j : j + 1, :])
        kpos = lax.broadcasted_iota(jnp.int32, (256, 256), 0)
        qpos = lax.broadcasted_iota(jnp.int32, (256, 256), 1)
        last = jnp.where(kpos <= qpos, probs[n - 256 :], 0.0)
        probs = last if j == 0 else jnp.concatenate([probs[: n - 256], last], axis=0)
        gctx = jnp.concatenate([dct[2 * j], dct[2 * j + 1]], axis=1)
        gprobs = dot(qkvr[2, 0:n, :], gctx)
        inner = jnp.sum(probs * gprobs, axis=0, keepdims=True)
        gscores = (probs * (gprobs - inner) * 0.125).astype(BF16)
        gq = dot(qkvt[0, 64:128, :], gscores[0:256])
        for i in range(1, j + 1):
            gq += dot(qkvt[i, 64:128, :], gscores[i * 256 : i * 256 + 256])
        gjt[j, 0:64, :] = gq.astype(BF16)
        dk[0:n, :] += dot(gscores, qkvr[0, at, :])
        dv[0:n, :] += dot(probs.astype(BF16), gctx.astype(F32).T.astype(BF16))
    for j in range(NF):
        at = slice(j * 256, j * 256 + 256)
        gjt[j, 64:128, :] = dk[at, :].T.astype(BF16)
        gjt[j, 128:192, :] = dv[at, :].T.astype(BF16)

    acc = jnp.zeros((192, D), F32)
    sums = jnp.zeros((192, 1), F32)
    for j in range(NF):
        acc += dot(gjt[j], nrm[2 * j : 2 * j + 2].reshape(2 * TOK, D))
        sums += jnp.sum(gjt[j].astype(F32), axis=1, keepdims=True)
    gqkv[...] = (acc * sm[0:1, :] + sums * sm[1:2, :]).astype(BF16)
    head = wq[...].astype(F32)
    gain = jnp.sum(acc * head, axis=0, keepdims=True)
    shift = jnp.sum(sums * head, axis=0, keepdims=True)
    line = jnp.concatenate([gain, shift, tok[2:8, :]], axis=0)
    for t in range(NF):
        tiles[t] = line[:, t * 128 : t * 128 + 128]
    loop(1, NS, lambda k: tokens(k).start())
    m1[me] = tiles[me // 2]
    m2[...] = jnp.zeros_like(m2)
    line = jnp.broadcast_to(sums, (192, 128)).T
    m2[8:9, 0:64] = line[0:1, 0:64]
    m2[8:9, 64:128] = line[0:1, 128:192]
    m2[9:10, :] = gub[0:1, 0:128]
    m2[10:11, :] = gub[0:1, 128:256]
    for kind in range(3):
        holder, slot, src, dst = q_block(kind)

        @pl.when(holder != me)
        def _():
            remote(src, dst, q_s.at[kind], q_r.at[slot], seq=holder).start()

        @pl.when(holder == me)
        def _():
            dst[...] = src[...]

    norms = Reduce(chips, part, pair, total, got, r1s, r1r, r2s, r2r)
    downs.back()
    during = {
        1: [lambda: norms.begin(0, 1), projs.turn],
        2: [downs.across],
        3: [lambda: norms.begin(2), projs.back],
        4: [projs.across],
        5: [lambda: norms.begin(5), norms.turn],
        6: [lambda: norms.begin(3)],
    }

    def step(k):
        m = chips.at(NF - 1 - k)
        rows = gjt[m].astype(F32).T.astype(BF16)
        part[pl.ds(2 * m, 2)] = dot(rows, wq[...]).astype(BF16).reshape(2, TOK, D)
        norms.pairing(m).start()

        @pl.when(k > 0)
        def _():
            norms.merge(chips.at(NF - k))

        for at, events in during.items():

            @pl.when(k == at)
            def _():
                for event in events:
                    event()

    loop(0, NF, step)
    norms.begin(4)
    norms.merge(chips.own)
    ups.middle(u_keep)
    loop(1, NS, tokens_from)
    vector = m1[0]
    for p in range(1, NS):
        vector += m1[p]
    m2[0:8, :] = vector
    loop(1, NF, lambda k: vectors(k).start())
    sgot[row] = m2[...]
    norms.back()
    for slot in range(3):

        @pl.when(lax.rem(3 * me + slot, H) != me)
        def _():
            remote(
                gqkv.at[pl.ds(0, HD), :], q1.at[pl.ds(slot * HD, HD), :], q_s.at[0], q_r.at[slot], seq=sib
            ).wait_recv()

    proj_sum = projs.finish().astype(BF16)
    for f in range(NF):
        lanes = slice(f * 128, f * 128 + 128)
        t_pack[f, 0:192, :] = q1[:, lanes]
        t_pack[f, 192:256, :] = proj_sum[:, lanes]
    rest.start()
    norms.across()
    layer_out[...] = (mid[...] + downs.finish() + sm[5:6, :]).astype(BF16)
    rest.middle(t_keep)
    rows = ups.finish(u_keep)
    for piece in range(4):
        w_down[:, piece * 128 : piece * 128 + 128] = rows[piece * HD : piece * HD + HD]
    w_up[:, 0:128] = rows[256:384]
    w_up[:, 128:256] = rows[384:512]
    back, _, _ = norm_back(hid_ref[...].astype(F32), sm[0:1, :], norms.finish())
    input_grad[...] = (gmid[...] + back).astype(BF16)
    rows = rest.finish(t_keep)
    w_qkv[...] = rows[0:192]
    w_proj[...] = rows[192:256]
    loop(1, NF, vectors_from)
    vector = sgot[0]
    for f in range(1, NF):
        vector += sgot[f]
    small[...] = vector
    norms.drain()
    downs.drain(False)
    projs.drain()
    ups.drain()
    rest.drain()
    loop(1, NS, lambda k: ctx_to(k).wait_send())
    loop(1, NS, lambda k: down_to(k).wait_send())
    loop(1, NS, lambda k: tokens(k).wait_send())
    loop(1, NF, lambda k: vectors(k).wait_send())
    for kind in range(3):
        holder, slot, src, dst = q_block(kind)

        @pl.when(holder != me)
        def _():
            remote(src, dst, q_s.at[kind], q_r.at[slot], seq=holder).wait_send()


def row_scratch(rows):
    return [
        pltpu.VMEM((NF, rows, 128), BF16),
        pltpu.VMEM((4, 2, rows, 128), BF16),
        pltpu.VMEM((2, rows, 128), BF16),
        pltpu.VMEM((rows, 128), BF16),
        pltpu.VMEM((rows, 128), F32),
    ]


def run_b(*operands):
    shapes = [
        ((TOK, D), BF16), ((TOK, D), BF16), ((192, 128), F32), ((HD, 128), F32), ((128, HID), F32), ((HD, 512), F32),
        ((16, 128), F32),
    ]
    return pl.pallas_call(
        kernel_b,
        out_shape=[jax.ShapeDtypeStruct(*s) for s in shapes],
        in_specs=[hbm() if i in (1, 2, 5, 7) else vm() for i in range(len(operands))],
        out_specs=[vm() for _ in shapes],
        scratch_shapes=[
            pltpu.VMEM((NS, HD, TOK), BF16),
            pltpu.VMEM((NF, 192, 256), BF16),
            pltpu.VMEM((NS * TOK, 128), BF16),
            pltpu.VMEM((NS * TOK, HD), F32),
            pltpu.VMEM((NS * TOK, HD), F32),
            pltpu.VMEM((NS, TOK, D), BF16),
        ]
        + reduce_scratch(TOK)
        + [pltpu.VMEM((NF, TOK, D), BF16), pltpu.VMEM((7, TOK, D), BF16), pltpu.VMEM((NS, HD, D), BF16)]
        + reduce_scratch(HD)
        + [pltpu.VMEM((NS, HD, HID), BF16)]
        + row_scratch(512)
        + row_scratch(256)
        + [
            pltpu.VMEM((192, D), BF16),
            pltpu.VMEM((192, D), BF16),
            pltpu.VMEM((NF, 8, 128), F32),
            pltpu.VMEM((NS, 8, 128), F32),
            pltpu.VMEM((16, 128), F32),
            pltpu.VMEM((NF, 16, 128), F32),
            pltpu.VMEM((NS, TOK, D), BF16),
            pltpu.VMEM((NF, 192, 256), BF16),
            pltpu.VMEM((3, NS * TOK, HD), BF16),
        ]
        + sems(16, 16, 8, 8, 16, 16, 16, 16, 8, 8, 16, 16, 16, 16, 4, 4, 4, 4, 3, 3, 16, 16, 8, 8)
        + [pltpu.SemaphoreType.DMA] * 4,
        compiler_params=params(2),
        name="attend_back",
    )(*operands)


def kernel_f(*refs):
    half = len(refs) // 2
    for src, dst in zip(refs[: half - 1], refs[half:-1]):
        dst[...] = src[...]
    values = refs[half - 1][...]
    mine = jnp.where(lax.rem(lax.axis_index("seq"), 2) == 0, values[0:8, 0:HD], values[0:8, HD:])
    refs[-1][...] = values
    refs[-1][0:8, 0:HD] = mine


def run_f(*operands):
    return pl.pallas_call(
        kernel_f,
        out_shape=[jax.ShapeDtypeStruct(o.shape, o.dtype) for o in operands],
        in_specs=[vm() for _ in operands],
        out_specs=[vm() for _ in operands],
        name="finish",
    )(*operands)


def per_device(
    hidden_in, norm1_gain, norm1_shift, qkv_weight, query_bias, value_bias, proj_weight, proj_bias,
    norm2_gain, norm2_shift, up_weight, up_bias, down_weight, down_bias, out_cotangent,
):
    hid, cot = hidden_in[0], out_cotangent[0]
    vectors = [norm1_gain, norm1_shift, proj_bias, norm2_gain, norm2_shift, down_bias, query_bias, value_bias]
    vectors = jnp.concatenate([v[None] for v in vectors] + [up_bias.reshape(4, HD)], axis=0)
    (nrm, qkvt, qkvr, lse, middle, ctx, wq, sm, gmid, branch, gctx, tok, downs, gup, gdn, gub) = run_a(
        hid, cot, qkv_weight.T, proj_weight.T, up_weight, down_weight.T, vectors
    )
    results = run_b(
        gctx, qkvt, qkvr, lse, wq, nrm, branch, downs, ctx, gdn, gup, hid, gmid, middle, sm, tok, gub
    )
    layer_out, input_grad, w_qkv, w_proj, w_up, w_down, vecs = run_f(*results)
    return (
        layer_out[None],
        input_grad[None],
        vecs[0, :64],
        vecs[1, :64],
        w_qkv.T,
        vecs[8, :64],
        vecs[8, 64:],
        w_proj.T,
        vecs[2, :64],
        vecs[3, :64],
        vecs[4, :64],
        w_up,
        vecs[9:11].reshape(256),
        w_down.T,
        vecs[5, :64],
    )


def solution(mesh):
    act, vec, mat = P("fsdp", "seq", None), P("seq"), P("fsdp", "seq")
    return jax.shard_map(
        per_device,
        mesh=mesh,
        in_specs=(act, vec, vec, mat, vec, vec, mat, vec, vec, vec, mat, vec, mat, vec, act),
        out_specs=(act, act, vec, vec, mat, vec, vec, mat, vec, vec, vec, mat, vec, mat, vec),
        check_vma=False,
    )
```
